32 devices in a mesh: groups: 2 (over x), ctx: 16 (over z, y, core).
Axes of the slice: x: 2, y: 2, z: 4, core: 2. Of those that a mesh axis runs over, the one named last changes fastest.
Arguments:
- queries: bfloat16 [4096, 2048], P(('groups', 'ctx')), parts along dimension 0, may hold values from -200 to 200
- rotated_keys: bfloat16 [4096, 256], P(('groups', 'ctx')), parts along dimension 0, may hold values from -6 to 6
- value_matrix: bfloat16 [4096, 256], P(('groups', 'ctx')), parts along dimension 0, may hold values from -6 to 6
- stretch_pos: int32 [32], P(('groups', 'ctx')), parts along dimension 0, may hold values from 0 to 15, each once
- residual: bfloat16 [4096, 2048], P(('groups', 'ctx')), parts along dimension 0, may hold values from -6 to 6
- norm_gain: float32 [2048], replicated, may hold values from 0.1 to 1.9
- routes: int32 [4096, 8], P(('groups', 'ctx')), parts along dimension 0, may hold values from 0 to 15, all different within a row; in each aligned block of 128 rows (0 to 127, 128 to 255, ...) at most 72 rows name the same one
- combine: float32 [4096, 8], P(('groups', 'ctx')), parts along dimension 0, may hold values from 0.05 to 1
- gate_weight: bfloat16 [16, 2048, 384], P('ctx'), may hold values from -0.125 to 0.125
- up_weight: bfloat16 [16, 2048, 384], P('ctx'), may hold values from -0.125 to 0.125
- down_weight: bfloat16 [16, 384, 2048], P('ctx'), may hold values from -0.3125 to 0.3125
Outputs:
- layer_out: bfloat16 [4096, 2048], P(('groups', 'ctx')), parts along dimension 0
The draws below stay inside these ranges and needn't reach their ends.
There are 2 independent parts, one for each index of `groups`. The reference program is written for one: setup_inputs(seed, part) draws one part's arguments, and reference() takes and returns one part's arrays. A program takes and returns all parts, laid end to end along the dimension named above; an argument that names none is the same for every part. Nothing has to cross between parts.
Inputs may be any that keep to these rules, and one draw needn't show every extreme that they name: `routes`: within the rows of one device no expert is named more than 72 times; some device names some expert exactly 72 times. `stretch_pos`: each block place appears once.
All inputs are finite; a program needn't handle non-finite values.
Results may differ from the reference program's by a relative error of at most 0.01.
Values may be sent and summed in bfloat16 or wider, within the bound.
No kernel may reach another device: no remote copies, remote signals or barrier semaphores. Data moves between devices by JAX's collectives and lax.ppermute only.
A program may use at most 128 MiB of HBM per device.

```python
import math
import jax
import jax.numpy as jnp
import numpy as np
from jax import lax

D = 2048
QUERY_HEAD_COUNT = 16
KEY_VALUE_HEADS = 2
HEAD_SIZE = 128
HID = 384
TOP = 8
TOKENS_PER_SHARD = 128
SEQUENCE_TOKENS = 2048
BLOCKS = 16
EXPERTS = 16
CAP = 72


def base_keys(key):
    unshaped_scores = jnp.clip(jax.random.normal(key, (SEQUENCE_TOKENS, KEY_VALUE_HEADS * HEAD_SIZE), jnp.float32), -6.0, 6.0)
    places = jnp.arange(SEQUENCE_TOKENS)
    chosen = places % TOKENS_PER_SHARD == TOKENS_PER_SHARD // 2
    before = jnp.roll(chosen, -1)
    mixed = unshaped_scores
    return jnp.where(before[:, None], mixed, unshaped_scores)


def draw_rotated_keys(key, part):
    reshaped_scores = base_keys(key)
    return reshaped_scores.astype(jnp.bfloat16)


def draw_queries(key, part):
    key = jax.random.fold_in(key, 11)
    result = jnp.clip(jax.random.normal(key, (SEQUENCE_TOKENS, QUERY_HEAD_COUNT * HEAD_SIZE), jnp.float32), -6.0, 6.0)
    return result.astype(jnp.bfloat16)


def block_levels(key, extent, split, least, high):
    loudness, own = 1.0, jax.random.fold_in(key, 6)
    for position, parts in split:
        heights = jnp.exp(jax.random.uniform(jax.random.fold_in(own, position), (parts,), jnp.float32, least / len(split), high / len(split)))
        loudness = loudness * jnp.repeat(heights, extent[position] // parts).reshape([-1 if axis == position else 1 for axis in range(len(extent))])
    return loudness


def assign_block(own_key, own, number, rows, amount, top, most, slope):
    ranking = jax.random.permutation(own_key, amount)
    crowded, common = load_shares(amount, rows * top, most, slope, True), load_shares(amount, rows * top, most, slope, False)
    places = jnp.arange(amount)

    def named(lengths, offset_by):
        used = int((lengths > 0).sum())
        fixed = max(1, used // 4)
        passed = fixed + (places - fixed + offset_by * (used - fixed)) % max(1, amount - fixed)
        return jnp.zeros((amount,), jnp.int32).at[ranking[jnp.where(places < fixed, places, passed)]].set(jnp.asarray(lengths, jnp.int32))

    lengths = jnp.where(number % 4 == 0, named(crowded, number // 4), named(common, number - number // 4 - 1))
    mixed = jax.random.permutation(jax.random.fold_in(own, 3), amount)
    giver, receiver = mixed[0:amount // 2 * 2:2], mixed[1:amount // 2 * 2:2]
    slack = jnp.minimum(lengths[giver] - 1, most - lengths[receiver]) // 2
    slack = jnp.where((giver == ranking[0]) | (receiver == ranking[0]) | (lengths[receiver] == 0), 0, jnp.maximum(slack, 0))
    passed = jax.random.randint(jax.random.fold_in(own, 4), (amount // 2,), 0, 1 << 20) % (slack + 1)
    lengths = lengths.at[giver].add(-passed).at[receiver].add(passed)
    labels = jnp.searchsorted(jnp.cumsum(lengths), jnp.arange(rows * top), side="right").astype(jnp.int32)
    listing = labels.reshape(top, rows).T
    listing = listing[jax.random.permutation(jax.random.fold_in(own, 1), rows)]
    offset_by = jax.random.randint(jax.random.fold_in(own, 2), (rows, 1), 0, top)
    return jnp.take_along_axis(listing, (jnp.arange(top)[None, :] + offset_by) % top, axis=1)


def load_shares(amount, total, most, slope, full):
    weights = [(1 << 20) // math.isqrt(rank ** slope) + 1 for rank in range(1, amount + 1)]
    largest = most if full else min(most, max(-(-total // amount), total * weights[0] // sum(weights)))
    least = 1 if total - largest >= amount - 1 else 0
    holding, surplus = [largest] + [least] * (amount - 1), total - largest - least * (amount - 1)
    while surplus > 0:
        candidates = [i for i in range(1, amount) if holding[i] < largest] or [i for i in range(1, amount) if holding[i] < most]
        whole, left = sum([weights[i] for i in candidates]), surplus
        for i in candidates:
            more = min(most - holding[i], max(1, left * weights[i] // whole), surplus)
            holding[i] = holding[i] + more
            surplus = surplus - more
    return np.array(holding)


def noise(own_key, shape, spread, bound, split=(), held_as=jnp.bfloat16):
    drawn = jax.random.normal(own_key, shape, jnp.float32) * spread
    if len(split) > 0:
        drawn = block_levels(own_key, shape, split, -0.22, 0.18) * drawn
    return jnp.clip(drawn, min=-bound, max=bound).astype(held_as)


def setup_inputs(seed: int = 0, part: int = 0) -> dict:
    key_list = jax.random.split(jax.random.key(seed), 12)
    own_keys = jax.random.split(jax.random.fold_in(key_list[11], part), 12)
    queries = draw_queries(jax.random.fold_in(jax.random.fold_in(key_list[11], part), 71), part)
    rotated_keys = draw_rotated_keys(jax.random.fold_in(jax.random.fold_in(key_list[11], part), 71), part)
    value_matrix = noise(own_keys[2], (SEQUENCE_TOKENS, KEY_VALUE_HEADS * HEAD_SIZE), 1.0, 6.0, ((0, 16),))
    stretch_pos = jax.random.permutation(own_keys[3], BLOCKS).astype(jnp.int32)
    residual = noise(own_keys[4], (SEQUENCE_TOKENS, D), 1.0, 6.0, ((0, 16),))
    norm_gain = jnp.clip(1.0 + 0.18 * jax.random.normal(key_list[5], (D,), jnp.float32), 0.1, 1.9)
    routes_keys = jax.random.split(jax.random.fold_in(own_keys[6], 1), SEQUENCE_TOKENS // TOKENS_PER_SHARD)
    routes_turns = jax.random.permutation(jax.random.fold_in(own_keys[6], 3), SEQUENCE_TOKENS // TOKENS_PER_SHARD)
    routes = jax.vmap(lambda own, number: assign_block(jax.random.fold_in(own_keys[6], 2), own, number, TOKENS_PER_SHARD, EXPERTS, TOP, CAP, 2))(routes_keys, routes_turns).reshape((SEQUENCE_TOKENS, TOP))
    combine = jnp.clip(jnp.exp(math.log(1.0) - 2.9957323 * jax.random.uniform(own_keys[7], (SEQUENCE_TOKENS, TOP), jnp.float32) ** block_levels(own_keys[7], (SEQUENCE_TOKENS, TOP), ((0, 16),), -0.2, 0.2)), 0.05, 1.0)
    gate_weight = noise(key_list[8], (EXPERTS, D, HID), D ** -0.5, 0.125, ((0, 16),))
    up_weight = noise(key_list[9], (EXPERTS, D, HID), D ** -0.5, 0.125, ((0, 16),))
    down_weight = noise(key_list[10], (EXPERTS, HID, D), HID ** -0.5, 0.3125, ((0, 16),))
    return dict(queries=queries, rotated_keys=rotated_keys, value_matrix=value_matrix, stretch_pos=stretch_pos, residual=residual, norm_gain=norm_gain, routes=routes, combine=combine, gate_weight=gate_weight, up_weight=up_weight, down_weight=down_weight)


NEG = -1e+30

def attend_block(query_tile, query_pos, rotated_keys, value_matrix, key_pos):
    query_group = QUERY_HEAD_COUNT // KEY_VALUE_HEADS
    query_tensor = query_tile.astype(jnp.float32).reshape(TOKENS_PER_SHARD, KEY_VALUE_HEADS, query_group, HEAD_SIZE)
    key_cube = rotated_keys.astype(jnp.float32).reshape(SEQUENCE_TOKENS, KEY_VALUE_HEADS, HEAD_SIZE)
    value_cube = value_matrix.astype(jnp.float32).reshape(SEQUENCE_TOKENS, KEY_VALUE_HEADS, HEAD_SIZE)
    scores = jnp.einsum('tagd,sad->agts', query_tensor, key_cube) / jnp.sqrt(jnp.float32(HEAD_SIZE))
    scores = jnp.where(key_pos[None, None, None, :] <= query_pos[None, None, :, None], scores, jnp.float32(NEG))
    biggest = lax.optimization_barrier(jnp.max(scores, axis=-1))
    expo = jnp.exp(scores - biggest[..., None])
    totals = lax.optimization_barrier(jnp.sum(expo, axis=-1))
    probs = expo.astype(jnp.bfloat16)
    summed = jnp.einsum('agts,sad->agtd', probs.astype(jnp.float32), value_cube)
    result = summed / totals[..., None]
    return jnp.transpose(result, (2, 0, 1, 3)).reshape(TOKENS_PER_SHARD, QUERY_HEAD_COUNT * HEAD_SIZE).astype(jnp.bfloat16)

def reference(queries, rotated_keys, value_matrix, stretch_pos, residual, norm_gain, routes, combine, gate_weight, up_weight, down_weight):
    offsets = jnp.arange(TOKENS_PER_SHARD, dtype=jnp.int32)
    positions = (stretch_pos.astype(jnp.int32)[:, None] * TOKENS_PER_SHARD + offsets[None, :]).reshape(SEQUENCE_TOKENS)
    query_blocks = queries.reshape(BLOCKS, TOKENS_PER_SHARD, QUERY_HEAD_COUNT * HEAD_SIZE)
    pos_blocks = positions.reshape(BLOCKS, TOKENS_PER_SHARD)
    attended = lax.map(lambda pair: attend_block(pair[0], pair[1], rotated_keys, value_matrix, positions), (query_blocks, pos_blocks))
    attended = attended.reshape(SEQUENCE_TOKENS, QUERY_HEAD_COUNT * HEAD_SIZE)
    hidden_state = residual.astype(jnp.float32) + attended.astype(jnp.float32)
    meansq = lax.optimization_barrier(jnp.mean(hidden_state * hidden_state, axis=-1, keepdims=True))
    normed = (hidden_state * lax.rsqrt(meansq + 1e-06) * norm_gain).astype(jnp.bfloat16)
    limit = BLOCKS * CAP
    flat_routes = routes.reshape(-1)
    flat_combine = combine.reshape(-1)

    def expert_step(mixture, items):
        expert_id, gate_e, up_e, down_e = items
        hits = flat_routes == expert_id
        where_hit = jnp.nonzero(hits, size=limit, fill_value=0)[0].astype(jnp.int32)
        count = jnp.sum(hits.astype(jnp.int32))
        valid = (jnp.arange(limit, dtype=jnp.int32) < count).astype(jnp.float32)
        token_ids = (where_hit // TOP).astype(jnp.int32)
        scaled = flat_combine[where_hit] * valid
        rows = normed[token_ids]
        gate = jnp.dot(rows, gate_e, preferred_element_type=jnp.float32)
        upper = jnp.dot(rows, up_e, preferred_element_type=jnp.float32)
        act = (jax.nn.silu(gate) * upper).astype(jnp.bfloat16)
        output = jnp.dot(act, down_e, preferred_element_type=jnp.float32).astype(jnp.bfloat16)
        mixture = mixture.at[token_ids].add(scaled[:, None] * output.astype(jnp.float32))
        return (mixture, None)
    start = jnp.zeros((SEQUENCE_TOKENS, D), jnp.float32)
    mixture, unused = lax.scan(expert_step, start, (jnp.arange(EXPERTS, dtype=jnp.int32), gate_weight, up_weight, down_weight))
    return (hidden_state + mixture).astype(jnp.bfloat16)
```

```python
import functools
import math

import jax
import jax.numpy as jnp
from jax import lax
from jax.experimental import pallas as pl
from jax.experimental.pallas import tpu as pltpu
from jax.sharding import PartitionSpec as P

D = 2048
HEAD_SIZE = 128
CORES = 2
EXTRA = 16


NEG = -1e30


def ring_pairs(chips):
    order = list(range(0, chips, 2)) + list(range(chips - 1, 0, -2))
    onward = [
        (order[i] * CORES + core, order[(i + 1) % chips] * CORES + core)
        for i in range(chips)
        for core in range(CORES)
    ]
    back = [(b, a) for a, b in onward]
    swap = [(i, i ^ 1) for i in range(chips * CORES)]
    return onward, back, swap


def pack_kernel(pos_ref, key_ref, value_ref, routes_ref, combine_ref, out_ref):
    rows, width = key_ref.shape
    top = routes_ref.shape[1]
    out_ref[0:rows, 0:width] = key_ref[...]
    out_ref[0:rows, width : 2 * width] = value_ref[...]
    weight = combine_ref[...]
    high = weight.astype(jnp.bfloat16)
    low = (weight - high.astype(jnp.float32)).astype(jnp.bfloat16)
    lane = lax.broadcasted_iota(jnp.int32, (top, HEAD_SIZE), 1)
    row = lax.broadcasted_iota(jnp.int32, (top, HEAD_SIZE), 0)

    def put(part, shift):
        spread = jnp.where(lane == row + shift, 1.0, 0.0).astype(jnp.bfloat16)
        return jnp.dot(part, spread, preferred_element_type=jnp.float32)

    names = routes_ref[...].astype(jnp.float32).astype(jnp.bfloat16)
    turned = (put(names, 0) + put(high, top) + put(low, 2 * top)).T
    out_ref[rows : rows + EXTRA, 0:128] = turned[0:EXTRA].astype(jnp.bfloat16)
    out_ref[rows : rows + EXTRA, 128:256] = turned[EXTRA : 2 * EXTRA].astype(jnp.bfloat16)
    place = jnp.full((EXTRA, 2 * width - 256), pos_ref[0].astype(jnp.float32), jnp.float32)
    out_ref[rows : rows + EXTRA, 256 : 2 * width] = place.astype(jnp.bfloat16)


def pack_message(stretch_pos, keys, values, routes, combine):
    rows, width = keys.shape
    vmem = pl.BlockSpec(memory_space=pltpu.VMEM)
    return pl.pallas_call(
        pack_kernel,
        out_shape=jax.ShapeDtypeStruct((rows + EXTRA, 2 * width), jnp.bfloat16),
        in_specs=[pl.BlockSpec(memory_space=pltpu.SMEM), vmem, vmem, vmem, vmem],
        out_specs=vmem,
        name="pack_message",
    )(stretch_pos, keys, values, routes, combine)


def attend_kernel(count, *refs):
    query_ref, residual_ref, gain_ref = refs[:3]
    messages = refs[3 : 3 + count]
    hidden_ref, normed_ref, key_ext, value_ext = refs[3 + count :]
    rows = query_ref.shape[0]
    kv_heads = key_ext.shape[0]
    heads = query_ref.shape[1] // HEAD_SIZE
    group = heads // kv_heads
    span = count * rows
    width = kv_heads * HEAD_SIZE
    sub = lax.broadcasted_iota(jnp.int32, (rows, rows), 0)
    lane = lax.broadcasted_iota(jnp.int32, (rows, rows), 1)
    ahead = (sub - lane).astype(jnp.float32)
    own_pos = messages[0][rows : rows + EXTRA, 256 : 256 + rows][0:1].astype(jnp.float32)
    ones = jnp.ones((rows, HEAD_SIZE), jnp.bfloat16)
    for block in range(count):
        ref = messages[block]
        at = slice(block * rows, (block + 1) * rows)
        pos = ref[rows : rows + EXTRA, 256 : 256 + rows][0:1].astype(jnp.float32)
        later = (pos - own_pos) * float(rows) + ahead
        bias = jnp.where(later > 0.0, NEG, 0.0).astype(jnp.bfloat16)
        for a in range(kv_heads):
            key_ext[a, at, 0:HEAD_SIZE] = ref[0:rows, a * HEAD_SIZE : (a + 1) * HEAD_SIZE]
            key_ext[a, at, HEAD_SIZE : HEAD_SIZE + rows] = bias
            value_ext[a, at, 0:HEAD_SIZE] = ref[
                0:rows, width + a * HEAD_SIZE : width + (a + 1) * HEAD_SIZE
            ]
            value_ext[a, at, HEAD_SIZE : 2 * HEAD_SIZE] = ones
    eye = jnp.where(sub == lane, 1.0, 0.0).astype(jnp.bfloat16)
    rate = math.log2(math.e) / math.sqrt(HEAD_SIZE)
    step = min(512, span)
    pair = 2
    squares = jnp.zeros((rows, HEAD_SIZE), jnp.float32)
    for first in range(0, heads, pair):
        a = first // group
        stacked = jnp.concatenate(
            [
                jnp.concatenate([query_ref[:, h * HEAD_SIZE : (h + 1) * HEAD_SIZE], eye], axis=1)
                for h in range(first, first + pair)
            ],
            axis=0,
        )
        scores = [
            lax.dot_general(
                stacked,
                key_ext[a, at : at + step, :],
                (((1,), (1,)), ((), ())),
                preferred_element_type=jnp.float32,
            )
            for at in range(0, span, step)
        ]
        best = functools.reduce(jnp.maximum, scores)
        best = jnp.max(best, axis=1, keepdims=True)
        total = None
        for i, part in enumerate(scores):
            probs = jnp.exp2((part - best) * rate).astype(jnp.bfloat16)
            term = jnp.dot(
                probs,
                value_ext[a, i * step : (i + 1) * step, :],
                preferred_element_type=jnp.float32,
            )
            total = term if total is None else total + term
        attended = (total[:, 0:HEAD_SIZE] / total[:, HEAD_SIZE:]).astype(jnp.bfloat16)
        for j in range(pair):
            cols = slice((first + j) * HEAD_SIZE, (first + j + 1) * HEAD_SIZE)
            state = residual_ref[:, cols].astype(jnp.float32) + attended[
                j * rows : (j + 1) * rows
            ].astype(jnp.float32)
            hidden_ref[:, cols] = state
            squares = squares + state * state
    meansq = jnp.sum(squares, axis=1, keepdims=True) / float(heads * HEAD_SIZE)
    inverse = lax.rsqrt(meansq + 1e-06)
    for h in range(heads):
        cols = slice(h * HEAD_SIZE, (h + 1) * HEAD_SIZE)
        normed_ref[:, cols] = (hidden_ref[:, cols] * inverse * gain_ref[:, cols]).astype(
            jnp.bfloat16
        )


def attend(queries, residual, gain, messages):
    rows, features = queries.shape
    count = len(messages)
    kv_heads = messages[0].shape[1] // (2 * HEAD_SIZE)
    vmem = pl.BlockSpec(memory_space=pltpu.VMEM)
    span = count * rows
    return pl.pallas_call(
        functools.partial(attend_kernel, count),
        out_shape=(
            jax.ShapeDtypeStruct((rows, features), jnp.float32),
            jax.ShapeDtypeStruct((rows, features), jnp.bfloat16),
        ),
        in_specs=[vmem] * (3 + count),
        out_specs=(vmem, vmem),
        scratch_shapes=[
            pltpu.VMEM((kv_heads, span, 2 * HEAD_SIZE), jnp.bfloat16),
            pltpu.VMEM((kv_heads, span, 2 * HEAD_SIZE), jnp.bfloat16),
        ],
        compiler_params=pltpu.CompilerParams(vmem_limit_bytes=40 * 1024 * 1024),
        cost_estimate=pl.CostEstimate(
            flops=8 * rows * span * features, bytes_accessed=8 * 1024 * 1024, transcendentals=0
        ),
        name="attend",
    )(queries, residual, gain.reshape(1, features), *messages)


def expert_kernel(blocks, *refs):
    own_ref = refs[0]
    tokens = refs[1 : 1 + blocks]
    messages = refs[1 + blocks : 1 + 2 * blocks]
    weights = refs[1 + 2 * blocks : 1 + 2 * blocks + 3 * CORES]
    outs = refs[1 + 2 * blocks + 3 * CORES : 1 + 3 * blocks + 3 * CORES]
    rows, features = tokens[0].shape
    top = 8
    if blocks == 1:
        normed = tokens[0][...]
    else:
        normed = jnp.concatenate([ref[...] for ref in tokens], axis=0)
    shares, acts = [], []
    for e in range(CORES):
        gate_ref, up_ref = weights[3 * e], weights[3 * e + 1]
        gate = jnp.dot(normed, gate_ref[0], preferred_element_type=jnp.float32)
        upper = jnp.dot(normed, up_ref[0], preferred_element_type=jnp.float32)
        acts.append((gate / (1.0 + jnp.exp(-gate)) * upper).astype(jnp.bfloat16))
        columns = []
        for ref in messages:
            extra = ref[...].astype(jnp.float32)
            named = extra[0:top, 0:128]
            value = extra[top : 2 * top, 0:128] + extra[0:top, 128:256]
            hit = jnp.where(named == own_ref[e].astype(jnp.float32), value, 0.0)
            line = jnp.sum(hit, axis=0, keepdims=True)
            columns.append(jnp.broadcast_to(line, (rows, rows)).T)
        shares.append(columns)
    step = 512
    for at in range(0, features, step):
        parts = [
            jnp.dot(acts[e], weights[3 * e + 2][0, :, at : at + step], preferred_element_type=jnp.float32)
            .astype(jnp.bfloat16)
            .astype(jnp.float32)
            for e in range(CORES)
        ]
        for b in range(blocks):
            for c in range(0, step, HEAD_SIZE):
                mixed = sum(
                    shares[e][b] * parts[e][b * rows : (b + 1) * rows, c : c + HEAD_SIZE]
                    for e in range(CORES)
                )
                outs[b][:, at + c : at + c + HEAD_SIZE] = mixed.astype(jnp.bfloat16)


def run_experts(own, tokens, messages, weights):
    rows, features = tokens[0].shape
    blocks = len(tokens)
    hidden = weights[0].shape[2]
    vmem = pl.BlockSpec(memory_space=pltpu.VMEM)
    tail = pl.BlockSpec((EXTRA, messages[0].shape[1]), lambda i: (rows // EXTRA, 0))

    def whole(shape):
        return pl.BlockSpec(shape, lambda i: (0,) * len(shape))

    return pl.pallas_call(
        functools.partial(expert_kernel, blocks),
        grid=(1,),
        out_shape=[jax.ShapeDtypeStruct((rows, features), jnp.bfloat16)] * blocks,
        in_specs=[pl.BlockSpec(memory_space=pltpu.SMEM)]
        + [whole((rows, features))] * blocks
        + [tail] * blocks
        + [whole(w.shape) for w in weights],
        out_specs=[whole((rows, features))] * blocks,
        compiler_params=pltpu.CompilerParams(vmem_limit_bytes=48 * 1024 * 1024),
        cost_estimate=pl.CostEstimate(
            flops=12 * blocks * rows * features * hidden,
            bytes_accessed=12 * features * hidden,
            transcendentals=0,
        ),
        name="experts",
    )(own, *tokens, *messages, *weights)


def add_parts(*parts):
    total = parts[0].astype(jnp.float32)
    for part in parts[1:]:
        total = total + part.astype(jnp.float32)
    return total.astype(jnp.bfloat16)


def ring_device(
    queries,
    rotated_keys,
    value_matrix,
    stretch_pos,
    residual,
    norm_gain,
    routes,
    combine,
    gate_weight,
    up_weight,
    down_weight,
):
    chips = lax.axis_size("ctx") // CORES
    far = chips // 2
    onward, back, swap = ring_pairs(chips)

    def send(array, pairs):
        return lax.ppermute(array, "ctx", pairs)

    message = pack_message(stretch_pos, rotated_keys, value_matrix, routes, combine)
    twins = tuple(send(w, swap) for w in (gate_weight, up_weight, down_weight))
    weights = (gate_weight, up_weight, down_weight) + twins
    me = lax.axis_index("ctx").astype(jnp.int32)
    own = jnp.stack([me, me ^ 1])

    left, right = {0: message}, {0: message}
    for hop in range(1, far + 1):
        left[hop] = send(left[hop - 1], onward)
        if hop < far:
            right[hop] = send(right[hop - 1], back)
    plane = [message] + [left[h] for h in range(1, far + 1)] + [right[h] for h in range(1, far)]
    everything = plane + [send(m, swap) for m in plane]
    hidden_state, normed = attend(queries, residual, norm_gain, everything)

    half = normed.shape[0] // 2
    from_left, from_right = {0: normed}, {0: normed}
    for hop in range(1, far):
        from_left[hop] = send(from_left[hop - 1], onward)
        from_right[hop] = send(from_right[hop - 1], back)
    upper_half = send(from_left[far - 1][:half], onward)
    lower_half = send(from_right[far - 1][half:], back)

    out_left, out_right = {}, {}
    (own_out,) = run_experts(own, [normed], [message], weights)
    for hop in range(1, far):
        out_left[hop], out_right[hop] = run_experts(
            own, [from_left[hop], from_right[hop]], [left[hop], right[hop]], weights
        )
    (out_far,) = run_experts(
        own, [jnp.concatenate([upper_half, lower_half], axis=0)], [left[far]], weights
    )

    moving_on = send(out_far[:half], onward)
    moving_back = send(out_far[half:], back)
    for hop in range(far - 1, 0, -1):
        if hop == far - 1:
            ready_on = jnp.concatenate(
                [add_parts(moving_on, out_right[hop][:half]), out_right[hop][half:]], axis=0
            )
            ready_back = jnp.concatenate(
                [out_left[hop][:half], add_parts(moving_back, out_left[hop][half:])], axis=0
            )
        else:
            ready_on = add_parts(moving_on, out_right[hop])
            ready_back = add_parts(moving_back, out_left[hop])
        moving_on = send(ready_on, onward)
        moving_back = send(ready_back, back)
    mixture = (
        own_out.astype(jnp.float32)
        + moving_on.astype(jnp.float32)
        + moving_back.astype(jnp.float32)
    )
    return (hidden_state + mixture).astype(jnp.bfloat16)


def exchange_device(
    queries,
    rotated_keys,
    value_matrix,
    stretch_pos,
    residual,
    norm_gain,
    routes,
    combine,
    gate_weight,
    up_weight,
    down_weight,
):
    tok_rows = queries.shape[0]
    kv_heads = rotated_keys.shape[1] // HEAD_SIZE
    head_group = queries.shape[1] // rotated_keys.shape[1]
    ctx_count = lax.axis_size("ctx")
    positions = stretch_pos[0] * tok_rows + jnp.arange(tok_rows, dtype=jnp.int32)
    latest = jnp.max(positions)
    query_heads = queries.reshape(tok_rows, kv_heads, head_group, HEAD_SIZE)
    scale_factor = 1.0 / math.sqrt(HEAD_SIZE)

    def update(state, key_block, value_block, key_pos):
        best, total, accum = state
        scores = (
            jnp.einsum(
                "tagd,sad->agts",
                query_heads,
                key_block.reshape(-1, kv_heads, HEAD_SIZE),
                preferred_element_type=jnp.float32,
            )
            * scale_factor
        )
        scores = jnp.where(
            key_pos[None, None, None, :] <= positions[None, None, :, None], scores, jnp.float32(NEG)
        )
        fresh = jnp.maximum(best, jnp.max(scores, axis=-1))
        shrink = jnp.exp(best - fresh)
        expo = jnp.exp(scores - fresh[..., None])
        total = total * shrink + jnp.sum(expo, axis=-1)
        weighted = jnp.einsum(
            "agts,sad->agtd",
            expo.astype(jnp.bfloat16),
            value_block.reshape(-1, kv_heads, HEAD_SIZE),
            preferred_element_type=jnp.float32,
        )
        accum = accum * shrink[..., None] + weighted
        return (fresh, total, accum)

    start_state = (
        jnp.full((kv_heads, head_group, tok_rows), NEG, jnp.float32),
        jnp.zeros((kv_heads, head_group, tok_rows), jnp.float32),
        jnp.zeros((kv_heads, head_group, tok_rows, HEAD_SIZE), jnp.float32),
    )
    key_part = lax.all_gather(rotated_keys, "ctx", axis=0, tiled=True)
    value_part = lax.all_gather(value_matrix, "ctx", axis=0, tiled=True)
    pos_part = lax.all_gather(positions, "ctx", axis=0, tiled=True)
    span = key_part.shape[0]
    width = 512
    blocks = span // width
    stacked = (
        key_part.reshape(blocks, width, -1),
        value_part.reshape(blocks, width, -1),
        pos_part.reshape(blocks, width),
    )

    def advance(inner, item):
        key_block, value_block, key_pos = item
        result = lax.cond(
            jnp.min(key_pos) > latest,
            lambda kept: kept,
            lambda kept: update(kept, key_block, value_block, key_pos),
            inner,
        )
        return (result, None)

    final, unused = lax.scan(advance, start_state, stacked)
    best, total, accum = final
    attended = (
        jnp.transpose(accum / total[..., None], (2, 0, 1, 3))
        .reshape(tok_rows, -1)
        .astype(jnp.bfloat16)
    )
    hidden_state = residual.astype(jnp.float32) + attended.astype(jnp.float32)
    meansq = jnp.mean(hidden_state * hidden_state, axis=-1, keepdims=True)
    normed = (hidden_state * lax.rsqrt(meansq + 1e-06) * norm_gain).astype(jnp.bfloat16)
    local_experts = gate_weight.shape[0]
    total_experts = local_experts * ctx_count
    top_count = routes.shape[1]
    capacity = min(
        tok_rows,
        tok_rows * top_count // total_experts + max(1, tok_rows * top_count // (8 * total_experts)),
    )
    flat_routes = routes.reshape(-1)
    onehot = (flat_routes[:, None] == jnp.arange(total_experts, dtype=jnp.int32)[None, :]).astype(
        jnp.int32
    )
    earlier = jnp.cumsum(onehot, axis=0) - onehot
    ranking = jnp.sum(earlier * onehot, axis=1)
    slot_ids = flat_routes * capacity + ranking
    selector = jnp.any(
        slot_ids.reshape(tok_rows, top_count)[:, :, None]
        == jnp.arange(total_experts * capacity, dtype=jnp.int32)[None, None, :],
        axis=1,
    ).astype(jnp.bfloat16)
    outgoing = jnp.einsum("ts,td->sd", selector, normed, preferred_element_type=jnp.float32).astype(
        jnp.bfloat16
    )
    outgoing = outgoing.reshape(ctx_count, local_experts, capacity, D)
    incoming = lax.all_to_all(outgoing, "ctx", split_axis=0, concat_axis=0, tiled=True)
    gate = jnp.einsum("secd,edh->sech", incoming, gate_weight, preferred_element_type=jnp.float32)
    upper = jnp.einsum("secd,edh->sech", incoming, up_weight, preferred_element_type=jnp.float32)
    act = (jax.nn.silu(gate) * upper).astype(jnp.bfloat16)
    returned = lax.all_to_all(
        jnp.einsum("sech,ehd->secd", act, down_weight, preferred_element_type=jnp.float32).astype(
            jnp.bfloat16
        ),
        "ctx",
        split_axis=0,
        concat_axis=0,
        tiled=True,
    )
    flat_back = returned.reshape(total_experts * capacity, D)
    picked = jnp.take(flat_back, slot_ids, axis=0).reshape(tok_rows, top_count, D)
    mixture = jnp.sum(combine[:, :, None] * picked.astype(jnp.float32), axis=1)
    return (hidden_state + mixture).astype(jnp.bfloat16)


def solution(mesh):
    placed = (
        P(("groups", "ctx"), None),
        P(("groups", "ctx"), None),
        P(("groups", "ctx"), None),
        P(("groups", "ctx")),
        P(("groups", "ctx"), None),
        P(),
        P(("groups", "ctx"), None),
        P(("groups", "ctx"), None),
        P("ctx", None, None),
        P("ctx", None, None),
        P("ctx", None, None),
    )
    ctx_count = mesh.shape["ctx"]

    def on_device(*arguments):
        routes, gate_weight = arguments[6], arguments[8]
        dense = 4 * routes.shape[1] >= gate_weight.shape[0] * ctx_count
        ringed = gate_weight.shape[0] == 1 and ctx_count % (2 * CORES) == 0
        return (ring_device if dense and ringed else exchange_device)(*arguments)

    return jax.shard_map(
        on_device, mesh=mesh, in_specs=placed, out_specs=P(("groups", "ctx"), None), check_vma=False
    )
```

```python
import functools
import math

import jax
import jax.numpy as jnp
from jax import lax
from jax.experimental import pallas as pl
from jax.experimental.pallas import tpu as pltpu
from jax.sharding import PartitionSpec as P

D = 2048
HEAD_SIZE = 128
CORES = 2
EXTRA = 16


NEG = -1e30


def ring_pairs(chips):
    order = list(range(0, chips, 2)) + list(range(chips - 1, 0, -2))
    onward = [
        (order[i] * CORES + core, order[(i + 1) % chips] * CORES + core)
        for i in range(chips)
        for core in range(CORES)
    ]
    back = [(b, a) for a, b in onward]
    swap = [(i, i ^ 1) for i in range(chips * CORES)]
    return onward, back, swap


def pack_kernel(pos_ref, key_ref, value_ref, routes_ref, combine_ref, out_ref):
    rows, width = key_ref.shape
    top = routes_ref.shape[0]
    out_ref[0:rows, 0:width] = key_ref[...]
    out_ref[0:rows, width : 2 * width] = value_ref[...]
    weight = combine_ref[...]
    high = weight.astype(jnp.bfloat16).astype(jnp.float32)
    low = weight - high
    names = routes_ref[...].astype(jnp.float32)
    place = jnp.full((EXTRA, 2 * width - 2 * rows), pos_ref[0].astype(jnp.float32), jnp.float32)
    tail = slice(rows, rows + EXTRA)
    out_ref[tail, 0:rows] = jnp.concatenate([names, high], axis=0).astype(jnp.bfloat16)
    out_ref[tail, rows : 2 * rows] = jnp.concatenate([low, jnp.zeros_like(low)], axis=0).astype(
        jnp.bfloat16
    )
    out_ref[tail, 2 * rows : 2 * width] = place.astype(jnp.bfloat16)


def pack_message(stretch_pos, keys, values, routes, combine):
    rows, width = keys.shape
    vmem = pl.BlockSpec(memory_space=pltpu.VMEM)
    return pl.pallas_call(
        pack_kernel,
        out_shape=jax.ShapeDtypeStruct((rows + EXTRA, 2 * width), jnp.bfloat16),
        in_specs=[pl.BlockSpec(memory_space=pltpu.SMEM), vmem, vmem, vmem, vmem],
        out_specs=vmem,
        name="pack_message",
    )(stretch_pos, keys, values, routes.T, combine.T)


def attend_kernel(count, *refs):
    query_hbm, residual_hbm, gain_hbm = refs[:3]
    messages = refs[3 : 3 + count]
    hidden_ref, upper_ref, lower_ref, key_ext, value_ext = refs[3 + count : 8 + count]
    query_ref, residual_ref, gain_ref, arrived = refs[8 + count :]
    fetches = [
        pltpu.make_async_copy(source, target, arrived.at[i])
        for i, (source, target) in enumerate(
            [(query_hbm, query_ref), (residual_hbm, residual_ref), (gain_hbm, gain_ref)]
        )
    ]
    for fetch in fetches:
        fetch.start()
    rows = query_ref.shape[0]
    kv_heads = key_ext.shape[0]
    heads = query_ref.shape[1] // HEAD_SIZE
    group = heads // kv_heads
    span = count * rows
    width = kv_heads * HEAD_SIZE
    sub = lax.broadcasted_iota(jnp.int32, (rows, rows), 0)
    lane = lax.broadcasted_iota(jnp.int32, (rows, rows), 1)
    ahead = (sub - lane).astype(jnp.float32)
    own_pos = messages[0][rows : rows + EXTRA, 256 : 256 + rows][0:1].astype(jnp.float32)
    ones = jnp.ones((rows, HEAD_SIZE), jnp.bfloat16)
    for block in range(count):
        ref = messages[block]
        at = slice(block * rows, (block + 1) * rows)
        pos = ref[rows : rows + EXTRA, 256 : 256 + rows][0:1].astype(jnp.float32)
        later = (pos - own_pos) * float(rows) + ahead
        bias = jnp.where(later > 0.0, NEG, 0.0).astype(jnp.bfloat16)
        for a in range(kv_heads):
            key_ext[a, at, 0:HEAD_SIZE] = ref[0:rows, a * HEAD_SIZE : (a + 1) * HEAD_SIZE]
            key_ext[a, at, HEAD_SIZE : HEAD_SIZE + rows] = bias
            value_ext[a, at, 0:HEAD_SIZE] = ref[
                0:rows, width + a * HEAD_SIZE : width + (a + 1) * HEAD_SIZE
            ]
            value_ext[a, at, HEAD_SIZE : 2 * HEAD_SIZE] = ones
    eye = jnp.where(sub == lane, 1.0, 0.0).astype(jnp.bfloat16)
    for fetch in fetches:
        fetch.wait()
    rate = math.log2(math.e) / math.sqrt(HEAD_SIZE)
    step = min(512, span)
    pair = 2
    squares = jnp.zeros((rows, HEAD_SIZE), jnp.float32)
    for first in range(0, heads, pair):
        a = first // group
        stacked = jnp.concatenate(
            [
                jnp.concatenate([query_ref[:, h * HEAD_SIZE : (h + 1) * HEAD_SIZE], eye], axis=1)
                for h in range(first, first + pair)
            ],
            axis=0,
        )
        scores = [
            lax.dot_general(
                stacked,
                key_ext[a, at : at + step, :],
                (((1,), (1,)), ((), ())),
                preferred_element_type=jnp.float32,
            )
            for at in range(0, span, step)
        ]
        best = functools.reduce(jnp.maximum, scores)
        best = jnp.max(best, axis=1, keepdims=True)
        total = None
        for i, part in enumerate(scores):
            probs = jnp.exp2((part - best) * rate).astype(jnp.bfloat16)
            term = jnp.dot(
                probs,
                value_ext[a, i * step : (i + 1) * step, :],
                preferred_element_type=jnp.float32,
            )
            total = term if total is None else total + term
        attended = (total[:, 0:HEAD_SIZE] / total[:, HEAD_SIZE:]).astype(jnp.bfloat16)
        for j in range(pair):
            cols = slice((first + j) * HEAD_SIZE, (first + j + 1) * HEAD_SIZE)
            state = residual_ref[:, cols].astype(jnp.float32) + attended[
                j * rows : (j + 1) * rows
            ].astype(jnp.float32)
            hidden_ref[:, cols] = state
            squares = squares + state * state
    meansq = jnp.sum(squares, axis=1, keepdims=True) / float(heads * HEAD_SIZE)
    inverse = lax.rsqrt(meansq + 1e-06)
    for h in range(heads):
        cols = slice(h * HEAD_SIZE, (h + 1) * HEAD_SIZE)
        normed = (hidden_ref[:, cols] * inverse * gain_ref[:, cols]).astype(jnp.bfloat16)
        upper_ref[:, cols] = normed[: rows // 2]
        lower_ref[:, cols] = normed[rows // 2 :]


def attend(queries, residual, gain, messages):
    rows, features = queries.shape
    count = len(messages)
    kv_heads = messages[0].shape[1] // (2 * HEAD_SIZE)
    vmem = pl.BlockSpec(memory_space=pltpu.VMEM)
    span = count * rows
    return pl.pallas_call(
        functools.partial(attend_kernel, count),
        out_shape=(
            jax.ShapeDtypeStruct((rows, features), jnp.float32),
            jax.ShapeDtypeStruct((rows // 2, features), jnp.bfloat16),
            jax.ShapeDtypeStruct((rows // 2, features), jnp.bfloat16),
        ),
        in_specs=[pl.BlockSpec(memory_space=pl.ANY)] * 3 + [vmem] * count,
        out_specs=(vmem, vmem, vmem),
        scratch_shapes=[
            pltpu.VMEM((kv_heads, span, 2 * HEAD_SIZE), jnp.bfloat16),
            pltpu.VMEM((kv_heads, span, 2 * HEAD_SIZE), jnp.bfloat16),
            pltpu.VMEM((rows, features), jnp.bfloat16),
            pltpu.VMEM((rows, features), jnp.bfloat16),
            pltpu.VMEM((1, features), jnp.float32),
            pltpu.SemaphoreType.DMA((3,)),
        ],
        compiler_params=pltpu.CompilerParams(vmem_limit_bytes=28 * 1024 * 1024),
        cost_estimate=pl.CostEstimate(
            flops=8 * rows * span * features, bytes_accessed=8 * 1024 * 1024, transcendentals=0
        ),
        name="attend",
    )(queries, residual, gain.reshape(1, features), *messages)


def expert_kernel(places, count, *refs):
    pieces = len(places)
    tokens = refs[:pieces]
    messages = refs[pieces : pieces + count]
    weights = refs[pieces + count : pieces + count + 3 * CORES]
    outs = refs[pieces + count + 3 * CORES :]
    rows, features = tokens[0].shape
    whole = messages[0].shape[0] - EXTRA
    top = EXTRA // 2
    me = lax.axis_index("ctx")
    normed = jnp.concatenate([ref[...] for ref in tokens], axis=0)
    shares, acts = [], []
    for e in range(CORES):
        gate_ref, up_ref = weights[3 * e], weights[3 * e + 1]
        gate = jnp.dot(normed, gate_ref[0], preferred_element_type=jnp.float32)
        upper = jnp.dot(normed, up_ref[0], preferred_element_type=jnp.float32)
        acts.append((gate / (1.0 + jnp.exp(-gate)) * upper).astype(jnp.bfloat16))
        name = jnp.bitwise_xor(me, e).astype(jnp.float32)
        columns = []
        for ref in messages:
            extra = ref[whole : whole + EXTRA, 0 : 2 * whole].astype(jnp.float32)
            value = extra[top : 2 * top, 0:whole] + extra[0:top, whole : 2 * whole]
            hit = jnp.where(extra[0:top, 0:whole] == name, value, 0.0)
            line = jnp.sum(hit, axis=0, keepdims=True)
            columns.append(jnp.broadcast_to(line, (whole, whole)).T)
        shares.append([columns[m][half * rows : (half + 1) * rows] for m, half in places])
    step = 512
    for at in range(0, features, step):
        parts = [
            jnp.dot(acts[e], weights[3 * e + 2][0, :, at : at + step], preferred_element_type=jnp.float32)
            .astype(jnp.bfloat16)
            .astype(jnp.float32)
            for e in range(CORES)
        ]
        for b in range(pieces):
            for c in range(0, step, whole):
                mixed = sum(
                    shares[e][b] * parts[e][b * rows : (b + 1) * rows, c : c + whole]
                    for e in range(CORES)
                )
                outs[b][:, at + c : at + c + whole] = mixed.astype(jnp.bfloat16)


def run_experts(pieces, messages, weights):
    tokens = [piece[0] for piece in pieces]
    rows, features = tokens[0].shape
    hidden = weights[0].shape[2]
    vmem = pl.BlockSpec(memory_space=pltpu.VMEM)
    return pl.pallas_call(
        functools.partial(expert_kernel, [piece[1:] for piece in pieces], len(messages)),
        out_shape=[jax.ShapeDtypeStruct((rows, features), jnp.bfloat16)] * len(pieces),
        in_specs=[vmem] * (len(pieces) + len(messages) + len(weights)),
        out_specs=[vmem] * len(pieces),
        compiler_params=pltpu.CompilerParams(vmem_limit_bytes=24 * 1024 * 1024),
        cost_estimate=pl.CostEstimate(
            flops=12 * len(pieces) * rows * features * hidden,
            bytes_accessed=12 * features * hidden,
            transcendentals=0,
        ),
        name="experts",
    )(*tokens, *messages, *weights)


def add_parts(*parts):
    total = parts[0].astype(jnp.float32)
    for part in parts[1:]:
        total = total + part.astype(jnp.float32)
    return total.astype(jnp.bfloat16)


def ring_device(
    queries,
    rotated_keys,
    value_matrix,
    stretch_pos,
    residual,
    norm_gain,
    routes,
    combine,
    gate_weight,
    up_weight,
    down_weight,
):
    chips = lax.axis_size("ctx") // CORES
    far = chips // 2
    onward, back, swap = ring_pairs(chips)

    def send(array, pairs):
        return lax.ppermute(array, "ctx", pairs)

    message = pack_message(stretch_pos, rotated_keys, value_matrix, routes, combine)
    twins = tuple(send(w, swap) for w in (gate_weight, up_weight, down_weight))

    left, right = {0: message}, {0: message}
    for hop in range(1, far + 1):
        left[hop] = send(left[hop - 1], onward)
        if hop < far:
            right[hop] = send(right[hop - 1], back)
    plane = [message] + [left[h] for h in range(1, far + 1)] + [right[h] for h in range(1, far)]
    everything = plane + [send(m, swap) for m in plane]
    norm_gain, twins = lax.optimization_barrier((norm_gain, twins))
    weights = (gate_weight, up_weight, down_weight) + twins
    hidden_state, upper, lower = attend(queries, residual, norm_gain, everything)

    from_left = {(0, 0): upper, (0, 1): lower}
    from_right = {(0, 0): upper, (0, 1): lower}
    out_left, out_right = {}, {}

    def pieces_of(hop):
        return [
            (from_left[hop, 0], 0, 0),
            (from_left[hop, 1], 0, 1),
            (from_right[hop, 0], 1, 0),
            (from_right[hop, 1], 1, 1),
        ]

    for hop in range(1, far + 1):
        first_left, first_right = from_left[hop - 1, 0], from_right[hop - 1, 1]
        if hop == 2:
            own_out = run_experts([(upper, 0, 0), (lower, 0, 1)], [message], weights)
            first_left, first_right, own_out = lax.optimization_barrier(
                (first_left, first_right, own_out)
            )
        if hop > 2:
            outs = run_experts(pieces_of(hop - 2), [left[hop - 2], right[hop - 2]], weights)
            first_left, first_right, outs = lax.optimization_barrier((first_left, first_right, outs))
            out_left[hop - 2], out_right[hop - 2] = outs[:2], outs[2:]
        from_left[hop, 0] = send(first_left, onward)
        from_right[hop, 1] = send(first_right, back)
        if hop < far:
            from_left[hop, 1] = send(from_left[hop - 1, 1], onward)
            from_right[hop, 0] = send(from_right[hop - 1, 0], back)
    outs = run_experts(pieces_of(far - 1), [left[far - 1], right[far - 1]], weights)
    out_left[far - 1], out_right[far - 1] = outs[:2], outs[2:]
    far_upper, far_lower = run_experts(
        [(from_left[far, 0], 0, 0), (from_right[far, 1], 0, 1)], [left[far]], weights
    )

    sums_on = {1: send(out_right[far - 1][1], onward)}
    sums_back = {0: send(out_left[far - 1][0], back)}
    sums_on[0] = send(far_upper, onward)
    sums_back[1] = send(far_lower, back)
    for hop in range(far - 1, 0, -1):
        if hop < far - 1:
            sums_on[1] = send(add_parts(sums_on[1], out_right[hop][1]), onward)
            sums_back[0] = send(add_parts(sums_back[0], out_left[hop][0]), back)
        sums_on[0] = send(add_parts(sums_on[0], out_right[hop][0]), onward)
        sums_back[1] = send(add_parts(sums_back[1], out_left[hop][1]), back)
    mixture = jnp.concatenate(
        [
            own_out[half].astype(jnp.float32)
            + sums_on[half].astype(jnp.float32)
            + sums_back[half].astype(jnp.float32)
            for half in range(2)
        ],
        axis=0,
    )
    return (hidden_state + mixture).astype(jnp.bfloat16)


def exchange_device(
    queries,
    rotated_keys,
    value_matrix,
    stretch_pos,
    residual,
    norm_gain,
    routes,
    combine,
    gate_weight,
    up_weight,
    down_weight,
):
    tok_rows = queries.shape[0]
    kv_heads = rotated_keys.shape[1] // HEAD_SIZE
    head_group = queries.shape[1] // rotated_keys.shape[1]
    ctx_count = lax.axis_size("ctx")
    positions = stretch_pos[0] * tok_rows + jnp.arange(tok_rows, dtype=jnp.int32)
    latest = jnp.max(positions)
    query_heads = queries.reshape(tok_rows, kv_heads, head_group, HEAD_SIZE)
    scale_factor = 1.0 / math.sqrt(HEAD_SIZE)

    def update(state, key_block, value_block, key_pos):
        best, total, accum = state
        scores = (
            jnp.einsum(
                "tagd,sad->agts",
                query_heads,
                key_block.reshape(-1, kv_heads, HEAD_SIZE),
                preferred_element_type=jnp.float32,
            )
            * scale_factor
        )
        scores = jnp.where(
            key_pos[None, None, None, :] <= positions[None, None, :, None], scores, jnp.float32(NEG)
        )
        fresh = jnp.maximum(best, jnp.max(scores, axis=-1))
        shrink = jnp.exp(best - fresh)
        expo = jnp.exp(scores - fresh[..., None])
        total = total * shrink + jnp.sum(expo, axis=-1)
        weighted = jnp.einsum(
            "agts,sad->agtd",
            expo.astype(jnp.bfloat16),
            value_block.reshape(-1, kv_heads, HEAD_SIZE),
            preferred_element_type=jnp.float32,
        )
        accum = accum * shrink[..., None] + weighted
        return (fresh, total, accum)

    start_state = (
        jnp.full((kv_heads, head_group, tok_rows), NEG, jnp.float32),
        jnp.zeros((kv_heads, head_group, tok_rows), jnp.float32),
        jnp.zeros((kv_heads, head_group, tok_rows, HEAD_SIZE), jnp.float32),
    )
    key_part = lax.all_gather(rotated_keys, "ctx", axis=0, tiled=True)
    value_part = lax.all_gather(value_matrix, "ctx", axis=0, tiled=True)
    pos_part = lax.all_gather(positions, "ctx", axis=0, tiled=True)
    span = key_part.shape[0]
    width = 512
    blocks = span // width
    stacked = (
        key_part.reshape(blocks, width, -1),
        value_part.reshape(blocks, width, -1),
        pos_part.reshape(blocks, width),
    )

    def advance(inner, item):
        key_block, value_block, key_pos = item
        result = lax.cond(
            jnp.min(key_pos) > latest,
            lambda kept: kept,
            lambda kept: update(kept, key_block, value_block, key_pos),
            inner,
        )
        return (result, None)

    final, unused = lax.scan(advance, start_state, stacked)
    best, total, accum = final
    attended = (
        jnp.transpose(accum / total[..., None], (2, 0, 1, 3))
        .reshape(tok_rows, -1)
        .astype(jnp.bfloat16)
    )
    hidden_state = residual.astype(jnp.float32) + attended.astype(jnp.float32)
    meansq = jnp.mean(hidden_state * hidden_state, axis=-1, keepdims=True)
    normed = (hidden_state * lax.rsqrt(meansq + 1e-06) * norm_gain).astype(jnp.bfloat16)
    local_experts = gate_weight.shape[0]
    total_experts = local_experts * ctx_count
    top_count = routes.shape[1]
    capacity = min(
        tok_rows,
        tok_rows * top_count // total_experts + max(1, tok_rows * top_count // (8 * total_experts)),
    )
    flat_routes = routes.reshape(-1)
    onehot = (flat_routes[:, None] == jnp.arange(total_experts, dtype=jnp.int32)[None, :]).astype(
        jnp.int32
    )
    earlier = jnp.cumsum(onehot, axis=0) - onehot
    ranking = jnp.sum(earlier * onehot, axis=1)
    slot_ids = flat_routes * capacity + ranking
    selector = jnp.any(
        slot_ids.reshape(tok_rows, top_count)[:, :, None]
        == jnp.arange(total_experts * capacity, dtype=jnp.int32)[None, None, :],
        axis=1,
    ).astype(jnp.bfloat16)
    outgoing = jnp.einsum("ts,td->sd", selector, normed, preferred_element_type=jnp.float32).astype(
        jnp.bfloat16
    )
    outgoing = outgoing.reshape(ctx_count, local_experts, capacity, D)
    incoming = lax.all_to_all(outgoing, "ctx", split_axis=0, concat_axis=0, tiled=True)
    gate = jnp.einsum("secd,edh->sech", incoming, gate_weight, preferred_element_type=jnp.float32)
    upper = jnp.einsum("secd,edh->sech", incoming, up_weight, preferred_element_type=jnp.float32)
    act = (jax.nn.silu(gate) * upper).astype(jnp.bfloat16)
    returned = lax.all_to_all(
        jnp.einsum("sech,ehd->secd", act, down_weight, preferred_element_type=jnp.float32).astype(
            jnp.bfloat16
        ),
        "ctx",
        split_axis=0,
        concat_axis=0,
        tiled=True,
    )
    flat_back = returned.reshape(total_experts * capacity, D)
    picked = jnp.take(flat_back, slot_ids, axis=0).reshape(tok_rows, top_count, D)
    mixture = jnp.sum(combine[:, :, None] * picked.astype(jnp.float32), axis=1)
    return (hidden_state + mixture).astype(jnp.bfloat16)


def solution(mesh):
    placed = (
        P(("groups", "ctx"), None),
        P(("groups", "ctx"), None),
        P(("groups", "ctx"), None),
        P(("groups", "ctx")),
        P(("groups", "ctx"), None),
        P(),
        P(("groups", "ctx"), None),
        P(("groups", "ctx"), None),
        P("ctx", None, None),
        P("ctx", None, None),
        P("ctx", None, None),
    )
    ctx_count = mesh.shape["ctx"]

    def on_device(*arguments):
        routes, gate_weight = arguments[6], arguments[8]
        dense = 4 * routes.shape[1] >= gate_weight.shape[0] * ctx_count
        ringed = gate_weight.shape[0] == 1 and ctx_count % (2 * CORES) == 0
        ringed = ringed and ctx_count >= 4 * CORES and 2 * routes.shape[1] == EXTRA
        return (ring_device if dense and ringed else exchange_device)(*arguments)

    return jax.shard_map(
        on_device, mesh=mesh, in_specs=placed, out_specs=P(("groups", "ctx"), None), check_vma=False
    )
```

```python
import functools
import math

import jax
import jax.numpy as jnp
from jax import lax
from jax.experimental import pallas as pl
from jax.experimental.pallas import tpu as pltpu
from jax.sharding import PartitionSpec as P

D = 2048
HEAD_SIZE = 128
CORES = 2
EXTRA = 16


NEG = -1e30


def ring_pairs(chips):
    order = list(range(0, chips, 2)) + list(range(chips - 1, 0, -2))
    onward = [
        (order[i] * CORES + core, order[(i + 1) % chips] * CORES + core)
        for i in range(chips)
        for core in range(CORES)
    ]
    back = [(b, a) for a, b in onward]
    swap = [(i, i ^ 1) for i in range(chips * CORES)]
    return onward, back, swap


def pack_kernel(pos_ref, key_ref, value_ref, routes_ref, combine_ref, out_ref):
    rows, width = key_ref.shape
    top = routes_ref.shape[0]
    out_ref[0:rows, 0:width] = key_ref[...]
    out_ref[0:rows, width : 2 * width] = value_ref[...]
    weight = combine_ref[...]
    high = weight.astype(jnp.bfloat16).astype(jnp.float32)
    low = weight - high
    names = routes_ref[...].astype(jnp.float32)
    place = jnp.full((EXTRA, 2 * width - 2 * rows), pos_ref[0].astype(jnp.float32), jnp.float32)
    tail = slice(rows, rows + EXTRA)
    out_ref[tail, 0:rows] = jnp.concatenate([names, high], axis=0).astype(jnp.bfloat16)
    out_ref[tail, rows : 2 * rows] = jnp.concatenate([low, jnp.zeros_like(low)], axis=0).astype(
        jnp.bfloat16
    )
    out_ref[tail, 2 * rows : 2 * width] = place.astype(jnp.bfloat16)


def pack_message(stretch_pos, keys, values, routes, combine):
    rows, width = keys.shape
    vmem = pl.BlockSpec(memory_space=pltpu.VMEM)
    return pl.pallas_call(
        pack_kernel,
        out_shape=jax.ShapeDtypeStruct((rows + EXTRA, 2 * width), jnp.bfloat16),
        in_specs=[pl.BlockSpec(memory_space=pltpu.SMEM), vmem, vmem, vmem, vmem],
        out_specs=vmem,
        name="pack_message",
    )(stretch_pos, keys, values, routes.T, combine.T)


def stage_kernel(query_ref, residual_ref, gain_ref, stacked_ref, residual_out, gain_out):
    rows = query_ref.shape[0]
    halves = stacked_ref.shape[0]
    some = rows // halves
    sub = lax.broadcasted_iota(jnp.int32, (rows, rows), 0)
    lane = lax.broadcasted_iota(jnp.int32, (rows, rows), 1)
    eye = jnp.where(sub == lane, 1.0, 0.0).astype(jnp.bfloat16)
    for half in range(halves):
        mine = slice(half * some, (half + 1) * some)
        for h in range(query_ref.shape[1] // HEAD_SIZE):
            at = slice(h * some, (h + 1) * some)
            stacked_ref[half, at, 0:HEAD_SIZE] = query_ref[mine, h * HEAD_SIZE : (h + 1) * HEAD_SIZE]
            stacked_ref[half, at, HEAD_SIZE : HEAD_SIZE + rows] = eye[mine]
        residual_out[half] = residual_ref[mine, :]
    gain_out[...] = gain_ref[...]


def stage(queries, residual, gain):
    rows, features = queries.shape
    heads = features // HEAD_SIZE
    vmem = pl.BlockSpec(memory_space=pltpu.VMEM)
    return pl.pallas_call(
        stage_kernel,
        out_shape=(
            jax.ShapeDtypeStruct((2, heads * rows // 2, HEAD_SIZE + rows), jnp.bfloat16),
            jax.ShapeDtypeStruct((2, rows // 2, features), jnp.bfloat16),
            jax.ShapeDtypeStruct((1, features), jnp.float32),
        ),
        in_specs=[vmem] * 3,
        out_specs=(vmem,) * 3,
        cost_estimate=pl.CostEstimate(
            flops=0, bytes_accessed=10 * rows * features, transcendentals=0
        ),
        name="stage",
    )(queries, residual, gain.reshape(1, features))


def attend_kernel(count, half, *refs):
    stacked_ref, residual_ref, gain_ref = refs[:3]
    messages = refs[3 : 3 + count]
    hidden_ref, normed_ref, key_ext, value_ext = refs[3 + count :]
    some, features = residual_ref.shape[1:]
    rows = messages[0].shape[0] - EXTRA
    kv_heads = key_ext.shape[0]
    heads = features // HEAD_SIZE
    group = heads // kv_heads
    span = count * rows
    width = kv_heads * HEAD_SIZE
    sub = lax.broadcasted_iota(jnp.int32, (rows, rows), 0)
    lane = lax.broadcasted_iota(jnp.int32, (rows, rows), 1)
    ahead = (sub - lane).astype(jnp.float32)
    own_pos = messages[0][rows : rows + EXTRA, 256 : 256 + rows][0:1].astype(jnp.float32)
    ones = jnp.ones((rows, HEAD_SIZE), jnp.bfloat16)
    for block in range(count):
        ref = messages[block]
        at = slice(block * rows, (block + 1) * rows)
        pos = ref[rows : rows + EXTRA, 256 : 256 + rows][0:1].astype(jnp.float32)
        later = (pos - own_pos) * float(rows) + ahead
        bias = jnp.where(later > 0.0, NEG, 0.0).astype(jnp.bfloat16)
        for a in range(kv_heads):
            key_ext[a, at, 0:HEAD_SIZE] = ref[0:rows, a * HEAD_SIZE : (a + 1) * HEAD_SIZE]
            key_ext[a, at, HEAD_SIZE : HEAD_SIZE + rows] = bias
            value_ext[a, at, 0:HEAD_SIZE] = ref[
                0:rows, width + a * HEAD_SIZE : width + (a + 1) * HEAD_SIZE
            ]
            value_ext[a, at, HEAD_SIZE : 2 * HEAD_SIZE] = ones
    rate = math.log2(math.e) / math.sqrt(HEAD_SIZE)
    step = min(512, span)
    pair = 4
    squares = jnp.zeros((some, HEAD_SIZE), jnp.float32)
    for first in range(0, heads, pair):
        a = first // group
        stacked = stacked_ref[half, first * some : (first + pair) * some, :]
        scores = [
            lax.dot_general(
                stacked,
                key_ext[a, at : at + step, :],
                (((1,), (1,)), ((), ())),
                preferred_element_type=jnp.float32,
            )
            for at in range(0, span, step)
        ]
        best = functools.reduce(jnp.maximum, scores)
        best = jnp.max(best, axis=1, keepdims=True)
        total = None
        for i, part in enumerate(scores):
            probs = jnp.exp2((part - best) * rate).astype(jnp.bfloat16)
            term = jnp.dot(
                probs,
                value_ext[a, i * step : (i + 1) * step, :],
                preferred_element_type=jnp.float32,
            )
            total = term if total is None else total + term
        attended = (total[:, 0:HEAD_SIZE] / total[:, HEAD_SIZE:]).astype(jnp.bfloat16)
        for j in range(pair):
            cols = slice((first + j) * HEAD_SIZE, (first + j + 1) * HEAD_SIZE)
            state = residual_ref[half, :, cols].astype(jnp.float32) + attended[
                j * some : (j + 1) * some
            ].astype(jnp.float32)
            hidden_ref[:, cols] = state
            squares = squares + state * state
    meansq = jnp.sum(squares, axis=1, keepdims=True) / float(heads * HEAD_SIZE)
    inverse = lax.rsqrt(meansq + 1e-06)
    for h in range(heads):
        cols = slice(h * HEAD_SIZE, (h + 1) * HEAD_SIZE)
        normed_ref[:, cols] = (hidden_ref[:, cols] * inverse * gain_ref[:, cols]).astype(
            jnp.bfloat16
        )


def attend(half, staged, messages):
    some, features = staged[1].shape[1:]
    rows = messages[0].shape[0] - EXTRA
    count = len(messages)
    kv_heads = messages[0].shape[1] // (2 * HEAD_SIZE)
    vmem = pl.BlockSpec(memory_space=pltpu.VMEM)
    span = count * rows
    return pl.pallas_call(
        functools.partial(attend_kernel, count, half),
        out_shape=(
            jax.ShapeDtypeStruct((some, features), jnp.float32),
            jax.ShapeDtypeStruct((some, features), jnp.bfloat16),
        ),
        in_specs=[vmem] * (3 + count),
        out_specs=(vmem, vmem),
        scratch_shapes=[
            pltpu.VMEM((kv_heads, span, 2 * HEAD_SIZE), jnp.bfloat16),
            pltpu.VMEM((kv_heads, span, 2 * HEAD_SIZE), jnp.bfloat16),
        ],
        compiler_params=pltpu.CompilerParams(vmem_limit_bytes=28 * 1024 * 1024),
        cost_estimate=pl.CostEstimate(
            flops=4 * rows * span * features, bytes_accessed=4 * 1024 * 1024, transcendentals=0
        ),
        name="attend",
    )(*staged, *messages)


def expert_kernel(places, count, *refs):
    pieces = len(places)
    tokens = refs[:pieces]
    messages = refs[pieces : pieces + count]
    weights = refs[pieces + count : pieces + count + 3 * CORES]
    outs = refs[pieces + count + 3 * CORES :]
    rows, features = tokens[0].shape
    whole = messages[0].shape[0] - EXTRA
    top = EXTRA // 2
    me = lax.axis_index("ctx")
    normed = jnp.concatenate([ref[...] for ref in tokens], axis=0)
    shares, acts = [], []
    for e in range(CORES):
        gate_ref, up_ref = weights[3 * e], weights[3 * e + 1]
        gate = jnp.dot(normed, gate_ref[0], preferred_element_type=jnp.float32)
        upper = jnp.dot(normed, up_ref[0], preferred_element_type=jnp.float32)
        acts.append((gate / (1.0 + jnp.exp(-gate)) * upper).astype(jnp.bfloat16))
        name = jnp.bitwise_xor(me, e).astype(jnp.float32)
        columns = []
        for ref in messages:
            extra = ref[whole : whole + EXTRA, 0 : 2 * whole].astype(jnp.float32)
            value = extra[top : 2 * top, 0:whole] + extra[0:top, whole : 2 * whole]
            hit = jnp.where(extra[0:top, 0:whole] == name, value, 0.0)
            line = jnp.sum(hit, axis=0, keepdims=True)
            columns.append(jnp.broadcast_to(line, (whole, whole)).T)
        shares.append([columns[m][half * rows : (half + 1) * rows] for m, half in places])
    step = 512
    for at in range(0, features, step):
        parts = [
            jnp.dot(acts[e], weights[3 * e + 2][0, :, at : at + step], preferred_element_type=jnp.float32)
            .astype(jnp.bfloat16)
            .astype(jnp.float32)
            for e in range(CORES)
        ]
        for b in range(pieces):
            for c in range(0, step, whole):
                mixed = sum(
                    shares[e][b] * parts[e][b * rows : (b + 1) * rows, c : c + whole]
                    for e in range(CORES)
                )
                outs[b][:, at + c : at + c + whole] = mixed.astype(jnp.bfloat16)


def run_experts(pieces, messages, weights):
    tokens = [piece[0] for piece in pieces]
    rows, features = tokens[0].shape
    hidden = weights[0].shape[2]
    vmem = pl.BlockSpec(memory_space=pltpu.VMEM)
    return pl.pallas_call(
        functools.partial(expert_kernel, [piece[1:] for piece in pieces], len(messages)),
        out_shape=[jax.ShapeDtypeStruct((rows, features), jnp.bfloat16)] * len(pieces),
        in_specs=[vmem] * (len(pieces) + len(messages) + len(weights)),
        out_specs=[vmem] * len(pieces),
        compiler_params=pltpu.CompilerParams(vmem_limit_bytes=24 * 1024 * 1024),
        cost_estimate=pl.CostEstimate(
            flops=12 * len(pieces) * rows * features * hidden,
            bytes_accessed=12 * features * hidden,
            transcendentals=0,
        ),
        name="experts",
    )(*tokens, *messages, *weights)


def add_parts(*parts):
    total = parts[0].astype(jnp.float32)
    for part in parts[1:]:
        total = total + part.astype(jnp.float32)
    return total.astype(jnp.bfloat16)


def ring_device(
    queries,
    rotated_keys,
    value_matrix,
    stretch_pos,
    residual,
    norm_gain,
    routes,
    combine,
    gate_weight,
    up_weight,
    down_weight,
):
    chips = lax.axis_size("ctx") // CORES
    far = chips // 2
    onward, back, swap = ring_pairs(chips)

    def send(array, pairs):
        return lax.ppermute(array, "ctx", pairs)

    message = pack_message(stretch_pos, rotated_keys, value_matrix, routes, combine)

    left, right = {0: message}, {0: message}
    for hop in range(1, far + 1):
        if hop == 3:
            inputs, unused = lax.optimization_barrier(
                ((queries, residual, norm_gain), (left[1], right[1]))
            )
            staged = stage(*inputs)
            left[2], staged = lax.optimization_barrier((left[2], staged))
        left[hop] = send(left[hop - 1], onward)
        if hop < far:
            right[hop] = send(right[hop - 1], back)
    plane = [message] + [left[h] for h in range(1, far + 1)] + [right[h] for h in range(1, far)]
    everything = plane + [send(m, swap) for m in plane]
    everything, to_swap = lax.optimization_barrier(
        (everything, (gate_weight, up_weight, down_weight))
    )
    weights = (gate_weight, up_weight, down_weight) + tuple(send(w, swap) for w in to_swap)
    hidden_upper, upper = attend(0, staged, everything)
    everything, upper = lax.optimization_barrier((everything, upper))
    hidden_lower, lower = attend(1, staged, everything)

    from_left, from_right = {(0, 0): upper, (0, 1): lower}, {(0, 0): upper, (0, 1): lower}
    outs = {}

    def experts_of(hop, after):
        if hop == 0:
            pieces, used = [(upper, 0, 0), (lower, 0, 1)], [message]
        elif hop == far:
            pieces, used = [(from_left[far, 0], 0, 0), (from_right[far, 1], 0, 1)], [left[far]]
        else:
            pieces = [(from_left[hop, 0], 0, 0), (from_left[hop, 1], 0, 1)]
            pieces += [(from_right[hop, 0], 1, 0), (from_right[hop, 1], 1, 1)]
            used = [left[hop], right[hop]]
        used, after = lax.optimization_barrier((used, after))
        return run_experts(pieces, used, weights), after

    for hop in range(1, far + 1):
        onto, backto = from_left[hop - 1, 0], from_right[hop - 1, 0]
        if hop > 2:
            outs[hop - 2], outs[hop - 3] = experts_of(hop - 2, outs[hop - 3])
            onto, backto, outs[hop - 2] = lax.optimization_barrier((onto, backto, outs[hop - 2]))
        from_left[hop, 0] = send(onto, onward)
        if hop < far:
            from_right[hop, 0] = send(backto, back)
        onto, backto = from_left[hop - 1, 1], from_right[hop - 1, 1]
        if hop == 2:
            outs[0], unused = experts_of(0, from_left[1, 0])
            onto, backto, outs[0] = lax.optimization_barrier((onto, backto, outs[0]))
        if hop < far:
            from_left[hop, 1] = send(onto, onward)
        from_right[hop, 1] = send(backto, back)
    outs[far - 1], outs[far - 2] = experts_of(far - 1, outs[far - 2])
    outs[far], outs[far - 1] = experts_of(far, outs[far - 1])
    out_left = {hop: outs[hop][:2] for hop in range(1, far)}
    out_right = {hop: outs[hop][2:] for hop in range(1, far)}
    far_upper, far_lower = outs[far]
    own_out = outs[0]

    sums_on = {1: send(out_right[far - 1][1], onward)}
    sums_back = {0: send(out_left[far - 1][0], back)}
    sums_on[0] = send(far_upper, onward)
    sums_back[1] = send(far_lower, back)
    for hop in range(far - 1, 0, -1):
        if hop < far - 1:
            sums_on[1] = send(add_parts(sums_on[1], out_right[hop][1]), onward)
            sums_back[0] = send(add_parts(sums_back[0], out_left[hop][0]), back)
        sums_on[0] = send(add_parts(sums_on[0], out_right[hop][0]), onward)
        sums_back[1] = send(add_parts(sums_back[1], out_left[hop][1]), back)
    hidden_state = (hidden_upper, hidden_lower)
    return jnp.concatenate(
        [
            (
                hidden_state[half]
                + own_out[half].astype(jnp.float32)
                + sums_on[half].astype(jnp.float32)
                + sums_back[half].astype(jnp.float32)
            ).astype(jnp.bfloat16)
            for half in range(2)
        ],
        axis=0,
    )


def exchange_device(
    queries,
    rotated_keys,
    value_matrix,
    stretch_pos,
    residual,
    norm_gain,
    routes,
    combine,
    gate_weight,
    up_weight,
    down_weight,
):
    tok_rows = queries.shape[0]
    kv_heads = rotated_keys.shape[1] // HEAD_SIZE
    head_group = queries.shape[1] // rotated_keys.shape[1]
    ctx_count = lax.axis_size("ctx")
    positions = stretch_pos[0] * tok_rows + jnp.arange(tok_rows, dtype=jnp.int32)
    latest = jnp.max(positions)
    query_heads = queries.reshape(tok_rows, kv_heads, head_group, HEAD_SIZE)
    scale_factor = 1.0 / math.sqrt(HEAD_SIZE)

    def update(state, key_block, value_block, key_pos):
        best, total, accum = state
        scores = (
            jnp.einsum(
                "tagd,sad->agts",
                query_heads,
                key_block.reshape(-1, kv_heads, HEAD_SIZE),
                preferred_element_type=jnp.float32,
            )
            * scale_factor
        )
        scores = jnp.where(
            key_pos[None, None, None, :] <= positions[None, None, :, None], scores, jnp.float32(NEG)
        )
        fresh = jnp.maximum(best, jnp.max(scores, axis=-1))
        shrink = jnp.exp(best - fresh)
        expo = jnp.exp(scores - fresh[..., None])
        total = total * shrink + jnp.sum(expo, axis=-1)
        weighted = jnp.einsum(
            "agts,sad->agtd",
            expo.astype(jnp.bfloat16),
            value_block.reshape(-1, kv_heads, HEAD_SIZE),
            preferred_element_type=jnp.float32,
        )
        accum = accum * shrink[..., None] + weighted
        return (fresh, total, accum)

    start_state = (
        jnp.full((kv_heads, head_group, tok_rows), NEG, jnp.float32),
        jnp.zeros((kv_heads, head_group, tok_rows), jnp.float32),
        jnp.zeros((kv_heads, head_group, tok_rows, HEAD_SIZE), jnp.float32),
    )
    key_part = lax.all_gather(rotated_keys, "ctx", axis=0, tiled=True)
    value_part = lax.all_gather(value_matrix, "ctx", axis=0, tiled=True)
    pos_part = lax.all_gather(positions, "ctx", axis=0, tiled=True)
    span = key_part.shape[0]
    width = 512
    blocks = span // width
    stacked = (
        key_part.reshape(blocks, width, -1),
        value_part.reshape(blocks, width, -1),
        pos_part.reshape(blocks, width),
    )

    def advance(inner, item):
        key_block, value_block, key_pos = item
        result = lax.cond(
            jnp.min(key_pos) > latest,
            lambda kept: kept,
            lambda kept: update(kept, key_block, value_block, key_pos),
            inner,
        )
        return (result, None)

    final, unused = lax.scan(advance, start_state, stacked)
    best, total, accum = final
    attended = (
        jnp.transpose(accum / total[..., None], (2, 0, 1, 3))
        .reshape(tok_rows, -1)
        .astype(jnp.bfloat16)
    )
    hidden_state = residual.astype(jnp.float32) + attended.astype(jnp.float32)
    meansq = jnp.mean(hidden_state * hidden_state, axis=-1, keepdims=True)
    normed = (hidden_state * lax.rsqrt(meansq + 1e-06) * norm_gain).astype(jnp.bfloat16)
    local_experts = gate_weight.shape[0]
    total_experts = local_experts * ctx_count
    top_count = routes.shape[1]
    capacity = min(
        tok_rows,
        tok_rows * top_count // total_experts + max(1, tok_rows * top_count // (8 * total_experts)),
    )
    flat_routes = routes.reshape(-1)
    onehot = (flat_routes[:, None] == jnp.arange(total_experts, dtype=jnp.int32)[None, :]).astype(
        jnp.int32
    )
    earlier = jnp.cumsum(onehot, axis=0) - onehot
    ranking = jnp.sum(earlier * onehot, axis=1)
    slot_ids = flat_routes * capacity + ranking
    selector = jnp.any(
        slot_ids.reshape(tok_rows, top_count)[:, :, None]
        == jnp.arange(total_experts * capacity, dtype=jnp.int32)[None, None, :],
        axis=1,
    ).astype(jnp.bfloat16)
    outgoing = jnp.einsum("ts,td->sd", selector, normed, preferred_element_type=jnp.float32).astype(
        jnp.bfloat16
    )
    outgoing = outgoing.reshape(ctx_count, local_experts, capacity, D)
    incoming = lax.all_to_all(outgoing, "ctx", split_axis=0, concat_axis=0, tiled=True)
    gate = jnp.einsum("secd,edh->sech", incoming, gate_weight, preferred_element_type=jnp.float32)
    upper = jnp.einsum("secd,edh->sech", incoming, up_weight, preferred_element_type=jnp.float32)
    act = (jax.nn.silu(gate) * upper).astype(jnp.bfloat16)
    returned = lax.all_to_all(
        jnp.einsum("sech,ehd->secd", act, down_weight, preferred_element_type=jnp.float32).astype(
            jnp.bfloat16
        ),
        "ctx",
        split_axis=0,
        concat_axis=0,
        tiled=True,
    )
    flat_back = returned.reshape(total_experts * capacity, D)
    picked = jnp.take(flat_back, slot_ids, axis=0).reshape(tok_rows, top_count, D)
    mixture = jnp.sum(combine[:, :, None] * picked.astype(jnp.float32), axis=1)
    return (hidden_state + mixture).astype(jnp.bfloat16)


def solution(mesh):
    placed = (
        P(("groups", "ctx"), None),
        P(("groups", "ctx"), None),
        P(("groups", "ctx"), None),
        P(("groups", "ctx")),
        P(("groups", "ctx"), None),
        P(),
        P(("groups", "ctx"), None),
        P(("groups", "ctx"), None),
        P("ctx", None, None),
        P("ctx", None, None),
        P("ctx", None, None),
    )
    ctx_count = mesh.shape["ctx"]

    def on_device(*arguments):
        routes, gate_weight = arguments[6], arguments[8]
        dense = 4 * routes.shape[1] >= gate_weight.shape[0] * ctx_count
        ringed = gate_weight.shape[0] == 1 and ctx_count % (2 * CORES) == 0
        ringed = ringed and ctx_count >= 6 * CORES and 2 * routes.shape[1] == EXTRA
        return (ring_device if dense and ringed else exchange_device)(*arguments)

    return jax.shard_map(
        on_device, mesh=mesh, in_specs=placed, out_specs=P(("groups", "ctx"), None), check_vma=False
    )
```

```python
import functools
import math

import jax
import jax.numpy as jnp
from jax import lax
from jax.experimental import pallas as pl
from jax.experimental.pallas import tpu as pltpu
from jax.sharding import PartitionSpec as P

D = 2048
HEAD_SIZE = 128
CORES = 2
EXTRA = 16
QUERY_SCALE = 0.125


NEG = -1e30


def ring_pairs(chips):
    order = list(range(0, chips, 2)) + list(range(chips - 1, 0, -2))
    onward = [
        (order[i] * CORES + core, order[(i + 1) % chips] * CORES + core)
        for i in range(chips)
        for core in range(CORES)
    ]
    back = [(b, a) for a, b in onward]
    swap = [(i, i ^ 1) for i in range(chips * CORES)]
    return onward, back, swap


def pack_kernel(pos_ref, key_ref, value_ref, routes_ref, combine_ref, out_ref):
    rows, width = key_ref.shape
    top = routes_ref.shape[0]
    out_ref[0:rows, 0:width] = key_ref[...]
    out_ref[0:rows, width : 2 * width] = value_ref[...]
    weight = combine_ref[...]
    high = weight.astype(jnp.bfloat16).astype(jnp.float32)
    low = weight - high
    names = routes_ref[...].astype(jnp.float32)
    place = jnp.full((EXTRA, 2 * width - 2 * rows), pos_ref[0].astype(jnp.float32), jnp.float32)
    tail = slice(rows, rows + EXTRA)
    out_ref[tail, 0:rows] = jnp.concatenate([names, high], axis=0).astype(jnp.bfloat16)
    out_ref[tail, rows : 2 * rows] = jnp.concatenate([low, jnp.zeros_like(low)], axis=0).astype(
        jnp.bfloat16
    )
    out_ref[tail, 2 * rows : 2 * width] = place.astype(jnp.bfloat16)


def pack_message(stretch_pos, keys, values, routes, combine):
    rows, width = keys.shape
    vmem = pl.BlockSpec(memory_space=pltpu.VMEM)
    return pl.pallas_call(
        pack_kernel,
        out_shape=jax.ShapeDtypeStruct((rows + EXTRA, 2 * width), jnp.bfloat16),
        in_specs=[pl.BlockSpec(memory_space=pltpu.SMEM), vmem, vmem, vmem, vmem],
        out_specs=vmem,
        name="pack_message",
    )(stretch_pos, keys, values, routes.T, combine.T)


def attend_kernel(count, half, *refs):
    query_ref, residual_ref, gain_ref = refs[:3]
    messages = refs[3 : 3 + count]
    hidden_ref, normed_ref, key_ext, value_ext = refs[3 + count :]
    features = query_ref.shape[1]
    some = query_ref.shape[0] // 2
    mine = slice(half * some, (half + 1) * some)
    rows = messages[0].shape[0] - EXTRA
    kv_heads = key_ext.shape[0]
    heads = features // HEAD_SIZE
    group = heads // kv_heads
    span = count * rows
    width = kv_heads * HEAD_SIZE
    sub = lax.broadcasted_iota(jnp.int32, (rows, rows), 0)
    lane = lax.broadcasted_iota(jnp.int32, (rows, rows), 1)
    ahead = (sub - lane).astype(jnp.float32)
    own_pos = messages[0][rows : rows + EXTRA, 256 : 256 + rows][0:1].astype(jnp.float32)
    ones = jnp.ones((rows, HEAD_SIZE), jnp.bfloat16)
    for block in range(count):
        ref = messages[block]
        at = slice(block * rows, (block + 1) * rows)
        pos = ref[rows : rows + EXTRA, 256 : 256 + rows][0:1].astype(jnp.float32)
        later = (pos - own_pos) * float(rows) + ahead
        bias = jnp.where(later > 0.0, NEG, 0.0).astype(jnp.bfloat16)
        for a in range(kv_heads):
            key_ext[a, at, 0:HEAD_SIZE] = ref[0:rows, a * HEAD_SIZE : (a + 1) * HEAD_SIZE]
            key_ext[a, at, HEAD_SIZE : HEAD_SIZE + rows] = bias
            value_ext[a, at, 0:HEAD_SIZE] = ref[
                0:rows, width + a * HEAD_SIZE : width + (a + 1) * HEAD_SIZE
            ]
            value_ext[a, at, HEAD_SIZE : 2 * HEAD_SIZE] = ones
    eye = jnp.where(sub == lane, 1.0, 0.0).astype(jnp.bfloat16)[mine]
    rate = math.log2(math.e) / math.sqrt(HEAD_SIZE) / QUERY_SCALE
    step = min(512, span)
    pair = 4
    squares = jnp.zeros((some, HEAD_SIZE), jnp.float32)
    for first in range(0, heads, pair):
        a = first // group
        stacked = jnp.concatenate(
            [
                jnp.concatenate([query_ref[mine, h * HEAD_SIZE : (h + 1) * HEAD_SIZE], eye], axis=1)
                for h in range(first, first + pair)
            ],
            axis=0,
        )
        scores = [
            lax.dot_general(
                stacked,
                key_ext[a, at : at + step, :],
                (((1,), (1,)), ((), ())),
                preferred_element_type=jnp.float32,
            )
            for at in range(0, span, step)
        ]
        best = functools.reduce(jnp.maximum, scores)
        best = jnp.max(best, axis=1, keepdims=True)
        total = None
        for i, part in enumerate(scores):
            probs = jnp.exp2((part - best) * rate).astype(jnp.bfloat16)
            term = jnp.dot(
                probs,
                value_ext[a, i * step : (i + 1) * step, :],
                preferred_element_type=jnp.float32,
            )
            total = term if total is None else total + term
        attended = (total[:, 0:HEAD_SIZE] / total[:, HEAD_SIZE:]).astype(jnp.bfloat16)
        for j in range(pair):
            cols = slice((first + j) * HEAD_SIZE, (first + j + 1) * HEAD_SIZE)
            state = residual_ref[mine, cols] + attended[
                j * some : (j + 1) * some
            ].astype(jnp.float32)
            hidden_ref[:, cols] = state
            squares = squares + state * state
    meansq = jnp.sum(squares, axis=1, keepdims=True) / float(heads * HEAD_SIZE)
    inverse = lax.rsqrt(meansq + 1e-06)
    for h in range(heads):
        cols = slice(h * HEAD_SIZE, (h + 1) * HEAD_SIZE)
        normed_ref[:, cols] = (hidden_ref[:, cols] * inverse * gain_ref[0:1, cols]).astype(
            jnp.bfloat16
        )


def attend(half, staged, messages):
    rows, features = staged[0].shape
    some = rows // 2
    count = len(messages)
    kv_heads = messages[0].shape[1] // (2 * HEAD_SIZE)
    vmem = pl.BlockSpec(memory_space=pltpu.VMEM)
    span = count * rows
    return pl.pallas_call(
        functools.partial(attend_kernel, count, half),
        out_shape=(
            jax.ShapeDtypeStruct((some, features), jnp.float32),
            jax.ShapeDtypeStruct((some, features), jnp.bfloat16),
        ),
        in_specs=[vmem] * (3 + count),
        out_specs=(vmem, vmem),
        scratch_shapes=[
            pltpu.VMEM((kv_heads, span, 2 * HEAD_SIZE), jnp.bfloat16),
            pltpu.VMEM((kv_heads, span, 2 * HEAD_SIZE), jnp.bfloat16),
        ],
        compiler_params=pltpu.CompilerParams(vmem_limit_bytes=28 * 1024 * 1024),
        cost_estimate=pl.CostEstimate(
            flops=4 * rows * span * features, bytes_accessed=4 * 1024 * 1024, transcendentals=0
        ),
        name="attend",
    )(*staged, *messages)


def expert_kernel(places, count, *refs):
    pieces = len(places)
    tokens = refs[:pieces]
    messages = refs[pieces : pieces + count]
    weights = refs[pieces + count : pieces + count + 3 * CORES]
    outs = refs[pieces + count + 3 * CORES :]
    rows, features = tokens[0].shape
    whole = messages[0].shape[0] - EXTRA
    top = EXTRA // 2
    me = lax.axis_index("ctx")
    normed = jnp.concatenate([ref[...] for ref in tokens], axis=0)
    shares, acts = [], []
    for e in range(CORES):
        gate_ref, up_ref = weights[3 * e], weights[3 * e + 1]
        gate = jnp.dot(normed, gate_ref[0], preferred_element_type=jnp.float32)
        upper = jnp.dot(normed, up_ref[0], preferred_element_type=jnp.float32)
        acts.append((gate / (1.0 + jnp.exp(-gate)) * upper).astype(jnp.bfloat16))
        name = jnp.bitwise_xor(me, e).astype(jnp.float32)
        columns = []
        for ref in messages:
            extra = ref[whole : whole + EXTRA, 0 : 2 * whole].astype(jnp.float32)
            value = extra[top : 2 * top, 0:whole] + extra[0:top, whole : 2 * whole]
            hit = jnp.where(extra[0:top, 0:whole] == name, value, 0.0)
            line = jnp.sum(hit, axis=0, keepdims=True)
            columns.append(jnp.broadcast_to(line, (whole, whole)).T)
        shares.append([columns[m][half * rows : (half + 1) * rows] for m, half in places])
    step = 512
    for at in range(0, features, step):
        parts = [
            jnp.dot(acts[e], weights[3 * e + 2][0, :, at : at + step], preferred_element_type=jnp.float32)
            .astype(jnp.bfloat16)
            .astype(jnp.float32)
            for e in range(CORES)
        ]
        for b in range(pieces):
            for c in range(0, step, whole):
                mixed = sum(
                    shares[e][b] * parts[e][b * rows : (b + 1) * rows, c : c + whole]
                    for e in range(CORES)
                )
                outs[b][:, at + c : at + c + whole] = mixed.astype(jnp.bfloat16)


def run_experts(pieces, messages, weights):
    tokens = [piece[0] for piece in pieces]
    rows, features = tokens[0].shape
    hidden = weights[0].shape[2]
    vmem = pl.BlockSpec(memory_space=pltpu.VMEM)
    return pl.pallas_call(
        functools.partial(expert_kernel, [piece[1:] for piece in pieces], len(messages)),
        out_shape=[jax.ShapeDtypeStruct((rows, features), jnp.bfloat16)] * len(pieces),
        in_specs=[vmem] * (len(pieces) + len(messages) + len(weights)),
        out_specs=[vmem] * len(pieces),
        compiler_params=pltpu.CompilerParams(vmem_limit_bytes=24 * 1024 * 1024),
        cost_estimate=pl.CostEstimate(
            flops=12 * len(pieces) * rows * features * hidden,
            bytes_accessed=12 * features * hidden,
            transcendentals=0,
        ),
        name="experts",
    )(*tokens, *messages, *weights)


def add_parts(*parts):
    total = parts[0].astype(jnp.float32)
    for part in parts[1:]:
        total = total + part.astype(jnp.float32)
    return total.astype(jnp.bfloat16)


def ring_device(
    queries,
    rotated_keys,
    value_matrix,
    stretch_pos,
    residual,
    norm_gain,
    routes,
    combine,
    gate_weight,
    up_weight,
    down_weight,
):
    chips = lax.axis_size("ctx") // CORES
    far = chips // 2
    onward, back, swap = ring_pairs(chips)

    def send(array, pairs):
        return lax.ppermute(array, "ctx", pairs)

    message = pack_message(stretch_pos, rotated_keys, value_matrix, routes, combine)

    tie = lax.optimization_barrier
    left, right = {0: message}, {0: message}
    gate_from, unused = tie((gate_weight, message))
    twin_gate = send(gate_from, swap)
    for hop in range(1, far + 1):
        if hop == 3:
            inputs, unused = tie(((queries, residual, norm_gain), (left[1], right[1])))
            staged = (
                inputs[0] * jnp.bfloat16(QUERY_SCALE),
                inputs[1].astype(jnp.float32),
                jnp.broadcast_to(inputs[2][None, :], (8, inputs[2].shape[0])),
            )
            left[2], staged, twin_gate = tie((left[2], staged, twin_gate))
            up_from, unused = tie((up_weight, left[2]))
            twin_up = send(up_from, swap)
        left[hop] = send(left[hop - 1], onward)
        if hop < far:
            right[hop] = send(right[hop - 1], back)
    plane = [message] + [left[h] for h in range(1, far + 1)] + [right[h] for h in range(1, far)]
    everything = plane + [send(m, swap) for m in plane]
    everything, down_from, twin_up = tie((everything, down_weight, twin_up))
    weights = (gate_weight, up_weight, down_weight, twin_gate, twin_up, send(down_from, swap))
    hidden_upper, upper = attend(0, staged, everything)
    everything, upper = tie((everything, upper))
    hidden_lower, lower = attend(1, staged, everything)

    from_left, from_right = {(0, 0): upper, (0, 1): lower}, {(0, 0): upper, (0, 1): lower}
    outs = {}

    def experts_on(tokens, used, after):
        used, after = tie((used, after))
        return run_experts(tokens, used, weights), after

    def experts_of(hop, half, after):
        tokens = [(from_left[hop, half], 0, half), (from_right[hop, half], 1, half)]
        return experts_on(tokens, [left[hop], right[hop]], after)

    last = (upper, lower)
    for hop in range(1, far + 1):
        for half in range(2):
            onto, backto = from_left[hop - 1, half], from_right[hop - 1, half]
            if hop > 1:
                before = (hop - 1, 1 - half) if half == 1 else (hop - 2, 1)
                if before[0] > 0:
                    outs[before], unused = experts_of(*before, last)
                    last = outs[before]
                    onto, backto, last = tie((onto, backto, last))
                    outs[before] = last
            if hop < far or half == 0:
                from_left[hop, half] = send(onto, onward)
            if hop < far or half == 1:
                from_right[hop, half] = send(backto, back)
    outs[far - 1, 1], unused = experts_of(far - 1, 1, last)
    outs[far - 1, 0], outs[far - 1, 1] = tie((outs[far - 1, 0], outs[far - 1, 1]))
    out_left = {key: pair[0] for key, pair in outs.items()}
    out_right = {key: pair[1] for key, pair in outs.items()}

    sums_on = {1: send(out_right[far - 1, 1], onward)}
    sums_back = {0: send(out_left[far - 1, 0], back)}
    (far_upper, far_lower), unused = experts_on(
        [(from_left[far, 0], 0, 0), (from_right[far, 1], 0, 1)], [left[far]], outs[far - 1, 1]
    )
    sums_on[0] = send(far_upper, onward)
    sums_back[1] = send(far_lower, back)
    own_out, unused = experts_on([(upper, 0, 0), (lower, 0, 1)], [message], (far_upper, far_lower))
    for hop in range(far - 1, 0, -1):
        if hop < far - 1:
            sums_on[1] = send(add_parts(sums_on[1], out_right[hop, 1]), onward)
            sums_back[0] = send(add_parts(sums_back[0], out_left[hop, 0]), back)
        onto, backto = sums_on[0], sums_back[1]
        if hop == far - 1:
            onto, backto, own_out = tie((onto, backto, own_out))
        sums_on[0] = send(add_parts(onto, out_right[hop, 0]), onward)
        sums_back[1] = send(add_parts(backto, out_left[hop, 1]), back)
    hidden_state = (hidden_upper, hidden_lower)
    return jnp.concatenate(
        [
            (
                hidden_state[half]
                + own_out[half].astype(jnp.float32)
                + sums_on[half].astype(jnp.float32)
                + sums_back[half].astype(jnp.float32)
            ).astype(jnp.bfloat16)
            for half in range(2)
        ],
        axis=0,
    )


def exchange_device(
    queries,
    rotated_keys,
    value_matrix,
    stretch_pos,
    residual,
    norm_gain,
    routes,
    combine,
    gate_weight,
    up_weight,
    down_weight,
):
    tok_rows = queries.shape[0]
    kv_heads = rotated_keys.shape[1] // HEAD_SIZE
    head_group = queries.shape[1] // rotated_keys.shape[1]
    ctx_count = lax.axis_size("ctx")
    positions = stretch_pos[0] * tok_rows + jnp.arange(tok_rows, dtype=jnp.int32)
    latest = jnp.max(positions)
    query_heads = queries.reshape(tok_rows, kv_heads, head_group, HEAD_SIZE)
    scale_factor = 1.0 / math.sqrt(HEAD_SIZE)

    def update(state, key_block, value_block, key_pos):
        best, total, accum = state
        scores = (
            jnp.einsum(
                "tagd,sad->agts",
                query_heads,
                key_block.reshape(-1, kv_heads, HEAD_SIZE),
                preferred_element_type=jnp.float32,
            )
            * scale_factor
        )
        scores = jnp.where(
            key_pos[None, None, None, :] <= positions[None, None, :, None], scores, jnp.float32(NEG)
        )
        fresh = jnp.maximum(best, jnp.max(scores, axis=-1))
        shrink = jnp.exp(best - fresh)
        expo = jnp.exp(scores - fresh[..., None])
        total = total * shrink + jnp.sum(expo, axis=-1)
        weighted = jnp.einsum(
            "agts,sad->agtd",
            expo.astype(jnp.bfloat16),
            value_block.reshape(-1, kv_heads, HEAD_SIZE),
            preferred_element_type=jnp.float32,
        )
        accum = accum * shrink[..., None] + weighted
        return (fresh, total, accum)

    start_state = (
        jnp.full((kv_heads, head_group, tok_rows), NEG, jnp.float32),
        jnp.zeros((kv_heads, head_group, tok_rows), jnp.float32),
        jnp.zeros((kv_heads, head_group, tok_rows, HEAD_SIZE), jnp.float32),
    )
    key_part = lax.all_gather(rotated_keys, "ctx", axis=0, tiled=True)
    value_part = lax.all_gather(value_matrix, "ctx", axis=0, tiled=True)
    pos_part = lax.all_gather(positions, "ctx", axis=0, tiled=True)
    span = key_part.shape[0]
    width = 512
    blocks = span // width
    stacked = (
        key_part.reshape(blocks, width, -1),
        value_part.reshape(blocks, width, -1),
        pos_part.reshape(blocks, width),
    )

    def advance(inner, item):
        key_block, value_block, key_pos = item
        result = lax.cond(
            jnp.min(key_pos) > latest,
            lambda kept: kept,
            lambda kept: update(kept, key_block, value_block, key_pos),
            inner,
        )
        return (result, None)

    final, unused = lax.scan(advance, start_state, stacked)
    best, total, accum = final
    attended = (
        jnp.transpose(accum / total[..., None], (2, 0, 1, 3))
        .reshape(tok_rows, -1)
        .astype(jnp.bfloat16)
    )
    hidden_state = residual.astype(jnp.float32) + attended.astype(jnp.float32)
    meansq = jnp.mean(hidden_state * hidden_state, axis=-1, keepdims=True)
    normed = (hidden_state * lax.rsqrt(meansq + 1e-06) * norm_gain).astype(jnp.bfloat16)
    local_experts = gate_weight.shape[0]
    total_experts = local_experts * ctx_count
    top_count = routes.shape[1]
    capacity = min(
        tok_rows,
        tok_rows * top_count // total_experts + max(1, tok_rows * top_count // (8 * total_experts)),
    )
    flat_routes = routes.reshape(-1)
    onehot = (flat_routes[:, None] == jnp.arange(total_experts, dtype=jnp.int32)[None, :]).astype(
        jnp.int32
    )
    earlier = jnp.cumsum(onehot, axis=0) - onehot
    ranking = jnp.sum(earlier * onehot, axis=1)
    slot_ids = flat_routes * capacity + ranking
    selector = jnp.any(
        slot_ids.reshape(tok_rows, top_count)[:, :, None]
        == jnp.arange(total_experts * capacity, dtype=jnp.int32)[None, None, :],
        axis=1,
    ).astype(jnp.bfloat16)
    outgoing = jnp.einsum("ts,td->sd", selector, normed, preferred_element_type=jnp.float32).astype(
        jnp.bfloat16
    )
    outgoing = outgoing.reshape(ctx_count, local_experts, capacity, D)
    incoming = lax.all_to_all(outgoing, "ctx", split_axis=0, concat_axis=0, tiled=True)
    gate = jnp.einsum("secd,edh->sech", incoming, gate_weight, preferred_element_type=jnp.float32)
    upper = jnp.einsum("secd,edh->sech", incoming, up_weight, preferred_element_type=jnp.float32)
    act = (jax.nn.silu(gate) * upper).astype(jnp.bfloat16)
    returned = lax.all_to_all(
        jnp.einsum("sech,ehd->secd", act, down_weight, preferred_element_type=jnp.float32).astype(
            jnp.bfloat16
        ),
        "ctx",
        split_axis=0,
        concat_axis=0,
        tiled=True,
    )
    flat_back = returned.reshape(total_experts * capacity, D)
    picked = jnp.take(flat_back, slot_ids, axis=0).reshape(tok_rows, top_count, D)
    mixture = jnp.sum(combine[:, :, None] * picked.astype(jnp.float32), axis=1)
    return (hidden_state + mixture).astype(jnp.bfloat16)


def solution(mesh):
    placed = (
        P(("groups", "ctx"), None),
        P(("groups", "ctx"), None),
        P(("groups", "ctx"), None),
        P(("groups", "ctx")),
        P(("groups", "ctx"), None),
        P(),
        P(("groups", "ctx"), None),
        P(("groups", "ctx"), None),
        P("ctx", None, None),
        P("ctx", None, None),
        P("ctx", None, None),
    )
    ctx_count = mesh.shape["ctx"]

    def on_device(*arguments):
        routes, gate_weight = arguments[6], arguments[8]
        dense = 4 * routes.shape[1] >= gate_weight.shape[0] * ctx_count
        ringed = gate_weight.shape[0] == 1 and ctx_count % (2 * CORES) == 0
        ringed = ringed and ctx_count >= 6 * CORES and 2 * routes.shape[1] == EXTRA
        return (ring_device if dense and ringed else exchange_device)(*arguments)

    return jax.shard_map(
        on_device, mesh=mesh, in_specs=placed, out_specs=P(("groups", "ctx"), None), check_vma=False
    )
```

```python
import functools
import math

import jax
import jax.numpy as jnp
from jax import lax
from jax.experimental import pallas as pl
from jax.experimental.pallas import tpu as pltpu
from jax.sharding import PartitionSpec as P

D = 2048
HEAD_SIZE = 128
CORES = 2
EXTRA = 16
QUERY_SCALE = 0.125


NEG = -1e30


def ring_pairs(chips):
    order = list(range(0, chips, 2)) + list(range(chips - 1, 0, -2))
    onward = [
        (order[i] * CORES + core, order[(i + 1) % chips] * CORES + core)
        for i in range(chips)
        for core in range(CORES)
    ]
    back = [(b, a) for a, b in onward]
    swap = [(i, i ^ 1) for i in range(chips * CORES)]
    return onward, back, swap


def pack_kernel(pos_ref, key_ref, value_ref, routes_ref, combine_ref, out_ref):
    rows, width = key_ref.shape
    top = routes_ref.shape[0]
    out_ref[0:rows, 0:width] = key_ref[...]
    out_ref[0:rows, width : 2 * width] = value_ref[...]
    weight = combine_ref[...]
    high = weight.astype(jnp.bfloat16).astype(jnp.float32)
    low = weight - high
    names = routes_ref[...].astype(jnp.float32)
    place = jnp.full((EXTRA, 2 * width - 2 * rows), pos_ref[0].astype(jnp.float32), jnp.float32)
    tail = slice(rows, rows + EXTRA)
    out_ref[tail, 0:rows] = jnp.concatenate([names, high], axis=0).astype(jnp.bfloat16)
    out_ref[tail, rows : 2 * rows] = jnp.concatenate([low, jnp.zeros_like(low)], axis=0).astype(
        jnp.bfloat16
    )
    out_ref[tail, 2 * rows : 2 * width] = place.astype(jnp.bfloat16)


def pack_message(stretch_pos, keys, values, routes, combine):
    rows, width = keys.shape
    vmem = pl.BlockSpec(memory_space=pltpu.VMEM)
    return pl.pallas_call(
        pack_kernel,
        out_shape=jax.ShapeDtypeStruct((rows + EXTRA, 2 * width), jnp.bfloat16),
        in_specs=[pl.BlockSpec(memory_space=pltpu.SMEM), vmem, vmem, vmem, vmem],
        out_specs=vmem,
        name="pack_message",
    )(stretch_pos, keys, values, routes.T, combine.T)


def attend_kernel(count, half, *refs):
    query_ref, residual_ref, gain_ref = refs[:3]
    messages = refs[3 : 3 + count]
    hidden_ref, normed_ref, key_ext, value_ext = refs[3 + count :]
    features = query_ref.shape[1]
    some = query_ref.shape[0] // 2
    mine = slice(half * some, (half + 1) * some)
    rows = messages[0].shape[0] - EXTRA
    kv_heads = key_ext.shape[0]
    heads = features // HEAD_SIZE
    group = heads // kv_heads
    span = count * rows
    width = kv_heads * HEAD_SIZE
    sub = lax.broadcasted_iota(jnp.int32, (rows, rows), 0)
    lane = lax.broadcasted_iota(jnp.int32, (rows, rows), 1)
    ahead = (sub - lane).astype(jnp.float32)
    own_pos = messages[0][rows : rows + EXTRA, 256 : 256 + rows][0:1].astype(jnp.float32)
    ones = jnp.ones((rows, HEAD_SIZE), jnp.bfloat16)
    for block in range(count):
        ref = messages[block]
        at = slice(block * rows, (block + 1) * rows)
        pos = ref[rows : rows + EXTRA, 256 : 256 + rows][0:1].astype(jnp.float32)
        later = (pos - own_pos) * float(rows) + ahead
        bias = jnp.where(later > 0.0, NEG, 0.0).astype(jnp.bfloat16)
        for a in range(kv_heads):
            key_ext[a, at, 0:HEAD_SIZE] = ref[0:rows, a * HEAD_SIZE : (a + 1) * HEAD_SIZE]
            key_ext[a, at, HEAD_SIZE : HEAD_SIZE + rows] = bias
            value_ext[a, at, 0:HEAD_SIZE] = ref[
                0:rows, width + a * HEAD_SIZE : width + (a + 1) * HEAD_SIZE
            ]
            value_ext[a, at, HEAD_SIZE : 2 * HEAD_SIZE] = ones
    eye = jnp.where(sub == lane, 1.0, 0.0).astype(jnp.bfloat16)[mine]
    rate = math.log2(math.e) / math.sqrt(HEAD_SIZE) / QUERY_SCALE
    step = min(512, span)
    pair = 4
    squares = jnp.zeros((some, HEAD_SIZE), jnp.float32)
    for first in range(0, heads, pair):
        a = first // group
        stacked = jnp.concatenate(
            [
                jnp.concatenate([query_ref[mine, h * HEAD_SIZE : (h + 1) * HEAD_SIZE], eye], axis=1)
                for h in range(first, first + pair)
            ],
            axis=0,
        )
        scores = [
            lax.dot_general(
                stacked,
                key_ext[a, at : at + step, :],
                (((1,), (1,)), ((), ())),
                preferred_element_type=jnp.float32,
            )
            for at in range(0, span, step)
        ]
        best = functools.reduce(jnp.maximum, scores)
        best = jnp.max(best, axis=1, keepdims=True)
        total = None
        for i, part in enumerate(scores):
            probs = jnp.exp2((part - best) * rate).astype(jnp.bfloat16)
            term = jnp.dot(
                probs,
                value_ext[a, i * step : (i + 1) * step, :],
                preferred_element_type=jnp.float32,
            )
            total = term if total is None else total + term
        attended = (total[:, 0:HEAD_SIZE] / total[:, HEAD_SIZE:]).astype(jnp.bfloat16)
        for j in range(pair):
            cols = slice((first + j) * HEAD_SIZE, (first + j + 1) * HEAD_SIZE)
            state = residual_ref[mine, cols] + attended[
                j * some : (j + 1) * some
            ].astype(jnp.float32)
            hidden_ref[:, cols] = state
            squares = squares + state * state
    meansq = jnp.sum(squares, axis=1, keepdims=True) / float(heads * HEAD_SIZE)
    inverse = lax.rsqrt(meansq + 1e-06)
    for h in range(heads):
        cols = slice(h * HEAD_SIZE, (h + 1) * HEAD_SIZE)
        normed_ref[:, cols] = (hidden_ref[:, cols] * inverse * gain_ref[0:1, cols]).astype(
            jnp.bfloat16
        )


def attend(half, staged, messages):
    rows, features = staged[0].shape
    some = rows // 2
    count = len(messages)
    kv_heads = messages[0].shape[1] // (2 * HEAD_SIZE)
    vmem = pl.BlockSpec(memory_space=pltpu.VMEM)
    span = count * rows
    return pl.pallas_call(
        functools.partial(attend_kernel, count, half),
        out_shape=(
            jax.ShapeDtypeStruct((some, features), jnp.float32),
            jax.ShapeDtypeStruct((some, features), jnp.bfloat16),
        ),
        in_specs=[vmem] * (3 + count),
        out_specs=(vmem, vmem),
        scratch_shapes=[
            pltpu.VMEM((kv_heads, span, 2 * HEAD_SIZE), jnp.bfloat16),
            pltpu.VMEM((kv_heads, span, 2 * HEAD_SIZE), jnp.bfloat16),
        ],
        compiler_params=pltpu.CompilerParams(vmem_limit_bytes=28 * 1024 * 1024),
        cost_estimate=pl.CostEstimate(
            flops=4 * rows * span * features, bytes_accessed=4 * 1024 * 1024, transcendentals=0
        ),
        name="attend",
    )(*staged, *messages)


def expert_kernel(places, count, *refs):
    pieces = len(places)
    tokens = refs[:pieces]
    messages = refs[pieces : pieces + count]
    weights = refs[pieces + count : pieces + count + 3 * CORES]
    outs = refs[pieces + count + 3 * CORES :]
    rows, features = tokens[0].shape
    whole = messages[0].shape[0] - EXTRA
    top = EXTRA // 2
    me = lax.axis_index("ctx")
    normed = jnp.concatenate([ref[...] for ref in tokens], axis=0)
    shares, acts = [], []
    for e in range(CORES):
        gate_ref, up_ref = weights[3 * e], weights[3 * e + 1]
        gate = jnp.dot(normed, gate_ref[0], preferred_element_type=jnp.float32)
        upper = jnp.dot(normed, up_ref[0], preferred_element_type=jnp.float32)
        acts.append((gate / (1.0 + jnp.exp(-gate)) * upper).astype(jnp.bfloat16))
        name = jnp.bitwise_xor(me, e).astype(jnp.float32)
        columns = []
        for ref in messages:
            extra = ref[whole : whole + EXTRA, 0 : 2 * whole].astype(jnp.float32)
            value = extra[top : 2 * top, 0:whole] + extra[0:top, whole : 2 * whole]
            hit = jnp.where(extra[0:top, 0:whole] == name, value, 0.0)
            line = jnp.sum(hit, axis=0, keepdims=True)
            columns.append(jnp.broadcast_to(line, (whole, whole)).T)
        shares.append([columns[m][half * rows : (half + 1) * rows] for m, half in places])
    step = 512
    for at in range(0, features, step):
        parts = [
            jnp.dot(acts[e], weights[3 * e + 2][0, :, at : at + step], preferred_element_type=jnp.float32)
            .astype(jnp.bfloat16)
            .astype(jnp.float32)
            for e in range(CORES)
        ]
        for b in range(pieces):
            for c in range(0, step, whole):
                mixed = sum(
                    shares[e][b] * parts[e][b * rows : (b + 1) * rows, c : c + whole]
                    for e in range(CORES)
                )
                outs[b][:, at + c : at + c + whole] = mixed.astype(jnp.bfloat16)


def run_experts(pieces, messages, weights):
    tokens = [piece[0] for piece in pieces]
    rows, features = tokens[0].shape
    hidden = weights[0].shape[2]
    vmem = pl.BlockSpec(memory_space=pltpu.VMEM)
    return pl.pallas_call(
        functools.partial(expert_kernel, [piece[1:] for piece in pieces], len(messages)),
        out_shape=[jax.ShapeDtypeStruct((rows, features), jnp.bfloat16)] * len(pieces),
        in_specs=[vmem] * (len(pieces) + len(messages) + len(weights)),
        out_specs=[vmem] * len(pieces),
        compiler_params=pltpu.CompilerParams(vmem_limit_bytes=24 * 1024 * 1024),
        cost_estimate=pl.CostEstimate(
            flops=12 * len(pieces) * rows * features * hidden,
            bytes_accessed=12 * features * hidden,
            transcendentals=0,
        ),
        name="experts",
    )(*tokens, *messages, *weights)


def add_parts(*parts):
    total = parts[0].astype(jnp.float32)
    for part in parts[1:]:
        total = total + part.astype(jnp.float32)
    return total.astype(jnp.bfloat16)


def ring_device(
    queries,
    rotated_keys,
    value_matrix,
    stretch_pos,
    residual,
    norm_gain,
    routes,
    combine,
    gate_weight,
    up_weight,
    down_weight,
):
    chips = lax.axis_size("ctx") // CORES
    far = chips // 2
    onward, back, swap = ring_pairs(chips)

    def send(array, pairs):
        return lax.ppermute(array, "ctx", pairs)

    message = pack_message(stretch_pos, rotated_keys, value_matrix, routes, combine)

    tie = lax.optimization_barrier
    left, right = {0: message}, {0: message}
    for hop in range(1, far + 1):
        if hop == 3:
            inputs, unused = tie(((queries, residual, norm_gain), (left[1], right[1])))
            staged = (
                inputs[0] * jnp.bfloat16(QUERY_SCALE),
                inputs[1].astype(jnp.float32),
                jnp.broadcast_to(inputs[2][None, :], (8, inputs[2].shape[0])),
            )
            left[2], staged = tie((left[2], staged))
        left[hop] = send(left[hop - 1], onward)
        if hop < far:
            right[hop] = send(right[hop - 1], back)
    plane = [message] + [left[h] for h in range(1, far + 1)] + [right[h] for h in range(1, far)]
    everything = plane + [send(m, swap) for m in plane]
    everything, own_weights = tie((everything, (gate_weight, up_weight, down_weight)))
    twin_gate, twin_up, twin_down = [send(w, swap) for w in own_weights]
    hidden_upper, upper = attend(0, staged, everything)
    everything, upper = tie((everything, upper))
    hidden_lower, lower = attend(1, staged, everything)
    lower, twin_gate, twin_up = tie((lower, twin_gate, twin_up))
    weights = (gate_weight, up_weight, down_weight, twin_gate, twin_up, twin_down)

    from_left, from_right = {(0, 0): upper, (0, 1): lower}, {(0, 0): upper, (0, 1): lower}
    outs = {}

    def later(array, than):
        return tie((array, than))[0]

    def experts_on(tokens, used, after):
        used, after = tie((used, after))
        return run_experts(tokens, used, weights), after

    def experts_of(hop, half, after):
        tokens = [(from_left[hop, half], 0, half), (from_right[hop, half], 1, half)]
        return experts_on(tokens, [left[hop], right[hop]], after)

    last = (upper, lower)
    for hop in range(1, far + 1):
        for half in range(2):
            onto, backto = from_left[hop - 1, half], from_right[hop - 1, half]
            if hop > 1:
                before = (hop - 1, 1 - half) if half == 1 else (hop - 2, 1)
                if before[0] > 0:
                    outs[before], unused = experts_of(*before, last)
                    last = outs[before]
                    onto, backto, last = tie((onto, backto, last))
                    outs[before] = last
            if hop < far or half == 0:
                from_left[hop, half] = send(onto, onward)
            if hop < far or half == 1:
                from_right[hop, half] = send(backto, back)
    outs[far - 1, 1], unused = experts_of(far - 1, 1, last)
    outs[far - 1, 0], outs[far - 1, 1] = tie((outs[far - 1, 0], outs[far - 1, 1]))
    out_left = {key: pair[0] for key, pair in outs.items()}
    out_right = {key: pair[1] for key, pair in outs.items()}

    sums_on = {1: send(out_right[far - 1, 1], onward)}
    sums_back = {0: send(out_left[far - 1, 0], back)}
    (far_upper, far_lower), unused = experts_on(
        [(from_left[far, 0], 0, 0), (from_right[far, 1], 0, 1)], [left[far]], outs[far - 1, 1]
    )
    sums_on[0] = send(far_upper, onward)
    sums_back[1] = send(far_lower, back)
    own_out, unused = experts_on([(upper, 0, 0), (lower, 0, 1)], [message], (far_upper, far_lower))
    for hop in range(far - 1, 0, -1):
        onto, backto = sums_on[0], sums_back[1]
        if hop < far - 1:
            sums_on[1] = later(sums_on[1], earlier[0])
            sums_back[0] = later(sums_back[0], earlier[1])
            sums_on[1] = send(add_parts(sums_on[1], out_right[hop, 1]), onward)
            sums_back[0] = send(add_parts(sums_back[0], out_left[hop, 0]), back)
        if hop == 1:
            onto, backto = later(onto, own_out), later(backto, own_out)
        earlier = (onto, backto)
        sums_on[0] = send(add_parts(onto, out_right[hop, 0]), onward)
        sums_back[1] = send(add_parts(backto, out_left[hop, 1]), back)
    hidden_state = (hidden_upper, hidden_lower)
    return jnp.concatenate(
        [
            (
                hidden_state[half]
                + own_out[half].astype(jnp.float32)
                + sums_on[half].astype(jnp.float32)
                + sums_back[half].astype(jnp.float32)
            ).astype(jnp.bfloat16)
            for half in range(2)
        ],
        axis=0,
    )


def exchange_device(
    queries,
    rotated_keys,
    value_matrix,
    stretch_pos,
    residual,
    norm_gain,
    routes,
    combine,
    gate_weight,
    up_weight,
    down_weight,
):
    tok_rows = queries.shape[0]
    kv_heads = rotated_keys.shape[1] // HEAD_SIZE
    head_group = queries.shape[1] // rotated_keys.shape[1]
    ctx_count = lax.axis_size("ctx")
    positions = stretch_pos[0] * tok_rows + jnp.arange(tok_rows, dtype=jnp.int32)
    latest = jnp.max(positions)
    query_heads = queries.reshape(tok_rows, kv_heads, head_group, HEAD_SIZE)
    scale_factor = 1.0 / math.sqrt(HEAD_SIZE)

    def update(state, key_block, value_block, key_pos):
        best, total, accum = state
        scores = (
            jnp.einsum(
                "tagd,sad->agts",
                query_heads,
                key_block.reshape(-1, kv_heads, HEAD_SIZE),
                preferred_element_type=jnp.float32,
            )
            * scale_factor
        )
        scores = jnp.where(
            key_pos[None, None, None, :] <= positions[None, None, :, None], scores, jnp.float32(NEG)
        )
        fresh = jnp.maximum(best, jnp.max(scores, axis=-1))
        shrink = jnp.exp(best - fresh)
        expo = jnp.exp(scores - fresh[..., None])
        total = total * shrink + jnp.sum(expo, axis=-1)
        weighted = jnp.einsum(
            "agts,sad->agtd",
            expo.astype(jnp.bfloat16),
            value_block.reshape(-1, kv_heads, HEAD_SIZE),
            preferred_element_type=jnp.float32,
        )
        accum = accum * shrink[..., None] + weighted
        return (fresh, total, accum)

    start_state = (
        jnp.full((kv_heads, head_group, tok_rows), NEG, jnp.float32),
        jnp.zeros((kv_heads, head_group, tok_rows), jnp.float32),
        jnp.zeros((kv_heads, head_group, tok_rows, HEAD_SIZE), jnp.float32),
    )
    key_part = lax.all_gather(rotated_keys, "ctx", axis=0, tiled=True)
    value_part = lax.all_gather(value_matrix, "ctx", axis=0, tiled=True)
    pos_part = lax.all_gather(positions, "ctx", axis=0, tiled=True)
    span = key_part.shape[0]
    width = 512
    blocks = span // width
    stacked = (
        key_part.reshape(blocks, width, -1),
        value_part.reshape(blocks, width, -1),
        pos_part.reshape(blocks, width),
    )

    def advance(inner, item):
        key_block, value_block, key_pos = item
        result = lax.cond(
            jnp.min(key_pos) > latest,
            lambda kept: kept,
            lambda kept: update(kept, key_block, value_block, key_pos),
            inner,
        )
        return (result, None)

    final, unused = lax.scan(advance, start_state, stacked)
    best, total, accum = final
    attended = (
        jnp.transpose(accum / total[..., None], (2, 0, 1, 3))
        .reshape(tok_rows, -1)
        .astype(jnp.bfloat16)
    )
    hidden_state = residual.astype(jnp.float32) + attended.astype(jnp.float32)
    meansq = jnp.mean(hidden_state * hidden_state, axis=-1, keepdims=True)
    normed = (hidden_state * lax.rsqrt(meansq + 1e-06) * norm_gain).astype(jnp.bfloat16)
    local_experts = gate_weight.shape[0]
    total_experts = local_experts * ctx_count
    top_count = routes.shape[1]
    capacity = min(
        tok_rows,
        tok_rows * top_count // total_experts + max(1, tok_rows * top_count // (8 * total_experts)),
    )
    flat_routes = routes.reshape(-1)
    onehot = (flat_routes[:, None] == jnp.arange(total_experts, dtype=jnp.int32)[None, :]).astype(
        jnp.int32
    )
    earlier = jnp.cumsum(onehot, axis=0) - onehot
    ranking = jnp.sum(earlier * onehot, axis=1)
    slot_ids = flat_routes * capacity + ranking
    selector = jnp.any(
        slot_ids.reshape(tok_rows, top_count)[:, :, None]
        == jnp.arange(total_experts * capacity, dtype=jnp.int32)[None, None, :],
        axis=1,
    ).astype(jnp.bfloat16)
    outgoing = jnp.einsum("ts,td->sd", selector, normed, preferred_element_type=jnp.float32).astype(
        jnp.bfloat16
    )
    outgoing = outgoing.reshape(ctx_count, local_experts, capacity, D)
    incoming = lax.all_to_all(outgoing, "ctx", split_axis=0, concat_axis=0, tiled=True)
    gate = jnp.einsum("secd,edh->sech", incoming, gate_weight, preferred_element_type=jnp.float32)
    upper = jnp.einsum("secd,edh->sech", incoming, up_weight, preferred_element_type=jnp.float32)
    act = (jax.nn.silu(gate) * upper).astype(jnp.bfloat16)
    returned = lax.all_to_all(
        jnp.einsum("sech,ehd->secd", act, down_weight, preferred_element_type=jnp.float32).astype(
            jnp.bfloat16
        ),
        "ctx",
        split_axis=0,
        concat_axis=0,
        tiled=True,
    )
    flat_back = returned.reshape(total_experts * capacity, D)
    picked = jnp.take(flat_back, slot_ids, axis=0).reshape(tok_rows, top_count, D)
    mixture = jnp.sum(combine[:, :, None] * picked.astype(jnp.float32), axis=1)
    return (hidden_state + mixture).astype(jnp.bfloat16)


def solution(mesh):
    placed = (
        P(("groups", "ctx"), None),
        P(("groups", "ctx"), None),
        P(("groups", "ctx"), None),
        P(("groups", "ctx")),
        P(("groups", "ctx"), None),
        P(),
        P(("groups", "ctx"), None),
        P(("groups", "ctx"), None),
        P("ctx", None, None),
        P("ctx", None, None),
        P("ctx", None, None),
    )
    ctx_count = mesh.shape["ctx"]

    def on_device(*arguments):
        routes, gate_weight = arguments[6], arguments[8]
        dense = 4 * routes.shape[1] >= gate_weight.shape[0] * ctx_count
        ringed = gate_weight.shape[0] == 1 and ctx_count % (2 * CORES) == 0
        ringed = ringed and ctx_count >= 6 * CORES and 2 * routes.shape[1] == EXTRA
        return (ring_device if dense and ringed else exchange_device)(*arguments)

    return jax.shard_map(
        on_device, mesh=mesh, in_specs=placed, out_specs=P(("groups", "ctx"), None), check_vma=False
    )
```

```python
import functools
import math

import jax
import jax.numpy as jnp
from jax import lax
from jax.experimental import pallas as pl
from jax.experimental.pallas import tpu as pltpu
from jax.sharding import PartitionSpec as P

D = 2048
HEAD_SIZE = 128
CORES = 2
EXTRA = 16
QUERY_SCALE = 0.125


NEG = -1e30


def ring_pairs(chips):
    order = list(range(0, chips, 2)) + list(range(chips - 1, 0, -2))
    onward = [
        (order[i] * CORES + core, order[(i + 1) % chips] * CORES + core)
        for i in range(chips)
        for core in range(CORES)
    ]
    back = [(b, a) for a, b in onward]
    swap = [(i, i ^ 1) for i in range(chips * CORES)]
    return onward, back, swap


def pack_kernel(pos_ref, key_ref, value_ref, routes_ref, combine_ref, out_ref):
    rows, width = key_ref.shape
    top = routes_ref.shape[0]
    out_ref[0:rows, 0:width] = key_ref[...]
    out_ref[0:rows, width : 2 * width] = value_ref[...]
    weight = combine_ref[...]
    high = weight.astype(jnp.bfloat16).astype(jnp.float32)
    low = weight - high
    names = routes_ref[...].astype(jnp.float32)
    place = jnp.full((EXTRA, 2 * width - 2 * rows), pos_ref[0].astype(jnp.float32), jnp.float32)
    tail = slice(rows, rows + EXTRA)
    out_ref[tail, 0:rows] = jnp.concatenate([names, high], axis=0).astype(jnp.bfloat16)
    out_ref[tail, rows : 2 * rows] = jnp.concatenate([low, jnp.zeros_like(low)], axis=0).astype(
        jnp.bfloat16
    )
    out_ref[tail, 2 * rows : 2 * width] = place.astype(jnp.bfloat16)


def pack_message(stretch_pos, keys, values, routes, combine):
    rows, width = keys.shape
    vmem = pl.BlockSpec(memory_space=pltpu.VMEM)
    return pl.pallas_call(
        pack_kernel,
        out_shape=jax.ShapeDtypeStruct((rows + EXTRA, 2 * width), jnp.bfloat16),
        in_specs=[pl.BlockSpec(memory_space=pltpu.SMEM), vmem, vmem, vmem, vmem],
        out_specs=vmem,
        name="pack_message",
    )(stretch_pos, keys, values, routes.T, combine.T)


def attend_kernel(count, half, *refs):
    query_ref, residual_ref, gain_ref = refs[:3]
    messages = refs[3 : 3 + count]
    hidden_ref, normed_ref, key_ext, value_ext = refs[3 + count :]
    features = query_ref.shape[1]
    some = query_ref.shape[0] // 2
    mine = slice(half * some, (half + 1) * some)
    rows = messages[0].shape[0] - EXTRA
    kv_heads = key_ext.shape[0]
    heads = features // HEAD_SIZE
    group = heads // kv_heads
    span = count * rows
    width = kv_heads * HEAD_SIZE
    sub = lax.broadcasted_iota(jnp.int32, (rows, rows), 0)
    lane = lax.broadcasted_iota(jnp.int32, (rows, rows), 1)
    ahead = (sub - lane).astype(jnp.float32)
    own_pos = messages[0][rows : rows + EXTRA, 256 : 256 + rows][0:1].astype(jnp.float32)
    ones = jnp.ones((rows, HEAD_SIZE), jnp.bfloat16)
    for block in range(count):
        ref = messages[block]
        at = slice(block * rows, (block + 1) * rows)
        pos = ref[rows : rows + EXTRA, 256 : 256 + rows][0:1].astype(jnp.float32)
        later = (pos - own_pos) * float(rows) + ahead
        bias = jnp.where(later > 0.0, NEG, 0.0).astype(jnp.bfloat16)
        for a in range(kv_heads):
            key_ext[a, at, 0:HEAD_SIZE] = ref[0:rows, a * HEAD_SIZE : (a + 1) * HEAD_SIZE]
            key_ext[a, at, HEAD_SIZE : HEAD_SIZE + rows] = bias
            value_ext[a, at, 0:HEAD_SIZE] = ref[
                0:rows, width + a * HEAD_SIZE : width + (a + 1) * HEAD_SIZE
            ]
            value_ext[a, at, HEAD_SIZE : 2 * HEAD_SIZE] = ones
    eye = jnp.where(sub == lane, 1.0, 0.0).astype(jnp.bfloat16)[mine]
    rate = math.log2(math.e) / math.sqrt(HEAD_SIZE) / QUERY_SCALE
    step = min(512, span)
    pair = 4
    squares = jnp.zeros((some, HEAD_SIZE), jnp.float32)
    for first in range(0, heads, pair):
        a = first // group
        stacked = jnp.concatenate(
            [
                jnp.concatenate([query_ref[mine, h * HEAD_SIZE : (h + 1) * HEAD_SIZE], eye], axis=1)
                for h in range(first, first + pair)
            ],
            axis=0,
        )
        scores = [
            lax.dot_general(
                stacked,
                key_ext[a, at : at + step, :],
                (((1,), (1,)), ((), ())),
                preferred_element_type=jnp.float32,
            )
            for at in range(0, span, step)
        ]
        best = functools.reduce(jnp.maximum, scores)
        best = jnp.max(best, axis=1, keepdims=True)
        total = None
        for i, part in enumerate(scores):
            probs = jnp.exp2((part - best) * rate).astype(jnp.bfloat16)
            term = jnp.dot(
                probs,
                value_ext[a, i * step : (i + 1) * step, :],
                preferred_element_type=jnp.float32,
            )
            total = term if total is None else total + term
        attended = (total[:, 0:HEAD_SIZE] / total[:, HEAD_SIZE:]).astype(jnp.bfloat16)
        for j in range(pair):
            cols = slice((first + j) * HEAD_SIZE, (first + j + 1) * HEAD_SIZE)
            state = residual_ref[mine, cols] + attended[
                j * some : (j + 1) * some
            ].astype(jnp.float32)
            hidden_ref[:, cols] = state
            squares = squares + state * state
    meansq = jnp.sum(squares, axis=1, keepdims=True) / float(heads * HEAD_SIZE)
    inverse = lax.rsqrt(meansq + 1e-06)
    for h in range(heads):
        cols = slice(h * HEAD_SIZE, (h + 1) * HEAD_SIZE)
        normed_ref[:, cols] = (hidden_ref[:, cols] * inverse * gain_ref[0:1, cols]).astype(
            jnp.bfloat16
        )


def attend(half, staged, messages):
    rows, features = staged[0].shape
    some = rows // 2
    count = len(messages)
    kv_heads = messages[0].shape[1] // (2 * HEAD_SIZE)
    vmem = pl.BlockSpec(memory_space=pltpu.VMEM)
    span = count * rows
    return pl.pallas_call(
        functools.partial(attend_kernel, count, half),
        out_shape=(
            jax.ShapeDtypeStruct((some, features), jnp.float32),
            jax.ShapeDtypeStruct((some, features), jnp.bfloat16),
        ),
        in_specs=[vmem] * (3 + count),
        out_specs=(vmem, vmem),
        scratch_shapes=[
            pltpu.VMEM((kv_heads, span, 2 * HEAD_SIZE), jnp.bfloat16),
            pltpu.VMEM((kv_heads, span, 2 * HEAD_SIZE), jnp.bfloat16),
        ],
        compiler_params=pltpu.CompilerParams(vmem_limit_bytes=28 * 1024 * 1024),
        cost_estimate=pl.CostEstimate(
            flops=4 * rows * span * features, bytes_accessed=4 * 1024 * 1024, transcendentals=0
        ),
        name="attend",
    )(*staged, *messages)


def expert_kernel(places, count, *refs):
    pieces = len(places)
    tokens = refs[:pieces]
    messages = refs[pieces : pieces + count]
    weights = refs[pieces + count : pieces + count + 3 * CORES]
    outs = refs[pieces + count + 3 * CORES :]
    rows, features = tokens[0].shape
    whole = messages[0].shape[0] - EXTRA
    top = EXTRA // 2
    me = lax.axis_index("ctx")
    normed = jnp.concatenate([ref[...] for ref in tokens], axis=0)
    shares, acts = [], []
    for e in range(CORES):
        gate_ref, up_ref = weights[3 * e], weights[3 * e + 1]
        gate = jnp.dot(normed, gate_ref[0], preferred_element_type=jnp.float32)
        upper = jnp.dot(normed, up_ref[0], preferred_element_type=jnp.float32)
        acts.append((gate / (1.0 + jnp.exp(-gate)) * upper).astype(jnp.bfloat16))
        name = jnp.bitwise_xor(me, e).astype(jnp.float32)
        columns = []
        for ref in messages:
            extra = ref[whole : whole + EXTRA, 0 : 2 * whole].astype(jnp.float32)
            value = extra[top : 2 * top, 0:whole] + extra[0:top, whole : 2 * whole]
            hit = jnp.where(extra[0:top, 0:whole] == name, value, 0.0)
            line = jnp.sum(hit, axis=0, keepdims=True)
            columns.append(jnp.broadcast_to(line, (whole, whole)).T)
        shares.append([columns[m][half * rows : (half + 1) * rows] for m, half in places])
    step = 512
    for at in range(0, features, step):
        parts = [
            jnp.dot(acts[e], weights[3 * e + 2][0, :, at : at + step], preferred_element_type=jnp.float32)
            .astype(jnp.bfloat16)
            .astype(jnp.float32)
            for e in range(CORES)
        ]
        for b in range(pieces):
            for c in range(0, step, whole):
                mixed = sum(
                    shares[e][b] * parts[e][b * rows : (b + 1) * rows, c : c + whole]
                    for e in range(CORES)
                )
                outs[b][:, at + c : at + c + whole] = mixed.astype(jnp.bfloat16)


def run_experts(pieces, messages, weights):
    tokens = [piece[0] for piece in pieces]
    rows, features = tokens[0].shape
    hidden = weights[0].shape[2]
    vmem = pl.BlockSpec(memory_space=pltpu.VMEM)
    return pl.pallas_call(
        functools.partial(expert_kernel, [piece[1:] for piece in pieces], len(messages)),
        out_shape=[jax.ShapeDtypeStruct((rows, features), jnp.bfloat16)] * len(pieces),
        in_specs=[vmem] * (len(pieces) + len(messages) + len(weights)),
        out_specs=[vmem] * len(pieces),
        compiler_params=pltpu.CompilerParams(vmem_limit_bytes=24 * 1024 * 1024),
        cost_estimate=pl.CostEstimate(
            flops=12 * len(pieces) * rows * features * hidden,
            bytes_accessed=12 * features * hidden,
            transcendentals=0,
        ),
        name="experts",
    )(*tokens, *messages, *weights)


def add_parts(*parts):
    total = parts[0].astype(jnp.float32)
    for part in parts[1:]:
        total = total + part.astype(jnp.float32)
    return total.astype(jnp.bfloat16)


def ring_device(
    queries,
    rotated_keys,
    value_matrix,
    stretch_pos,
    residual,
    norm_gain,
    routes,
    combine,
    gate_weight,
    up_weight,
    down_weight,
):
    chips = lax.axis_size("ctx") // CORES
    far = chips // 2
    onward, back, swap = ring_pairs(chips)

    def send(array, pairs):
        return lax.ppermute(array, "ctx", pairs)

    message = pack_message(stretch_pos, rotated_keys, value_matrix, routes, combine)

    tie = lax.optimization_barrier
    left, right = {0: message}, {0: message}
    for hop in range(1, far + 1):
        if hop == 3:
            inputs, unused = tie(((queries, residual, norm_gain), (left[1], right[1])))
            staged = (
                inputs[0] * jnp.bfloat16(QUERY_SCALE),
                inputs[1].astype(jnp.float32),
                jnp.broadcast_to(inputs[2][None, :], (8, inputs[2].shape[0])),
            )
            left[2], staged = tie((left[2], staged))
        left[hop] = send(left[hop - 1], onward)
        if hop < far:
            right[hop] = send(right[hop - 1], back)
    plane = [message] + [left[h] for h in range(1, far + 1)] + [right[h] for h in range(1, far)]
    everything = plane + [send(m, swap) for m in plane]
    everything, own_weights = tie((everything, (gate_weight, up_weight, down_weight)))
    twin_gate, twin_up, twin_down = [send(w, swap) for w in own_weights]
    hidden_upper, upper = attend(0, staged, everything)
    everything, upper = tie((everything, upper))
    hidden_lower, lower = attend(1, staged, everything)
    lower, twin_gate, twin_up = tie((lower, twin_gate, twin_up))
    weights = (gate_weight, up_weight, down_weight, twin_gate, twin_up, twin_down)

    from_left, from_right = {(0, 0): upper, (0, 1): lower}, {(0, 0): upper, (0, 1): lower}
    outs = {}

    def later(array, than):
        return tie((array, than))[0]

    def experts_on(tokens, used, after):
        used, after = tie((used, after))
        return run_experts(tokens, used, weights), after

    def experts_of(hop, half, after):
        tokens = [(from_left[hop, half], 0, half), (from_right[hop, half], 1, half)]
        return experts_on(tokens, [left[hop], right[hop]], after)

    last = (upper, lower)
    for hop in range(1, far + 1):
        for half in range(2):
            onto, backto = from_left[hop - 1, half], from_right[hop - 1, half]
            if hop > 1:
                before = (hop - 1, 1 - half) if half == 1 else (hop - 2, 1)
                if before[0] > 0:
                    outs[before], unused = experts_of(*before, last)
                    last = outs[before]
                    onto, backto, last = tie((onto, backto, last))
                    outs[before] = last
            if hop < far or half == 0:
                from_left[hop, half] = send(onto, onward)
            if hop < far or half == 1:
                from_right[hop, half] = send(backto, back)
    outs[far - 1, 1], unused = experts_of(far - 1, 1, last)
    outs[far - 1, 0], outs[far - 1, 1] = tie((outs[far - 1, 0], outs[far - 1, 1]))
    out_left = {key: pair[0] for key, pair in outs.items()}
    out_right = {key: pair[1] for key, pair in outs.items()}

    sums_on = {1: send(out_right[far - 1, 1], onward)}
    sums_back = {0: send(out_left[far - 1, 0], back)}
    (far_upper, far_lower), unused = experts_on(
        [(from_left[far, 0], 0, 0), (from_right[far, 1], 0, 1)], [left[far]], outs[far - 1, 1]
    )
    sums_on[0] = send(far_upper, onward)
    sums_back[1] = send(far_lower, back)
    own_out, unused = experts_on(
        [(upper, 0, 0), (lower, 0, 1)], [message], (far_upper, far_lower, sums_on[1], sums_back[0])
    )
    for hop in range(far - 1, 0, -1):
        onto, backto = sums_on[0], sums_back[1]
        if hop < far - 1:
            sums_on[1] = later(sums_on[1], earlier[0])
            sums_back[0] = later(sums_back[0], earlier[1])
            sums_on[1] = send(add_parts(sums_on[1], out_right[hop, 1]), onward)
            sums_back[0] = send(add_parts(sums_back[0], out_left[hop, 0]), back)
        if hop == 1:
            onto, backto = later(onto, own_out), later(backto, own_out)
        earlier = (add_parts(onto, out_right[hop, 0]), add_parts(backto, out_left[hop, 1]))
        sums_on[0], sums_back[1] = send(earlier[0], onward), send(earlier[1], back)
    hidden_state = (hidden_upper, hidden_lower)
    return jnp.concatenate(
        [
            (
                hidden_state[half]
                + own_out[half].astype(jnp.float32)
                + sums_on[half].astype(jnp.float32)
                + sums_back[half].astype(jnp.float32)
            ).astype(jnp.bfloat16)
            for half in range(2)
        ],
        axis=0,
    )


def exchange_device(
    queries,
    rotated_keys,
    value_matrix,
    stretch_pos,
    residual,
    norm_gain,
    routes,
    combine,
    gate_weight,
    up_weight,
    down_weight,
):
    tok_rows = queries.shape[0]
    kv_heads = rotated_keys.shape[1] // HEAD_SIZE
    head_group = queries.shape[1] // rotated_keys.shape[1]
    ctx_count = lax.axis_size("ctx")
    positions = stretch_pos[0] * tok_rows + jnp.arange(tok_rows, dtype=jnp.int32)
    latest = jnp.max(positions)
    query_heads = queries.reshape(tok_rows, kv_heads, head_group, HEAD_SIZE)
    scale_factor = 1.0 / math.sqrt(HEAD_SIZE)

    def update(state, key_block, value_block, key_pos):
        best, total, accum = state
        scores = (
            jnp.einsum(
                "tagd,sad->agts",
                query_heads,
                key_block.reshape(-1, kv_heads, HEAD_SIZE),
                preferred_element_type=jnp.float32,
            )
            * scale_factor
        )
        scores = jnp.where(
            key_pos[None, None, None, :] <= positions[None, None, :, None], scores, jnp.float32(NEG)
        )
        fresh = jnp.maximum(best, jnp.max(scores, axis=-1))
        shrink = jnp.exp(best - fresh)
        expo = jnp.exp(scores - fresh[..., None])
        total = total * shrink + jnp.sum(expo, axis=-1)
        weighted = jnp.einsum(
            "agts,sad->agtd",
            expo.astype(jnp.bfloat16),
            value_block.reshape(-1, kv_heads, HEAD_SIZE),
            preferred_element_type=jnp.float32,
        )
        accum = accum * shrink[..., None] + weighted
        return (fresh, total, accum)

    start_state = (
        jnp.full((kv_heads, head_group, tok_rows), NEG, jnp.float32),
        jnp.zeros((kv_heads, head_group, tok_rows), jnp.float32),
        jnp.zeros((kv_heads, head_group, tok_rows, HEAD_SIZE), jnp.float32),
    )
    key_part = lax.all_gather(rotated_keys, "ctx", axis=0, tiled=True)
    value_part = lax.all_gather(value_matrix, "ctx", axis=0, tiled=True)
    pos_part = lax.all_gather(positions, "ctx", axis=0, tiled=True)
    span = key_part.shape[0]
    width = 512
    blocks = span // width
    stacked = (
        key_part.reshape(blocks, width, -1),
        value_part.reshape(blocks, width, -1),
        pos_part.reshape(blocks, width),
    )

    def advance(inner, item):
        key_block, value_block, key_pos = item
        result = lax.cond(
            jnp.min(key_pos) > latest,
            lambda kept: kept,
            lambda kept: update(kept, key_block, value_block, key_pos),
            inner,
        )
        return (result, None)

    final, unused = lax.scan(advance, start_state, stacked)
    best, total, accum = final
    attended = (
        jnp.transpose(accum / total[..., None], (2, 0, 1, 3))
        .reshape(tok_rows, -1)
        .astype(jnp.bfloat16)
    )
    hidden_state = residual.astype(jnp.float32) + attended.astype(jnp.float32)
    meansq = jnp.mean(hidden_state * hidden_state, axis=-1, keepdims=True)
    normed = (hidden_state * lax.rsqrt(meansq + 1e-06) * norm_gain).astype(jnp.bfloat16)
    local_experts = gate_weight.shape[0]
    total_experts = local_experts * ctx_count
    top_count = routes.shape[1]
    capacity = min(
        tok_rows,
        tok_rows * top_count // total_experts + max(1, tok_rows * top_count // (8 * total_experts)),
    )
    flat_routes = routes.reshape(-1)
    onehot = (flat_routes[:, None] == jnp.arange(total_experts, dtype=jnp.int32)[None, :]).astype(
        jnp.int32
    )
    earlier = jnp.cumsum(onehot, axis=0) - onehot
    ranking = jnp.sum(earlier * onehot, axis=1)
    slot_ids = flat_routes * capacity + ranking
    selector = jnp.any(
        slot_ids.reshape(tok_rows, top_count)[:, :, None]
        == jnp.arange(total_experts * capacity, dtype=jnp.int32)[None, None, :],
        axis=1,
    ).astype(jnp.bfloat16)
    outgoing = jnp.einsum("ts,td->sd", selector, normed, preferred_element_type=jnp.float32).astype(
        jnp.bfloat16
    )
    outgoing = outgoing.reshape(ctx_count, local_experts, capacity, D)
    incoming = lax.all_to_all(outgoing, "ctx", split_axis=0, concat_axis=0, tiled=True)
    gate = jnp.einsum("secd,edh->sech", incoming, gate_weight, preferred_element_type=jnp.float32)
    upper = jnp.einsum("secd,edh->sech", incoming, up_weight, preferred_element_type=jnp.float32)
    act = (jax.nn.silu(gate) * upper).astype(jnp.bfloat16)
    returned = lax.all_to_all(
        jnp.einsum("sech,ehd->secd", act, down_weight, preferred_element_type=jnp.float32).astype(
            jnp.bfloat16
        ),
        "ctx",
        split_axis=0,
        concat_axis=0,
        tiled=True,
    )
    flat_back = returned.reshape(total_experts * capacity, D)
    picked = jnp.take(flat_back, slot_ids, axis=0).reshape(tok_rows, top_count, D)
    mixture = jnp.sum(combine[:, :, None] * picked.astype(jnp.float32), axis=1)
    return (hidden_state + mixture).astype(jnp.bfloat16)


def solution(mesh):
    placed = (
        P(("groups", "ctx"), None),
        P(("groups", "ctx"), None),
        P(("groups", "ctx"), None),
        P(("groups", "ctx")),
        P(("groups", "ctx"), None),
        P(),
        P(("groups", "ctx"), None),
        P(("groups", "ctx"), None),
        P("ctx", None, None),
        P("ctx", None, None),
        P("ctx", None, None),
    )
    ctx_count = mesh.shape["ctx"]

    def on_device(*arguments):
        routes, gate_weight = arguments[6], arguments[8]
        dense = 4 * routes.shape[1] >= gate_weight.shape[0] * ctx_count
        ringed = gate_weight.shape[0] == 1 and ctx_count % (2 * CORES) == 0
        ringed = ringed and ctx_count >= 6 * CORES and 2 * routes.shape[1] == EXTRA
        return (ring_device if dense and ringed else exchange_device)(*arguments)

    return jax.shard_map(
        on_device, mesh=mesh, in_specs=placed, out_specs=P(("groups", "ctx"), None), check_vma=False
    )
```

```python
import functools
import math

import jax
import jax.numpy as jnp
from jax import lax
from jax.experimental import pallas as pl
from jax.experimental.pallas import tpu as pltpu
from jax.sharding import PartitionSpec as P

D = 2048
HEAD_SIZE = 128
CORES = 2
EXTRA = 16
QUERY_SCALE = 0.125


NEG = -1e30


def ring_pairs(chips):
    order = list(range(0, chips, 2)) + list(range(chips - 1, 0, -2))
    onward = [
        (order[i] * CORES + core, order[(i + 1) % chips] * CORES + core)
        for i in range(chips)
        for core in range(CORES)
    ]
    back = [(b, a) for a, b in onward]
    across = [
        (order[i] * CORES + core, order[(i + chips // 2) % chips] * CORES + core)
        for i in range(chips)
        for core in range(CORES)
    ]
    swap = [(i, i ^ 1) for i in range(chips * CORES)]
    return onward, back, across, swap


def pack_kernel(pos_ref, key_ref, value_ref, routes_ref, combine_ref, out_ref):
    rows, width = key_ref.shape
    top = routes_ref.shape[0]
    out_ref[0:rows, 0:width] = key_ref[...]
    out_ref[0:rows, width : 2 * width] = value_ref[...]
    weight = combine_ref[...]
    high = weight.astype(jnp.bfloat16).astype(jnp.float32)
    low = weight - high
    names = routes_ref[...].astype(jnp.float32)
    place = jnp.full((EXTRA, 2 * width - 2 * rows), pos_ref[0].astype(jnp.float32), jnp.float32)
    tail = slice(rows, rows + EXTRA)
    out_ref[tail, 0:rows] = jnp.concatenate([names, high], axis=0).astype(jnp.bfloat16)
    out_ref[tail, rows : 2 * rows] = jnp.concatenate([low, jnp.zeros_like(low)], axis=0).astype(
        jnp.bfloat16
    )
    out_ref[tail, 2 * rows : 2 * width] = place.astype(jnp.bfloat16)


def pack_message(stretch_pos, keys, values, routes, combine):
    rows, width = keys.shape
    vmem = pl.BlockSpec(memory_space=pltpu.VMEM)
    return pl.pallas_call(
        pack_kernel,
        out_shape=jax.ShapeDtypeStruct((rows + EXTRA, 2 * width), jnp.bfloat16),
        in_specs=[pl.BlockSpec(memory_space=pltpu.SMEM), vmem, vmem, vmem, vmem],
        out_specs=vmem,
        name="pack_message",
    )(stretch_pos, keys, values, routes.T, combine.T)


def attend_kernel(count, half, *refs):
    query_ref, residual_ref, gain_ref = refs[:3]
    messages = refs[3 : 3 + count]
    hidden_ref, normed_ref, key_ext, value_ext = refs[3 + count :]
    features = query_ref.shape[1]
    some = query_ref.shape[0] // 2
    mine = slice(half * some, (half + 1) * some)
    rows = messages[0].shape[0] - EXTRA
    kv_heads = key_ext.shape[0]
    heads = features // HEAD_SIZE
    group = heads // kv_heads
    span = count * rows
    width = kv_heads * HEAD_SIZE
    sub = lax.broadcasted_iota(jnp.int32, (rows, rows), 0)
    lane = lax.broadcasted_iota(jnp.int32, (rows, rows), 1)
    ahead = (sub - lane).astype(jnp.float32)
    own_pos = messages[0][rows : rows + EXTRA, 256 : 256 + rows][0:1].astype(jnp.float32)
    ones = jnp.ones((rows, HEAD_SIZE), jnp.bfloat16)
    for block in range(count):
        ref = messages[block]
        at = slice(block * rows, (block + 1) * rows)
        pos = ref[rows : rows + EXTRA, 256 : 256 + rows][0:1].astype(jnp.float32)
        later = (pos - own_pos) * float(rows) + ahead
        bias = jnp.where(later > 0.0, NEG, 0.0).astype(jnp.bfloat16)
        for a in range(kv_heads):
            key_ext[a, at, 0:HEAD_SIZE] = ref[0:rows, a * HEAD_SIZE : (a + 1) * HEAD_SIZE]
            key_ext[a, at, HEAD_SIZE : HEAD_SIZE + rows] = bias
            value_ext[a, at, 0:HEAD_SIZE] = ref[
                0:rows, width + a * HEAD_SIZE : width + (a + 1) * HEAD_SIZE
            ]
            value_ext[a, at, HEAD_SIZE : 2 * HEAD_SIZE] = ones
    eye = jnp.where(sub == lane, 1.0, 0.0).astype(jnp.bfloat16)[mine]
    rate = math.log2(math.e) / math.sqrt(HEAD_SIZE) / QUERY_SCALE
    step = min(512, span)
    pair = 4
    squares = jnp.zeros((some, HEAD_SIZE), jnp.float32)

    def scores_of(first):
        stacked = jnp.concatenate(
            [
                jnp.concatenate([query_ref[mine, h * HEAD_SIZE : (h + 1) * HEAD_SIZE], eye], axis=1)
                for h in range(first, first + pair)
            ],
            axis=0,
        )
        return [
            lax.dot_general(
                stacked,
                key_ext[first // group, at : at + step, :],
                (((1,), (1,)), ((), ())),
                preferred_element_type=jnp.float32,
            )
            for at in range(0, span, step)
        ]

    ready = scores_of(0)
    for first in range(0, heads, pair):
        a = first // group
        scores = ready
        if first + pair < heads:
            ready = scores_of(first + pair)
        best = functools.reduce(jnp.maximum, scores)
        best = jnp.max(best, axis=1, keepdims=True)
        total = None
        for i, part in enumerate(scores):
            probs = jnp.exp2((part - best) * rate).astype(jnp.bfloat16)
            term = jnp.dot(
                probs,
                value_ext[a, i * step : (i + 1) * step, :],
                preferred_element_type=jnp.float32,
            )
            total = term if total is None else total + term
        attended = (total[:, 0:HEAD_SIZE] / total[:, HEAD_SIZE:]).astype(jnp.bfloat16)
        for j in range(pair):
            cols = slice((first + j) * HEAD_SIZE, (first + j + 1) * HEAD_SIZE)
            state = residual_ref[mine, cols] + attended[
                j * some : (j + 1) * some
            ].astype(jnp.float32)
            hidden_ref[:, cols] = state
            squares = squares + state * state
    meansq = jnp.sum(squares, axis=1, keepdims=True) / float(heads * HEAD_SIZE)
    inverse = lax.rsqrt(meansq + 1e-06)
    for h in range(heads):
        cols = slice(h * HEAD_SIZE, (h + 1) * HEAD_SIZE)
        normed_ref[:, cols] = (hidden_ref[:, cols] * inverse * gain_ref[0:1, cols]).astype(
            jnp.bfloat16
        )


def attend(half, staged, messages):
    rows, features = staged[0].shape
    some = rows // 2
    count = len(messages)
    kv_heads = messages[0].shape[1] // (2 * HEAD_SIZE)
    vmem = pl.BlockSpec(memory_space=pltpu.VMEM)
    span = count * rows
    return pl.pallas_call(
        functools.partial(attend_kernel, count, half),
        out_shape=(
            jax.ShapeDtypeStruct((some, features), jnp.float32),
            jax.ShapeDtypeStruct((some, features), jnp.bfloat16),
        ),
        in_specs=[vmem] * (3 + count),
        out_specs=(vmem, vmem),
        scratch_shapes=[
            pltpu.VMEM((kv_heads, span, 2 * HEAD_SIZE), jnp.bfloat16),
            pltpu.VMEM((kv_heads, span, 2 * HEAD_SIZE), jnp.bfloat16),
        ],
        compiler_params=pltpu.CompilerParams(vmem_limit_bytes=28 * 1024 * 1024),
        cost_estimate=pl.CostEstimate(
            flops=4 * rows * span * features, bytes_accessed=4 * 1024 * 1024, transcendentals=0
        ),
        name="attend",
    )(*staged, *messages)


def expert_kernel(places, count, *refs):
    pieces = len(places)
    tokens = refs[:pieces]
    messages = refs[pieces : pieces + count]
    weights = refs[pieces + count : pieces + count + 3 * CORES]
    outs = refs[pieces + count + 3 * CORES :]
    rows, features = tokens[0].shape
    whole = messages[0].shape[0] - EXTRA
    top = EXTRA // 2
    me = lax.axis_index("ctx")
    normed = jnp.concatenate([ref[...] for ref in tokens], axis=0)
    shares, acts = [], []
    for e in range(CORES):
        gate_ref, up_ref = weights[3 * e], weights[3 * e + 1]
        gate = jnp.dot(normed, gate_ref[0], preferred_element_type=jnp.float32)
        upper = jnp.dot(normed, up_ref[0], preferred_element_type=jnp.float32)
        acts.append((gate / (1.0 + jnp.exp(-gate)) * upper).astype(jnp.bfloat16))
        name = jnp.bitwise_xor(me, e).astype(jnp.float32)
        columns = []
        for ref in messages:
            extra = ref[whole : whole + EXTRA, 0 : 2 * whole].astype(jnp.float32)
            value = extra[top : 2 * top, 0:whole] + extra[0:top, whole : 2 * whole]
            hit = jnp.where(extra[0:top, 0:whole] == name, value, 0.0)
            line = jnp.sum(hit, axis=0, keepdims=True)
            columns.append(jnp.broadcast_to(line, (whole, whole)).T)
        shares.append([columns[m][half * rows : (half + 1) * rows] for m, half in places])
    step = 512
    for at in range(0, features, step):
        parts = [
            jnp.dot(acts[e], weights[3 * e + 2][0, :, at : at + step], preferred_element_type=jnp.float32)
            .astype(jnp.bfloat16)
            .astype(jnp.float32)
            for e in range(CORES)
        ]
        for b in range(pieces):
            for c in range(0, step, whole):
                mixed = sum(
                    shares[e][b] * parts[e][b * rows : (b + 1) * rows, c : c + whole]
                    for e in range(CORES)
                )
                outs[b][:, at + c : at + c + whole] = mixed.astype(jnp.bfloat16)


def run_experts(pieces, messages, weights):
    tokens = [piece[0] for piece in pieces]
    rows, features = tokens[0].shape
    hidden = weights[0].shape[2]
    vmem = pl.BlockSpec(memory_space=pltpu.VMEM)
    return pl.pallas_call(
        functools.partial(expert_kernel, [piece[1:] for piece in pieces], len(messages)),
        out_shape=[jax.ShapeDtypeStruct((rows, features), jnp.bfloat16)] * len(pieces),
        in_specs=[vmem] * (len(pieces) + len(messages) + len(weights)),
        out_specs=[vmem] * len(pieces),
        compiler_params=pltpu.CompilerParams(vmem_limit_bytes=24 * 1024 * 1024),
        cost_estimate=pl.CostEstimate(
            flops=12 * len(pieces) * rows * features * hidden,
            bytes_accessed=12 * features * hidden,
            transcendentals=0,
        ),
        name="experts",
    )(*tokens, *messages, *weights)


def add_parts(*parts):
    total = parts[0].astype(jnp.float32)
    for part in parts[1:]:
        total = total + part.astype(jnp.float32)
    return total.astype(jnp.bfloat16)


def ring_device(
    queries,
    rotated_keys,
    value_matrix,
    stretch_pos,
    residual,
    norm_gain,
    routes,
    combine,
    gate_weight,
    up_weight,
    down_weight,
):
    chips = lax.axis_size("ctx") // CORES
    far = chips // 2
    onward, back, across, swap = ring_pairs(chips)

    def send(array, pairs):
        return lax.ppermute(array, "ctx", pairs)

    message = pack_message(stretch_pos, rotated_keys, value_matrix, routes, combine)

    tie = lax.optimization_barrier
    left, right = {0: message}, {0: message}
    for hop in range(1, far + 1):
        if hop == 3:
            inputs, unused = tie(((queries, residual, norm_gain), (left[1], right[1])))
            staged = (
                inputs[0] * jnp.bfloat16(QUERY_SCALE),
                inputs[1].astype(jnp.float32),
                jnp.broadcast_to(inputs[2][None, :], (8, inputs[2].shape[0])),
            )
            left[2], staged = tie((left[2], staged))
        if hop < far:
            left[hop] = send(left[hop - 1], onward)
            right[hop] = send(right[hop - 1], back)
        if hop == 1:
            left[far] = send(message, across)
    plane = [message] + [left[h] for h in range(1, far + 1)] + [right[h] for h in range(1, far)]
    left[far], unused = tie((left[far], right[far - 1]))
    plane[far] = left[far]
    everything = plane + [send(m, swap) for m in plane]
    everything, own_weights = tie((everything, (gate_weight, up_weight, down_weight)))
    twin_gate, twin_up, twin_down = [send(w, swap) for w in own_weights]
    hidden_upper, upper = attend(0, staged, everything)
    everything, upper = tie((everything, upper))
    hidden_lower, lower = attend(1, staged, everything)
    lower, twin_gate, twin_up = tie((lower, twin_gate, twin_up))
    weights = (gate_weight, up_weight, down_weight, twin_gate, twin_up, twin_down)

    from_left, from_right = {(0, 0): upper, (0, 1): lower}, {(0, 0): upper, (0, 1): lower}
    outs = {}

    def later(array, than):
        return tie((array, than))[0]

    def experts_on(tokens, used, after):
        used, after = tie((used, after))
        return run_experts(tokens, used, weights), after

    def experts_of(hop, half, after):
        tokens = [(from_left[hop, half], 0, half), (from_right[hop, half], 1, half)]
        return experts_on(tokens, [left[hop], right[hop]], after)

    last = (upper, lower)
    for hop in range(1, far + 1):
        for half in range(2):
            onto, backto = from_left[hop - 1, half], from_right[hop - 1, half]
            if hop > 1:
                before = (hop - 1, 1 - half) if half == 1 else (hop - 2, 1)
                if before[0] > 0:
                    outs[before], unused = experts_of(*before, last)
                    last = outs[before]
                    onto, backto, last = tie((onto, backto, last))
                    outs[before] = last
            if hop < far or half == 0:
                from_left[hop, half] = send(onto, onward)
            if hop < far or half == 1:
                from_right[hop, half] = send(backto, back)
    outs[far - 1, 1], unused = experts_of(far - 1, 1, last)
    outs[far - 1, 0], outs[far - 1, 1] = tie((outs[far - 1, 0], outs[far - 1, 1]))
    out_left = {key: pair[0] for key, pair in outs.items()}
    out_right = {key: pair[1] for key, pair in outs.items()}

    sums_on = {1: send(out_right[far - 1, 1], onward)}
    sums_back = {0: send(out_left[far - 1, 0], back)}
    (far_upper, far_lower), unused = experts_on(
        [(from_left[far, 0], 0, 0), (from_right[far, 1], 0, 1)], [left[far]], outs[far - 1, 1]
    )
    sums_on[0] = send(far_upper, onward)
    sums_back[1] = send(far_lower, back)
    own_out, unused = experts_on(
        [(upper, 0, 0), (lower, 0, 1)], [message], (far_upper, far_lower, sums_on[1], sums_back[0])
    )
    for hop in range(far - 1, 0, -1):
        onto, backto = sums_on[0], sums_back[1]
        if hop < far - 1:
            sums_on[1] = later(sums_on[1], earlier[0])
            sums_back[0] = later(sums_back[0], earlier[1])
            sums_on[1] = send(add_parts(sums_on[1], out_right[hop, 1]), onward)
            sums_back[0] = send(add_parts(sums_back[0], out_left[hop, 0]), back)
        if hop == 1:
            onto, backto = later(onto, own_out), later(backto, own_out)
        earlier = (add_parts(onto, out_right[hop, 0]), add_parts(backto, out_left[hop, 1]))
        sums_on[0], sums_back[1] = send(earlier[0], onward), send(earlier[1], back)
    hidden_state = (hidden_upper, hidden_lower)
    return jnp.concatenate(
        [
            (
                hidden_state[half]
                + own_out[half].astype(jnp.float32)
                + sums_on[half].astype(jnp.float32)
                + sums_back[half].astype(jnp.float32)
            ).astype(jnp.bfloat16)
            for half in range(2)
        ],
        axis=0,
    )


def exchange_device(
    queries,
    rotated_keys,
    value_matrix,
    stretch_pos,
    residual,
    norm_gain,
    routes,
    combine,
    gate_weight,
    up_weight,
    down_weight,
):
    tok_rows = queries.shape[0]
    kv_heads = rotated_keys.shape[1] // HEAD_SIZE
    head_group = queries.shape[1] // rotated_keys.shape[1]
    ctx_count = lax.axis_size("ctx")
    positions = stretch_pos[0] * tok_rows + jnp.arange(tok_rows, dtype=jnp.int32)
    latest = jnp.max(positions)
    query_heads = queries.reshape(tok_rows, kv_heads, head_group, HEAD_SIZE)
    scale_factor = 1.0 / math.sqrt(HEAD_SIZE)

    def update(state, key_block, value_block, key_pos):
        best, total, accum = state
        scores = (
            jnp.einsum(
                "tagd,sad->agts",
                query_heads,
                key_block.reshape(-1, kv_heads, HEAD_SIZE),
                preferred_element_type=jnp.float32,
            )
            * scale_factor
        )
        scores = jnp.where(
            key_pos[None, None, None, :] <= positions[None, None, :, None], scores, jnp.float32(NEG)
        )
        fresh = jnp.maximum(best, jnp.max(scores, axis=-1))
        shrink = jnp.exp(best - fresh)
        expo = jnp.exp(scores - fresh[..., None])
        total = total * shrink + jnp.sum(expo, axis=-1)
        weighted = jnp.einsum(
            "agts,sad->agtd",
            expo.astype(jnp.bfloat16),
            value_block.reshape(-1, kv_heads, HEAD_SIZE),
            preferred_element_type=jnp.float32,
        )
        accum = accum * shrink[..., None] + weighted
        return (fresh, total, accum)

    start_state = (
        jnp.full((kv_heads, head_group, tok_rows), NEG, jnp.float32),
        jnp.zeros((kv_heads, head_group, tok_rows), jnp.float32),
        jnp.zeros((kv_heads, head_group, tok_rows, HEAD_SIZE), jnp.float32),
    )
    key_part = lax.all_gather(rotated_keys, "ctx", axis=0, tiled=True)
    value_part = lax.all_gather(value_matrix, "ctx", axis=0, tiled=True)
    pos_part = lax.all_gather(positions, "ctx", axis=0, tiled=True)
    span = key_part.shape[0]
    width = 512
    blocks = span // width
    stacked = (
        key_part.reshape(blocks, width, -1),
        value_part.reshape(blocks, width, -1),
        pos_part.reshape(blocks, width),
    )

    def advance(inner, item):
        key_block, value_block, key_pos = item
        result = lax.cond(
            jnp.min(key_pos) > latest,
            lambda kept: kept,
            lambda kept: update(kept, key_block, value_block, key_pos),
            inner,
        )
        return (result, None)

    final, unused = lax.scan(advance, start_state, stacked)
    best, total, accum = final
    attended = (
        jnp.transpose(accum / total[..., None], (2, 0, 1, 3))
        .reshape(tok_rows, -1)
        .astype(jnp.bfloat16)
    )
    hidden_state = residual.astype(jnp.float32) + attended.astype(jnp.float32)
    meansq = jnp.mean(hidden_state * hidden_state, axis=-1, keepdims=True)
    normed = (hidden_state * lax.rsqrt(meansq + 1e-06) * norm_gain).astype(jnp.bfloat16)
    local_experts = gate_weight.shape[0]
    total_experts = local_experts * ctx_count
    top_count = routes.shape[1]
    capacity = min(
        tok_rows,
        tok_rows * top_count // total_experts + max(1, tok_rows * top_count // (8 * total_experts)),
    )
    flat_routes = routes.reshape(-1)
    onehot = (flat_routes[:, None] == jnp.arange(total_experts, dtype=jnp.int32)[None, :]).astype(
        jnp.int32
    )
    earlier = jnp.cumsum(onehot, axis=0) - onehot
    ranking = jnp.sum(earlier * onehot, axis=1)
    slot_ids = flat_routes * capacity + ranking
    selector = jnp.any(
        slot_ids.reshape(tok_rows, top_count)[:, :, None]
        == jnp.arange(total_experts * capacity, dtype=jnp.int32)[None, None, :],
        axis=1,
    ).astype(jnp.bfloat16)
    outgoing = jnp.einsum("ts,td->sd", selector, normed, preferred_element_type=jnp.float32).astype(
        jnp.bfloat16
    )
    outgoing = outgoing.reshape(ctx_count, local_experts, capacity, D)
    incoming = lax.all_to_all(outgoing, "ctx", split_axis=0, concat_axis=0, tiled=True)
    gate = jnp.einsum("secd,edh->sech", incoming, gate_weight, preferred_element_type=jnp.float32)
    upper = jnp.einsum("secd,edh->sech", incoming, up_weight, preferred_element_type=jnp.float32)
    act = (jax.nn.silu(gate) * upper).astype(jnp.bfloat16)
    returned = lax.all_to_all(
        jnp.einsum("sech,ehd->secd", act, down_weight, preferred_element_type=jnp.float32).astype(
            jnp.bfloat16
        ),
        "ctx",
        split_axis=0,
        concat_axis=0,
        tiled=True,
    )
    flat_back = returned.reshape(total_experts * capacity, D)
    picked = jnp.take(flat_back, slot_ids, axis=0).reshape(tok_rows, top_count, D)
    mixture = jnp.sum(combine[:, :, None] * picked.astype(jnp.float32), axis=1)
    return (hidden_state + mixture).astype(jnp.bfloat16)


def solution(mesh):
    placed = (
        P(("groups", "ctx"), None),
        P(("groups", "ctx"), None),
        P(("groups", "ctx"), None),
        P(("groups", "ctx")),
        P(("groups", "ctx"), None),
        P(),
        P(("groups", "ctx"), None),
        P(("groups", "ctx"), None),
        P("ctx", None, None),
        P("ctx", None, None),
        P("ctx", None, None),
    )
    ctx_count = mesh.shape["ctx"]

    def on_device(*arguments):
        routes, gate_weight = arguments[6], arguments[8]
        dense = 4 * routes.shape[1] >= gate_weight.shape[0] * ctx_count
        ringed = gate_weight.shape[0] == 1 and ctx_count % (2 * CORES) == 0
        ringed = ringed and ctx_count >= 6 * CORES and 2 * routes.shape[1] == EXTRA
        return (ring_device if dense and ringed else exchange_device)(*arguments)

    return jax.shard_map(
        on_device, mesh=mesh, in_specs=placed, out_specs=P(("groups", "ctx"), None), check_vma=False
    )
```

```python
import functools
import math

import jax
import jax.numpy as jnp
from jax import lax
from jax.experimental import pallas as pl
from jax.experimental.pallas import tpu as pltpu
from jax.sharding import PartitionSpec as P

D = 2048
HEAD_SIZE = 128
CORES = 2
EXTRA = 16
QUERY_SCALE = 0.125


NEG = -1e30


def ring_pairs(chips):
    order = list(range(0, chips, 2)) + list(range(chips - 1, 0, -2))
    onward = [
        (order[i] * CORES + core, order[(i + 1) % chips] * CORES + core)
        for i in range(chips)
        for core in range(CORES)
    ]
    back = [(b, a) for a, b in onward]
    swap = [(i, i ^ 1) for i in range(chips * CORES)]
    return onward, back, swap


def pack_kernel(pos_ref, key_ref, value_ref, routes_ref, combine_ref, out_ref):
    rows, width = key_ref.shape
    top = routes_ref.shape[0]
    out_ref[0:rows, 0:width] = key_ref[...]
    out_ref[0:rows, width : 2 * width] = value_ref[...]
    weight = combine_ref[...]
    high = weight.astype(jnp.bfloat16).astype(jnp.float32)
    low = weight - high
    names = routes_ref[...].astype(jnp.float32)
    place = jnp.full((EXTRA, 2 * width - 2 * rows), pos_ref[0].astype(jnp.float32), jnp.float32)
    tail = slice(rows, rows + EXTRA)
    out_ref[tail, 0:rows] = jnp.concatenate([names, high], axis=0).astype(jnp.bfloat16)
    out_ref[tail, rows : 2 * rows] = jnp.concatenate([low, jnp.zeros_like(low)], axis=0).astype(
        jnp.bfloat16
    )
    out_ref[tail, 2 * rows : 2 * width] = place.astype(jnp.bfloat16)


def pack_message(stretch_pos, keys, values, routes, combine):
    rows, width = keys.shape
    vmem = pl.BlockSpec(memory_space=pltpu.VMEM)
    return pl.pallas_call(
        pack_kernel,
        out_shape=jax.ShapeDtypeStruct((rows + EXTRA, 2 * width), jnp.bfloat16),
        in_specs=[pl.BlockSpec(memory_space=pltpu.SMEM), vmem, vmem, vmem, vmem],
        out_specs=vmem,
        name="pack_message",
    )(stretch_pos, keys, values, routes.T, combine.T)


def attend_kernel(count, half, begun, ended, *refs):
    refs = list(refs)

    def take(number):
        taken, refs[:number] = refs[:number], []
        return taken

    query_ref, own_ref = take(2)
    messages = take(count)
    if begun:
        begun_sums, begun_best = take(2)
    if ended:
        residual_ref, gain_ref, hidden_ref, normed_ref = take(4)
    else:
        sums_ref, best_ref = take(2)
    key_ext, value_ext = refs
    features = query_ref.shape[1]
    some = query_ref.shape[0] // 2
    mine = slice(half * some, (half + 1) * some)
    rows = messages[0].shape[0] - EXTRA
    kv_heads = key_ext.shape[0]
    heads = features // HEAD_SIZE
    group = heads // kv_heads
    span = count * rows
    width = kv_heads * HEAD_SIZE
    sub = lax.broadcasted_iota(jnp.int32, (rows, rows), 0)
    lane = lax.broadcasted_iota(jnp.int32, (rows, rows), 1)
    ahead = (sub - lane).astype(jnp.float32)
    own_pos = own_ref[rows : rows + EXTRA, 256 : 256 + rows][0:1].astype(jnp.float32)
    ones = jnp.ones((rows, HEAD_SIZE), jnp.bfloat16)
    for block in range(count):
        ref = messages[block]
        at = slice(block * rows, (block + 1) * rows)
        pos = ref[rows : rows + EXTRA, 256 : 256 + rows][0:1].astype(jnp.float32)
        later = (pos - own_pos) * float(rows) + ahead
        bias = jnp.where(later > 0.0, NEG, 0.0).astype(jnp.bfloat16)
        for a in range(kv_heads):
            key_ext[a, at, 0:HEAD_SIZE] = ref[0:rows, a * HEAD_SIZE : (a + 1) * HEAD_SIZE]
            key_ext[a, at, HEAD_SIZE : HEAD_SIZE + rows] = bias
            value_ext[a, at, 0:HEAD_SIZE] = ref[
                0:rows, width + a * HEAD_SIZE : width + (a + 1) * HEAD_SIZE
            ]
            value_ext[a, at, HEAD_SIZE : 2 * HEAD_SIZE] = ones
    eye = jnp.where(sub == lane, 1.0, 0.0).astype(jnp.bfloat16)[mine]
    rate = math.log2(math.e) / math.sqrt(HEAD_SIZE) / QUERY_SCALE
    step = min(512 if span % 512 == 0 else 256, span)
    pair = 4
    squares = jnp.zeros((some, HEAD_SIZE), jnp.float32)

    def scores_of(first):
        stacked = jnp.concatenate(
            [
                jnp.concatenate([query_ref[mine, h * HEAD_SIZE : (h + 1) * HEAD_SIZE], eye], axis=1)
                for h in range(first, first + pair)
            ],
            axis=0,
        )
        return [
            lax.dot_general(
                stacked,
                key_ext[first // group, at : at + step, :],
                (((1,), (1,)), ((), ())),
                preferred_element_type=jnp.float32,
            )
            for at in range(0, span, step)
        ]

    ready = scores_of(0)
    for first in range(0, heads, pair):
        a = first // group
        scores = ready
        if first + pair < heads:
            ready = scores_of(first + pair)
        best = functools.reduce(jnp.maximum, scores)
        best = jnp.max(best, axis=1, keepdims=True)
        total = None
        at = slice(first * some, (first + pair) * some)
        if begun:
            before = begun_best[at]
            best = jnp.maximum(best, before[:, 0:1])
            shrink = jnp.exp2((before - best) * rate)
            total = begun_sums[at] * jnp.concatenate([shrink, shrink], axis=1)
        for i, part in enumerate(scores):
            probs = jnp.exp2((part - best) * rate).astype(jnp.bfloat16)
            term = jnp.dot(
                probs,
                value_ext[a, i * step : (i + 1) * step, :],
                preferred_element_type=jnp.float32,
            )
            total = term if total is None else total + term
        if not ended:
            sums_ref[at] = total
            best_ref[at] = jnp.broadcast_to(best, (pair * some, HEAD_SIZE))
            continue
        attended = (total[:, 0:HEAD_SIZE] / total[:, HEAD_SIZE:]).astype(jnp.bfloat16)
        for j in range(pair):
            cols = slice((first + j) * HEAD_SIZE, (first + j + 1) * HEAD_SIZE)
            state = residual_ref[mine, cols] + attended[
                j * some : (j + 1) * some
            ].astype(jnp.float32)
            hidden_ref[:, cols] = state
            squares = squares + state * state
    if not ended:
        return
    meansq = jnp.sum(squares, axis=1, keepdims=True) / float(heads * HEAD_SIZE)
    inverse = lax.rsqrt(meansq + 1e-06)
    for h in range(heads):
        cols = slice(h * HEAD_SIZE, (h + 1) * HEAD_SIZE)
        normed_ref[:, cols] = (hidden_ref[:, cols] * inverse * gain_ref[0:1, cols]).astype(
            jnp.bfloat16
        )


def attend_call(half, begun, ended, queries, messages, inputs, out_shape):
    rows, features = queries.shape
    count = len(messages) - 1
    kv_heads = messages[0].shape[1] // (2 * HEAD_SIZE)
    vmem = pl.BlockSpec(memory_space=pltpu.VMEM)
    span = count * rows
    return pl.pallas_call(
        functools.partial(attend_kernel, count, half, begun, ended),
        out_shape=out_shape,
        in_specs=[vmem] * (1 + len(messages) + len(inputs)),
        out_specs=(vmem,) * len(out_shape),
        scratch_shapes=[
            pltpu.VMEM((kv_heads, span, 2 * HEAD_SIZE), jnp.bfloat16),
            pltpu.VMEM((kv_heads, span, 2 * HEAD_SIZE), jnp.bfloat16),
        ],
        compiler_params=pltpu.CompilerParams(vmem_limit_bytes=28 * 1024 * 1024),
        cost_estimate=pl.CostEstimate(
            flops=4 * rows * span * features, bytes_accessed=4 * 1024 * 1024, transcendentals=0
        ),
        name="attend",
    )(queries, *messages, *inputs)


def attend_start(half, queries, own, messages):
    rows, features = queries.shape
    lines = rows // 2 * (features // HEAD_SIZE)
    return attend_call(
        half,
        False,
        False,
        queries,
        [own] + messages,
        (),
        (
            jax.ShapeDtypeStruct((lines, 2 * HEAD_SIZE), jnp.float32),
            jax.ShapeDtypeStruct((lines, HEAD_SIZE), jnp.float32),
        ),
    )


def attend(half, staged, own, messages, begun=()):
    queries, residual, gain = staged
    rows, features = queries.shape
    return attend_call(
        half,
        len(begun) > 0,
        True,
        queries,
        [own] + messages,
        (*begun, residual, gain),
        (
            jax.ShapeDtypeStruct((rows // 2, features), jnp.float32),
            jax.ShapeDtypeStruct((rows // 2, features), jnp.bfloat16),
        ),
    )


def expert_kernel(places, count, *refs):
    pieces = len(places)
    tokens = refs[:pieces]
    messages = refs[pieces : pieces + count]
    weights = refs[pieces + count : pieces + count + 3 * CORES]
    outs = refs[pieces + count + 3 * CORES :]
    rows, features = tokens[0].shape
    whole = messages[0].shape[0] - EXTRA
    top = EXTRA // 2
    me = lax.axis_index("ctx")
    normed = jnp.concatenate([ref[...] for ref in tokens], axis=0)
    shares, acts = [], []
    for e in range(CORES):
        gate_ref, up_ref = weights[3 * e], weights[3 * e + 1]
        gate = jnp.dot(normed, gate_ref[0], preferred_element_type=jnp.float32)
        upper = jnp.dot(normed, up_ref[0], preferred_element_type=jnp.float32)
        acts.append((gate / (1.0 + jnp.exp(-gate)) * upper).astype(jnp.bfloat16))
        name = jnp.bitwise_xor(me, e).astype(jnp.float32)
        columns = []
        for ref in messages:
            extra = ref[whole : whole + EXTRA, 0 : 2 * whole].astype(jnp.float32)
            value = extra[top : 2 * top, 0:whole] + extra[0:top, whole : 2 * whole]
            hit = jnp.where(extra[0:top, 0:whole] == name, value, 0.0)
            line = jnp.sum(hit, axis=0, keepdims=True)
            columns.append(jnp.broadcast_to(line, (whole, whole)).T)
        shares.append([columns[m][half * rows : (half + 1) * rows] for m, half in places])
    step = 512
    for at in range(0, features, step):
        parts = [
            jnp.dot(acts[e], weights[3 * e + 2][0, :, at : at + step], preferred_element_type=jnp.float32)
            .astype(jnp.bfloat16)
            .astype(jnp.float32)
            for e in range(CORES)
        ]
        for b in range(pieces):
            for c in range(0, step, whole):
                mixed = sum(
                    shares[e][b] * parts[e][b * rows : (b + 1) * rows, c : c + whole]
                    for e in range(CORES)
                )
                outs[b][:, at + c : at + c + whole] = mixed.astype(jnp.bfloat16)


def run_experts(pieces, messages, weights):
    tokens = [piece[0] for piece in pieces]
    rows, features = tokens[0].shape
    hidden = weights[0].shape[2]
    vmem = pl.BlockSpec(memory_space=pltpu.VMEM)
    return pl.pallas_call(
        functools.partial(expert_kernel, [piece[1:] for piece in pieces], len(messages)),
        out_shape=[jax.ShapeDtypeStruct((rows, features), jnp.bfloat16)] * len(pieces),
        in_specs=[vmem] * (len(pieces) + len(messages) + len(weights)),
        out_specs=[vmem] * len(pieces),
        compiler_params=pltpu.CompilerParams(vmem_limit_bytes=24 * 1024 * 1024),
        cost_estimate=pl.CostEstimate(
            flops=12 * len(pieces) * rows * features * hidden,
            bytes_accessed=12 * features * hidden,
            transcendentals=0,
        ),
        name="experts",
    )(*tokens, *messages, *weights)


def add_parts(*parts):
    total = parts[0].astype(jnp.float32)
    for part in parts[1:]:
        total = total + part.astype(jnp.float32)
    return total.astype(jnp.bfloat16)


def ring_device(
    queries,
    rotated_keys,
    value_matrix,
    stretch_pos,
    residual,
    norm_gain,
    routes,
    combine,
    gate_weight,
    up_weight,
    down_weight,
):
    chips = lax.axis_size("ctx") // CORES
    far = chips // 2
    onward, back, swap = ring_pairs(chips)

    def send(array, pairs):
        return lax.ppermute(array, "ctx", pairs)

    message = pack_message(stretch_pos, rotated_keys, value_matrix, routes, combine)

    tie = lax.optimization_barrier
    left, right = {0: message}, {0: message}
    for hop in range(1, far + 1):
        if hop == 3:
            inputs, unused = tie(((queries, residual, norm_gain), (left[1], right[1])))
            staged = (
                inputs[0] * jnp.bfloat16(QUERY_SCALE),
                inputs[1].astype(jnp.float32),
                jnp.broadcast_to(inputs[2][None, :], (8, inputs[2].shape[0])),
            )
            left[2], staged = tie((left[2], staged))
        left[hop] = send(left[hop - 1], onward)
        if hop < far:
            right[hop] = send(right[hop - 1], back)
    plane = [message] + [left[h] for h in range(1, far + 1)] + [right[h] for h in range(1, far)]
    near = [message] + [left[h] for h in range(1, far)] + [right[h] for h in range(1, far)]
    near = near + [send(m, swap) for m in near]
    begun = attend_start(0, staged[0], message, near)
    left[far], begun = tie((left[far], begun))
    distant = [left[far], send(left[far], swap)]
    everything = near + distant
    everything, own_weights = tie((everything, (gate_weight, up_weight, down_weight)))
    twin_gate, twin_up, twin_down = [send(w, swap) for w in own_weights]
    hidden_upper, upper = attend(0, staged, message, everything[len(near) :], begun)
    everything, upper = tie((everything, upper))
    hidden_lower, lower = attend(1, staged, message, everything)
    lower, twin_gate, twin_up = tie((lower, twin_gate, twin_up))
    weights = (gate_weight, up_weight, down_weight, twin_gate, twin_up, twin_down)

    from_left, from_right = {(0, 0): upper, (0, 1): lower}, {(0, 0): upper, (0, 1): lower}
    outs = {}

    def later(array, than):
        return tie((array, than))[0]

    def experts_on(tokens, used, after):
        used, after = tie((used, after))
        return run_experts(tokens, used, weights), after

    def experts_of(hop, half, after):
        tokens = [(from_left[hop, half], 0, half), (from_right[hop, half], 1, half)]
        return experts_on(tokens, [left[hop], right[hop]], after)

    last = (upper, lower)
    for hop in range(1, far + 1):
        for half in range(2):
            onto, backto = from_left[hop - 1, half], from_right[hop - 1, half]
            if hop > 1:
                before = (hop - 1, 1 - half) if half == 1 else (hop - 2, 1)
                if before[0] > 0:
                    outs[before], unused = experts_of(*before, last)
                    last = outs[before]
                    onto, backto, last = tie((onto, backto, last))
                    outs[before] = last
            if hop < far or half == 0:
                from_left[hop, half] = send(onto, onward)
            if hop < far or half == 1:
                from_right[hop, half] = send(backto, back)
    outs[far - 1, 1], unused = experts_of(far - 1, 1, last)
    outs[far - 1, 0], outs[far - 1, 1] = tie((outs[far - 1, 0], outs[far - 1, 1]))
    out_left = {key: pair[0] for key, pair in outs.items()}
    out_right = {key: pair[1] for key, pair in outs.items()}

    sums_on = {1: send(out_right[far - 1, 1], onward)}
    sums_back = {0: send(out_left[far - 1, 0], back)}
    (far_upper, far_lower), unused = experts_on(
        [(from_left[far, 0], 0, 0), (from_right[far, 1], 0, 1)], [left[far]], outs[far - 1, 1]
    )
    sums_on[0] = send(far_upper, onward)
    sums_back[1] = send(far_lower, back)
    own_out, unused = experts_on(
        [(upper, 0, 0), (lower, 0, 1)], [message], (far_upper, far_lower, sums_on[1], sums_back[0])
    )
    for hop in range(far - 1, 0, -1):
        onto, backto = sums_on[0], sums_back[1]
        if hop < far - 1:
            sums_on[1] = later(sums_on[1], earlier[0])
            sums_back[0] = later(sums_back[0], earlier[1])
            sums_on[1] = send(add_parts(sums_on[1], out_right[hop, 1]), onward)
            sums_back[0] = send(add_parts(sums_back[0], out_left[hop, 0]), back)
        if hop == 1:
            onto, backto = later(onto, own_out), later(backto, own_out)
        earlier = (add_parts(onto, out_right[hop, 0]), add_parts(backto, out_left[hop, 1]))
        sums_on[0], sums_back[1] = send(earlier[0], onward), send(earlier[1], back)
    hidden_state = (hidden_upper, hidden_lower)
    return jnp.concatenate(
        [
            (
                hidden_state[half]
                + own_out[half].astype(jnp.float32)
                + sums_on[half].astype(jnp.float32)
                + sums_back[half].astype(jnp.float32)
            ).astype(jnp.bfloat16)
            for half in range(2)
        ],
        axis=0,
    )


def exchange_device(
    queries,
    rotated_keys,
    value_matrix,
    stretch_pos,
    residual,
    norm_gain,
    routes,
    combine,
    gate_weight,
    up_weight,
    down_weight,
):
    tok_rows = queries.shape[0]
    kv_heads = rotated_keys.shape[1] // HEAD_SIZE
    head_group = queries.shape[1] // rotated_keys.shape[1]
    ctx_count = lax.axis_size("ctx")
    positions = stretch_pos[0] * tok_rows + jnp.arange(tok_rows, dtype=jnp.int32)
    latest = jnp.max(positions)
    query_heads = queries.reshape(tok_rows, kv_heads, head_group, HEAD_SIZE)
    scale_factor = 1.0 / math.sqrt(HEAD_SIZE)

    def update(state, key_block, value_block, key_pos):
        best, total, accum = state
        scores = (
            jnp.einsum(
                "tagd,sad->agts",
                query_heads,
                key_block.reshape(-1, kv_heads, HEAD_SIZE),
                preferred_element_type=jnp.float32,
            )
            * scale_factor
        )
        scores = jnp.where(
            key_pos[None, None, None, :] <= positions[None, None, :, None], scores, jnp.float32(NEG)
        )
        fresh = jnp.maximum(best, jnp.max(scores, axis=-1))
        shrink = jnp.exp(best - fresh)
        expo = jnp.exp(scores - fresh[..., None])
        total = total * shrink + jnp.sum(expo, axis=-1)
        weighted = jnp.einsum(
            "agts,sad->agtd",
            expo.astype(jnp.bfloat16),
            value_block.reshape(-1, kv_heads, HEAD_SIZE),
            preferred_element_type=jnp.float32,
        )
        accum = accum * shrink[..., None] + weighted
        return (fresh, total, accum)

    start_state = (
        jnp.full((kv_heads, head_group, tok_rows), NEG, jnp.float32),
        jnp.zeros((kv_heads, head_group, tok_rows), jnp.float32),
        jnp.zeros((kv_heads, head_group, tok_rows, HEAD_SIZE), jnp.float32),
    )
    key_part = lax.all_gather(rotated_keys, "ctx", axis=0, tiled=True)
    value_part = lax.all_gather(value_matrix, "ctx", axis=0, tiled=True)
    pos_part = lax.all_gather(positions, "ctx", axis=0, tiled=True)
    span = key_part.shape[0]
    width = 512
    blocks = span // width
    stacked = (
        key_part.reshape(blocks, width, -1),
        value_part.reshape(blocks, width, -1),
        pos_part.reshape(blocks, width),
    )

    def advance(inner, item):
        key_block, value_block, key_pos = item
        result = lax.cond(
            jnp.min(key_pos) > latest,
            lambda kept: kept,
            lambda kept: update(kept, key_block, value_block, key_pos),
            inner,
        )
        return (result, None)

    final, unused = lax.scan(advance, start_state, stacked)
    best, total, accum = final
    attended = (
        jnp.transpose(accum / total[..., None], (2, 0, 1, 3))
        .reshape(tok_rows, -1)
        .astype(jnp.bfloat16)
    )
    hidden_state = residual.astype(jnp.float32) + attended.astype(jnp.float32)
    meansq = jnp.mean(hidden_state * hidden_state, axis=-1, keepdims=True)
    normed = (hidden_state * lax.rsqrt(meansq + 1e-06) * norm_gain).astype(jnp.bfloat16)
    local_experts = gate_weight.shape[0]
    total_experts = local_experts * ctx_count
    top_count = routes.shape[1]
    capacity = min(
        tok_rows,
        tok_rows * top_count // total_experts + max(1, tok_rows * top_count // (8 * total_experts)),
    )
    flat_routes = routes.reshape(-1)
    onehot = (flat_routes[:, None] == jnp.arange(total_experts, dtype=jnp.int32)[None, :]).astype(
        jnp.int32
    )
    earlier = jnp.cumsum(onehot, axis=0) - onehot
    ranking = jnp.sum(earlier * onehot, axis=1)
    slot_ids = flat_routes * capacity + ranking
    selector = jnp.any(
        slot_ids.reshape(tok_rows, top_count)[:, :, None]
        == jnp.arange(total_experts * capacity, dtype=jnp.int32)[None, None, :],
        axis=1,
    ).astype(jnp.bfloat16)
    outgoing = jnp.einsum("ts,td->sd", selector, normed, preferred_element_type=jnp.float32).astype(
        jnp.bfloat16
    )
    outgoing = outgoing.reshape(ctx_count, local_experts, capacity, D)
    incoming = lax.all_to_all(outgoing, "ctx", split_axis=0, concat_axis=0, tiled=True)
    gate = jnp.einsum("secd,edh->sech", incoming, gate_weight, preferred_element_type=jnp.float32)
    upper = jnp.einsum("secd,edh->sech", incoming, up_weight, preferred_element_type=jnp.float32)
    act = (jax.nn.silu(gate) * upper).astype(jnp.bfloat16)
    returned = lax.all_to_all(
        jnp.einsum("sech,ehd->secd", act, down_weight, preferred_element_type=jnp.float32).astype(
            jnp.bfloat16
        ),
        "ctx",
        split_axis=0,
        concat_axis=0,
        tiled=True,
    )
    flat_back = returned.reshape(total_experts * capacity, D)
    picked = jnp.take(flat_back, slot_ids, axis=0).reshape(tok_rows, top_count, D)
    mixture = jnp.sum(combine[:, :, None] * picked.astype(jnp.float32), axis=1)
    return (hidden_state + mixture).astype(jnp.bfloat16)


def solution(mesh):
    placed = (
        P(("groups", "ctx"), None),
        P(("groups", "ctx"), None),
        P(("groups", "ctx"), None),
        P(("groups", "ctx")),
        P(("groups", "ctx"), None),
        P(),
        P(("groups", "ctx"), None),
        P(("groups", "ctx"), None),
        P("ctx", None, None),
        P("ctx", None, None),
        P("ctx", None, None),
    )
    ctx_count = mesh.shape["ctx"]

    def on_device(*arguments):
        routes, gate_weight = arguments[6], arguments[8]
        dense = 4 * routes.shape[1] >= gate_weight.shape[0] * ctx_count
        ringed = gate_weight.shape[0] == 1 and ctx_count % (2 * CORES) == 0
        ringed = ringed and ctx_count >= 6 * CORES and 2 * routes.shape[1] == EXTRA
        return (ring_device if dense and ringed else exchange_device)(*arguments)

    return jax.shard_map(
        on_device, mesh=mesh, in_specs=placed, out_specs=P(("groups", "ctx"), None), check_vma=False
    )
```

```python
import functools
import math

import jax
import jax.numpy as jnp
from jax import lax
from jax.experimental import pallas as pl
from jax.experimental.pallas import tpu as pltpu
from jax.sharding import PartitionSpec as P

D = 2048
HEAD_SIZE = 128
CORES = 2
EXTRA = 16
QUERY_SCALE = 0.125


NEG = -1e30


def ring_pairs(chips):
    order = list(range(0, chips, 2)) + list(range(chips - 1, 0, -2))
    onward = [
        (order[i] * CORES + core, order[(i + 1) % chips] * CORES + core)
        for i in range(chips)
        for core in range(CORES)
    ]
    back = [(b, a) for a, b in onward]
    swap = [(i, i ^ 1) for i in range(chips * CORES)]
    return onward, back, swap


def pack_kernel(pos_ref, key_ref, value_ref, routes_ref, combine_ref, out_ref):
    rows, width = key_ref.shape
    top = routes_ref.shape[0]
    out_ref[0:rows, 0:width] = key_ref[...]
    out_ref[0:rows, width : 2 * width] = value_ref[...]
    weight = combine_ref[...]
    high = weight.astype(jnp.bfloat16).astype(jnp.float32)
    low = weight - high
    names = routes_ref[...].astype(jnp.float32)
    place = jnp.full((EXTRA, 2 * width - 2 * rows), pos_ref[0].astype(jnp.float32), jnp.float32)
    tail = slice(rows, rows + EXTRA)
    out_ref[tail, 0:rows] = jnp.concatenate([names, high], axis=0).astype(jnp.bfloat16)
    out_ref[tail, rows : 2 * rows] = jnp.concatenate([low, jnp.zeros_like(low)], axis=0).astype(
        jnp.bfloat16
    )
    out_ref[tail, 2 * rows : 2 * width] = place.astype(jnp.bfloat16)


def pack_message(stretch_pos, keys, values, routes, combine):
    rows, width = keys.shape
    vmem = pl.BlockSpec(memory_space=pltpu.VMEM)
    return pl.pallas_call(
        pack_kernel,
        out_shape=jax.ShapeDtypeStruct((rows + EXTRA, 2 * width), jnp.bfloat16),
        in_specs=[pl.BlockSpec(memory_space=pltpu.SMEM), vmem, vmem, vmem, vmem],
        out_specs=vmem,
        name="pack_message",
    )(stretch_pos, keys, values, routes.T, combine.T)


def attend_kernel(count, half, begun, ended, *refs):
    refs = list(refs)

    def take(number):
        taken, refs[:number] = refs[:number], []
        return taken

    query_ref, own_ref = take(2)
    messages = take(count)
    if begun:
        begun_sums, begun_best = take(2)
    if ended:
        residual_ref, gain_ref, hidden_ref, normed_ref = take(4)
    else:
        sums_ref, best_ref = take(2)
    key_ext, value_ext = refs
    features = query_ref.shape[1]
    some = query_ref.shape[0] // 2
    mine = slice(half * some, (half + 1) * some)
    rows = messages[0].shape[0] - EXTRA
    kv_heads = key_ext.shape[0]
    heads = features // HEAD_SIZE
    group = heads // kv_heads
    span = count * rows
    width = kv_heads * HEAD_SIZE
    sub = lax.broadcasted_iota(jnp.int32, (rows, rows), 0)
    lane = lax.broadcasted_iota(jnp.int32, (rows, rows), 1)
    ahead = (sub - lane).astype(jnp.float32)
    own_pos = own_ref[rows : rows + EXTRA, 256 : 256 + rows][0:1].astype(jnp.float32)
    ones = jnp.ones((rows, HEAD_SIZE), jnp.bfloat16)
    for block in range(count):
        ref = messages[block]
        at = slice(block * rows, (block + 1) * rows)
        pos = ref[rows : rows + EXTRA, 256 : 256 + rows][0:1].astype(jnp.float32)
        later = (pos - own_pos) * float(rows) + ahead
        bias = jnp.where(later > 0.0, NEG, 0.0).astype(jnp.bfloat16)
        for a in range(kv_heads):
            key_ext[a, at, 0:HEAD_SIZE] = ref[0:rows, a * HEAD_SIZE : (a + 1) * HEAD_SIZE]
            key_ext[a, at, HEAD_SIZE : HEAD_SIZE + rows] = bias
            value_ext[a, at, 0:HEAD_SIZE] = ref[
                0:rows, width + a * HEAD_SIZE : width + (a + 1) * HEAD_SIZE
            ]
            value_ext[a, at, HEAD_SIZE : 2 * HEAD_SIZE] = ones
    eye = jnp.where(sub == lane, 1.0, 0.0).astype(jnp.bfloat16)[mine]
    rate = math.log2(math.e) / math.sqrt(HEAD_SIZE) / QUERY_SCALE
    step = min(512 if span % 512 == 0 else 256, span)
    pair = 4
    squares = jnp.zeros((some, HEAD_SIZE), jnp.float32)

    def scores_of(first):
        stacked = jnp.concatenate(
            [
                jnp.concatenate([query_ref[mine, h * HEAD_SIZE : (h + 1) * HEAD_SIZE], eye], axis=1)
                for h in range(first, first + pair)
            ],
            axis=0,
        )
        return [
            lax.dot_general(
                stacked,
                key_ext[first // group, at : at + step, :],
                (((1,), (1,)), ((), ())),
                preferred_element_type=jnp.float32,
            )
            for at in range(0, span, step)
        ]

    ready = scores_of(0)
    for first in range(0, heads, pair):
        a = first // group
        scores = ready
        if first + pair < heads:
            ready = scores_of(first + pair)
        best = functools.reduce(jnp.maximum, scores)
        best = jnp.max(best, axis=1, keepdims=True)
        total = None
        at = slice(first * some, (first + pair) * some)
        if begun:
            before = begun_best[at]
            best = jnp.maximum(best, before[:, 0:1])
            shrink = jnp.exp2((before - best) * rate)
            total = begun_sums[at] * jnp.concatenate([shrink, shrink], axis=1)
        for i, part in enumerate(scores):
            probs = jnp.exp2((part - best) * rate).astype(jnp.bfloat16)
            term = jnp.dot(
                probs,
                value_ext[a, i * step : (i + 1) * step, :],
                preferred_element_type=jnp.float32,
            )
            total = term if total is None else total + term
        if not ended:
            sums_ref[at] = total
            best_ref[at] = jnp.broadcast_to(best, (pair * some, HEAD_SIZE))
            continue
        attended = (total[:, 0:HEAD_SIZE] / total[:, HEAD_SIZE:]).astype(jnp.bfloat16)
        for j in range(pair):
            cols = slice((first + j) * HEAD_SIZE, (first + j + 1) * HEAD_SIZE)
            state = residual_ref[mine, cols] + attended[
                j * some : (j + 1) * some
            ].astype(jnp.float32)
            hidden_ref[:, cols] = state
            squares = squares + state * state
    if not ended:
        return
    meansq = jnp.sum(squares, axis=1, keepdims=True) / float(heads * HEAD_SIZE)
    inverse = lax.rsqrt(meansq + 1e-06)
    for h in range(heads):
        cols = slice(h * HEAD_SIZE, (h + 1) * HEAD_SIZE)
        normed_ref[:, cols] = (hidden_ref[:, cols] * inverse * gain_ref[0:1, cols]).astype(
            jnp.bfloat16
        )


def attend_call(half, begun, ended, queries, messages, inputs, out_shape):
    rows, features = queries.shape
    count = len(messages) - 1
    kv_heads = messages[0].shape[1] // (2 * HEAD_SIZE)
    vmem = pl.BlockSpec(memory_space=pltpu.VMEM)
    span = count * rows
    return pl.pallas_call(
        functools.partial(attend_kernel, count, half, begun, ended),
        out_shape=out_shape,
        in_specs=[vmem] * (1 + len(messages) + len(inputs)),
        out_specs=(vmem,) * len(out_shape),
        scratch_shapes=[
            pltpu.VMEM((kv_heads, span, 2 * HEAD_SIZE), jnp.bfloat16),
            pltpu.VMEM((kv_heads, span, 2 * HEAD_SIZE), jnp.bfloat16),
        ],
        compiler_params=pltpu.CompilerParams(vmem_limit_bytes=28 * 1024 * 1024),
        cost_estimate=pl.CostEstimate(
            flops=4 * rows * span * features if ended else 0,
            bytes_accessed=4 * 1024 * 1024 if ended else 1024,
            transcendentals=0,
        ),
        name="attend",
    )(queries, *messages, *inputs)


def attend_start(half, queries, own, messages):
    rows, features = queries.shape
    lines = rows // 2 * (features // HEAD_SIZE)
    return attend_call(
        half,
        False,
        False,
        queries,
        [own] + messages,
        (),
        (
            jax.ShapeDtypeStruct((lines, 2 * HEAD_SIZE), jnp.float32),
            jax.ShapeDtypeStruct((lines, HEAD_SIZE), jnp.float32),
        ),
    )


def attend(half, staged, own, messages, begun=()):
    queries, residual, gain = staged
    rows, features = queries.shape
    return attend_call(
        half,
        len(begun) > 0,
        True,
        queries,
        [own] + messages,
        (*begun, residual, gain),
        (
            jax.ShapeDtypeStruct((rows // 2, features), jnp.float32),
            jax.ShapeDtypeStruct((rows // 2, features), jnp.bfloat16),
        ),
    )


def expert_kernel(places, count, *refs):
    pieces = len(places)
    tokens = refs[:pieces]
    messages = refs[pieces : pieces + count]
    weights = refs[pieces + count : pieces + count + 3 * CORES]
    outs = refs[pieces + count + 3 * CORES :]
    rows, features = tokens[0].shape
    whole = messages[0].shape[0] - EXTRA
    top = EXTRA // 2
    me = lax.axis_index("ctx")
    normed = jnp.concatenate([ref[...] for ref in tokens], axis=0)
    shares, acts = [], []
    for e in range(CORES):
        gate_ref, up_ref = weights[3 * e], weights[3 * e + 1]
        gate = jnp.dot(normed, gate_ref[0], preferred_element_type=jnp.float32)
        upper = jnp.dot(normed, up_ref[0], preferred_element_type=jnp.float32)
        acts.append((gate / (1.0 + jnp.exp(-gate)) * upper).astype(jnp.bfloat16))
        name = jnp.bitwise_xor(me, e).astype(jnp.float32)
        columns = []
        for ref in messages:
            extra = ref[whole : whole + EXTRA, 0 : 2 * whole].astype(jnp.float32)
            value = extra[top : 2 * top, 0:whole] + extra[0:top, whole : 2 * whole]
            hit = jnp.where(extra[0:top, 0:whole] == name, value, 0.0)
            line = jnp.sum(hit, axis=0, keepdims=True)
            columns.append(jnp.broadcast_to(line, (whole, whole)).T)
        shares.append([columns[m][half * rows : (half + 1) * rows] for m, half in places])
    step = 512
    for at in range(0, features, step):
        parts = [
            jnp.dot(acts[e], weights[3 * e + 2][0, :, at : at + step], preferred_element_type=jnp.float32)
            .astype(jnp.bfloat16)
            .astype(jnp.float32)
            for e in range(CORES)
        ]
        for b in range(pieces):
            for c in range(0, step, whole):
                mixed = sum(
                    shares[e][b] * parts[e][b * rows : (b + 1) * rows, c : c + whole]
                    for e in range(CORES)
                )
                outs[b][:, at + c : at + c + whole] = mixed.astype(jnp.bfloat16)


def run_experts(pieces, messages, weights):
    tokens = [piece[0] for piece in pieces]
    rows, features = tokens[0].shape
    hidden = weights[0].shape[2]
    vmem = pl.BlockSpec(memory_space=pltpu.VMEM)
    return pl.pallas_call(
        functools.partial(expert_kernel, [piece[1:] for piece in pieces], len(messages)),
        out_shape=[jax.ShapeDtypeStruct((rows, features), jnp.bfloat16)] * len(pieces),
        in_specs=[vmem] * (len(pieces) + len(messages) + len(weights)),
        out_specs=[vmem] * len(pieces),
        compiler_params=pltpu.CompilerParams(vmem_limit_bytes=24 * 1024 * 1024),
        cost_estimate=pl.CostEstimate(
            flops=12 * len(pieces) * rows * features * hidden,
            bytes_accessed=12 * features * hidden,
            transcendentals=0,
        ),
        name="experts",
    )(*tokens, *messages, *weights)


def add_parts(*parts):
    total = parts[0].astype(jnp.float32)
    for part in parts[1:]:
        total = total + part.astype(jnp.float32)
    return total.astype(jnp.bfloat16)


def ring_device(
    queries,
    rotated_keys,
    value_matrix,
    stretch_pos,
    residual,
    norm_gain,
    routes,
    combine,
    gate_weight,
    up_weight,
    down_weight,
):
    chips = lax.axis_size("ctx") // CORES
    far = chips // 2
    onward, back, swap = ring_pairs(chips)

    def send(array, pairs):
        return lax.ppermute(array, "ctx", pairs)

    message = pack_message(stretch_pos, rotated_keys, value_matrix, routes, combine)

    tie = lax.optimization_barrier
    left, right = {0: message}, {0: message}
    for hop in range(1, far + 1):
        if hop == 3:
            inputs, unused = tie(((queries, residual, norm_gain), (left[1], right[1])))
            staged = (
                inputs[0] * jnp.bfloat16(QUERY_SCALE),
                inputs[1].astype(jnp.float32),
                jnp.broadcast_to(inputs[2][None, :], (8, inputs[2].shape[0])),
            )
            left[2], staged = tie((left[2], staged))
        left[hop] = send(left[hop - 1], onward)
        if hop < far:
            right[hop] = send(right[hop - 1], back)
    plane = [message] + [left[h] for h in range(1, far + 1)] + [right[h] for h in range(1, far)]
    near = [message] + [left[h] for h in range(1, far)] + [right[h] for h in range(1, far)]
    last = [left[far - 1], right[far - 1]]
    near = near + [send(m, swap) for m in near if all(m is not other for other in last)]
    begun = attend_start(0, staged[0], message, near)
    left[far], begun = tie((left[far], begun))
    distant = [left[far]] + [send(m, swap) for m in [*last, left[far]]]
    everything = near + distant
    everything, own_weights = tie((everything, (gate_weight, up_weight, down_weight)))
    twin_gate, twin_up, twin_down = [send(w, swap) for w in own_weights]
    hidden_upper, upper = attend(0, staged, message, everything[len(near) :], begun)
    everything, upper = tie((everything, upper))
    hidden_lower, lower = attend(1, staged, message, everything)
    lower, twin_gate, twin_up = tie((lower, twin_gate, twin_up))
    weights = (gate_weight, up_weight, down_weight, twin_gate, twin_up, twin_down)

    from_left, from_right = {(0, 0): upper, (0, 1): lower}, {(0, 0): upper, (0, 1): lower}
    outs = {}

    def later(array, than):
        return tie((array, than))[0]

    def experts_on(tokens, used, after):
        used, after = tie((used, after))
        return run_experts(tokens, used, weights), after

    def experts_of(hop, half, after):
        tokens = [(from_left[hop, half], 0, half), (from_right[hop, half], 1, half)]
        return experts_on(tokens, [left[hop], right[hop]], after)

    last = (upper, lower)
    for hop in range(1, far + 1):
        for half in range(2):
            onto, backto = from_left[hop - 1, half], from_right[hop - 1, half]
            if hop > 1:
                before = (hop - 1, 1 - half) if half == 1 else (hop - 2, 1)
                if before[0] > 0:
                    outs[before], unused = experts_of(*before, last)
                    last = outs[before]
                    onto, backto, last = tie((onto, backto, last))
                    outs[before] = last
            if hop < far or half == 0:
                from_left[hop, half] = send(onto, onward)
            if hop < far or half == 1:
                from_right[hop, half] = send(backto, back)
    outs[far - 1, 1], unused = experts_of(far - 1, 1, last)
    outs[far - 1, 0], outs[far - 1, 1] = tie((outs[far - 1, 0], outs[far - 1, 1]))
    out_left = {key: pair[0] for key, pair in outs.items()}
    out_right = {key: pair[1] for key, pair in outs.items()}

    sums_on = {1: send(out_right[far - 1, 1], onward)}
    sums_back = {0: send(out_left[far - 1, 0], back)}
    (far_upper, far_lower), unused = experts_on(
        [(from_left[far, 0], 0, 0), (from_right[far, 1], 0, 1)], [left[far]], outs[far - 1, 1]
    )
    sums_on[0] = send(far_upper, onward)
    sums_back[1] = send(far_lower, back)
    own_out, unused = experts_on(
        [(upper, 0, 0), (lower, 0, 1)], [message], (far_upper, far_lower, sums_on[1], sums_back[0])
    )
    for hop in range(far - 1, 0, -1):
        onto, backto = sums_on[0], sums_back[1]
        if hop < far - 1:
            sums_on[1] = later(sums_on[1], earlier[0])
            sums_back[0] = later(sums_back[0], earlier[1])
            sums_on[1] = send(add_parts(sums_on[1], out_right[hop, 1]), onward)
            sums_back[0] = send(add_parts(sums_back[0], out_left[hop, 0]), back)
        if hop == 1:
            onto, backto = later(onto, own_out), later(backto, own_out)
        earlier = (add_parts(onto, out_right[hop, 0]), add_parts(backto, out_left[hop, 1]))
        sums_on[0], sums_back[1] = send(earlier[0], onward), send(earlier[1], back)
    hidden_state = (hidden_upper, hidden_lower)
    return jnp.concatenate(
        [
            (
                hidden_state[half]
                + own_out[half].astype(jnp.float32)
                + sums_on[half].astype(jnp.float32)
                + sums_back[half].astype(jnp.float32)
            ).astype(jnp.bfloat16)
            for half in range(2)
        ],
        axis=0,
    )


def exchange_device(
    queries,
    rotated_keys,
    value_matrix,
    stretch_pos,
    residual,
    norm_gain,
    routes,
    combine,
    gate_weight,
    up_weight,
    down_weight,
):
    tok_rows = queries.shape[0]
    kv_heads = rotated_keys.shape[1] // HEAD_SIZE
    head_group = queries.shape[1] // rotated_keys.shape[1]
    ctx_count = lax.axis_size("ctx")
    positions = stretch_pos[0] * tok_rows + jnp.arange(tok_rows, dtype=jnp.int32)
    latest = jnp.max(positions)
    query_heads = queries.reshape(tok_rows, kv_heads, head_group, HEAD_SIZE)
    scale_factor = 1.0 / math.sqrt(HEAD_SIZE)

    def update(state, key_block, value_block, key_pos):
        best, total, accum = state
        scores = (
            jnp.einsum(
                "tagd,sad->agts",
                query_heads,
                key_block.reshape(-1, kv_heads, HEAD_SIZE),
                preferred_element_type=jnp.float32,
            )
            * scale_factor
        )
        scores = jnp.where(
            key_pos[None, None, None, :] <= positions[None, None, :, None], scores, jnp.float32(NEG)
        )
        fresh = jnp.maximum(best, jnp.max(scores, axis=-1))
        shrink = jnp.exp(best - fresh)
        expo = jnp.exp(scores - fresh[..., None])
        total = total * shrink + jnp.sum(expo, axis=-1)
        weighted = jnp.einsum(
            "agts,sad->agtd",
            expo.astype(jnp.bfloat16),
            value_block.reshape(-1, kv_heads, HEAD_SIZE),
            preferred_element_type=jnp.float32,
        )
        accum = accum * shrink[..., None] + weighted
        return (fresh, total, accum)

    start_state = (
        jnp.full((kv_heads, head_group, tok_rows), NEG, jnp.float32),
        jnp.zeros((kv_heads, head_group, tok_rows), jnp.float32),
        jnp.zeros((kv_heads, head_group, tok_rows, HEAD_SIZE), jnp.float32),
    )
    key_part = lax.all_gather(rotated_keys, "ctx", axis=0, tiled=True)
    value_part = lax.all_gather(value_matrix, "ctx", axis=0, tiled=True)
    pos_part = lax.all_gather(positions, "ctx", axis=0, tiled=True)
    span = key_part.shape[0]
    width = 512
    blocks = span // width
    stacked = (
        key_part.reshape(blocks, width, -1),
        value_part.reshape(blocks, width, -1),
        pos_part.reshape(blocks, width),
    )

    def advance(inner, item):
        key_block, value_block, key_pos = item
        result = lax.cond(
            jnp.min(key_pos) > latest,
            lambda kept: kept,
            lambda kept: update(kept, key_block, value_block, key_pos),
            inner,
        )
        return (result, None)

    final, unused = lax.scan(advance, start_state, stacked)
    best, total, accum = final
    attended = (
        jnp.transpose(accum / total[..., None], (2, 0, 1, 3))
        .reshape(tok_rows, -1)
        .astype(jnp.bfloat16)
    )
    hidden_state = residual.astype(jnp.float32) + attended.astype(jnp.float32)
    meansq = jnp.mean(hidden_state * hidden_state, axis=-1, keepdims=True)
    normed = (hidden_state * lax.rsqrt(meansq + 1e-06) * norm_gain).astype(jnp.bfloat16)
    local_experts = gate_weight.shape[0]
    total_experts = local_experts * ctx_count
    top_count = routes.shape[1]
    capacity = min(
        tok_rows,
        tok_rows * top_count // total_experts + max(1, tok_rows * top_count // (8 * total_experts)),
    )
    flat_routes = routes.reshape(-1)
    onehot = (flat_routes[:, None] == jnp.arange(total_experts, dtype=jnp.int32)[None, :]).astype(
        jnp.int32
    )
    earlier = jnp.cumsum(onehot, axis=0) - onehot
    ranking = jnp.sum(earlier * onehot, axis=1)
    slot_ids = flat_routes * capacity + ranking
    selector = jnp.any(
        slot_ids.reshape(tok_rows, top_count)[:, :, None]
        == jnp.arange(total_experts * capacity, dtype=jnp.int32)[None, None, :],
        axis=1,
    ).astype(jnp.bfloat16)
    outgoing = jnp.einsum("ts,td->sd", selector, normed, preferred_element_type=jnp.float32).astype(
        jnp.bfloat16
    )
    outgoing = outgoing.reshape(ctx_count, local_experts, capacity, D)
    incoming = lax.all_to_all(outgoing, "ctx", split_axis=0, concat_axis=0, tiled=True)
    gate = jnp.einsum("secd,edh->sech", incoming, gate_weight, preferred_element_type=jnp.float32)
    upper = jnp.einsum("secd,edh->sech", incoming, up_weight, preferred_element_type=jnp.float32)
    act = (jax.nn.silu(gate) * upper).astype(jnp.bfloat16)
    returned = lax.all_to_all(
        jnp.einsum("sech,ehd->secd", act, down_weight, preferred_element_type=jnp.float32).astype(
            jnp.bfloat16
        ),
        "ctx",
        split_axis=0,
        concat_axis=0,
        tiled=True,
    )
    flat_back = returned.reshape(total_experts * capacity, D)
    picked = jnp.take(flat_back, slot_ids, axis=0).reshape(tok_rows, top_count, D)
    mixture = jnp.sum(combine[:, :, None] * picked.astype(jnp.float32), axis=1)
    return (hidden_state + mixture).astype(jnp.bfloat16)


def solution(mesh):
    placed = (
        P(("groups", "ctx"), None),
        P(("groups", "ctx"), None),
        P(("groups", "ctx"), None),
        P(("groups", "ctx")),
        P(("groups", "ctx"), None),
        P(),
        P(("groups", "ctx"), None),
        P(("groups", "ctx"), None),
        P("ctx", None, None),
        P("ctx", None, None),
        P("ctx", None, None),
    )
    ctx_count = mesh.shape["ctx"]

    def on_device(*arguments):
        routes, gate_weight = arguments[6], arguments[8]
        dense = 4 * routes.shape[1] >= gate_weight.shape[0] * ctx_count
        ringed = gate_weight.shape[0] == 1 and ctx_count % (2 * CORES) == 0
        ringed = ringed and ctx_count >= 6 * CORES and 2 * routes.shape[1] == EXTRA
        return (ring_device if dense and ringed else exchange_device)(*arguments)

    return jax.shard_map(
        on_device, mesh=mesh, in_specs=placed, out_specs=P(("groups", "ctx"), None), check_vma=False
    )
```

```python
import functools
import math

import jax
import jax.numpy as jnp
from jax import lax
from jax.experimental import pallas as pl
from jax.experimental.pallas import tpu as pltpu
from jax.sharding import PartitionSpec as P

D = 2048
HEAD_SIZE = 128
CORES = 2
EXTRA = 16
QUERY_SCALE = 0.125


NEG = -1e30


def ring_pairs(chips):
    order = list(range(0, chips, 2)) + list(range(chips - 1, 0, -2))
    onward = [
        (order[i] * CORES + core, order[(i + 1) % chips] * CORES + core)
        for i in range(chips)
        for core in range(CORES)
    ]
    back = [(b, a) for a, b in onward]
    swap = [(i, i ^ 1) for i in range(chips * CORES)]
    return onward, back, swap


def pack_kernel(pos_ref, key_ref, value_ref, routes_ref, combine_ref, out_ref):
    rows, width = key_ref.shape
    top = routes_ref.shape[0]
    out_ref[0:rows, 0:width] = key_ref[...]
    out_ref[0:rows, width : 2 * width] = value_ref[...]
    weight = combine_ref[...]
    high = weight.astype(jnp.bfloat16).astype(jnp.float32)
    low = weight - high
    names = routes_ref[...].astype(jnp.float32)
    place = jnp.full((EXTRA, 2 * width - 2 * rows), pos_ref[0].astype(jnp.float32), jnp.float32)
    tail = slice(rows, rows + EXTRA)
    out_ref[tail, 0:rows] = jnp.concatenate([names, high], axis=0).astype(jnp.bfloat16)
    out_ref[tail, rows : 2 * rows] = jnp.concatenate([low, jnp.zeros_like(low)], axis=0).astype(
        jnp.bfloat16
    )
    out_ref[tail, 2 * rows : 2 * width] = place.astype(jnp.bfloat16)


def pack_message(stretch_pos, keys, values, routes, combine):
    rows, width = keys.shape
    vmem = pl.BlockSpec(memory_space=pltpu.VMEM)
    return pl.pallas_call(
        pack_kernel,
        out_shape=jax.ShapeDtypeStruct((rows + EXTRA, 2 * width), jnp.bfloat16),
        in_specs=[pl.BlockSpec(memory_space=pltpu.SMEM), vmem, vmem, vmem, vmem],
        out_specs=vmem,
        name="pack_message",
    )(stretch_pos, keys, values, routes.T, combine.T)


def attend_kernel(count, half, begun, ended, *refs):
    refs = list(refs)

    def take(number):
        taken, refs[:number] = refs[:number], []
        return taken

    query_ref, own_ref = take(2)
    messages = take(count)
    if begun:
        begun_sums, begun_best = take(2)
    if ended:
        residual_ref, gain_ref, hidden_ref, normed_ref = take(4)
    else:
        sums_ref, best_ref = take(2)
    key_ext, value_ext = refs
    features = query_ref.shape[1]
    some = query_ref.shape[0] // 2
    mine = slice(half * some, (half + 1) * some)
    rows = messages[0].shape[0] - EXTRA
    kv_heads = key_ext.shape[0]
    heads = features // HEAD_SIZE
    group = heads // kv_heads
    span = count * rows
    width = kv_heads * HEAD_SIZE
    sub = lax.broadcasted_iota(jnp.int32, (rows, rows), 0)
    lane = lax.broadcasted_iota(jnp.int32, (rows, rows), 1)
    ahead = (sub - lane).astype(jnp.float32)
    own_pos = own_ref[rows : rows + EXTRA, 256 : 256 + rows][0:1].astype(jnp.float32)
    ones = jnp.ones((rows, HEAD_SIZE), jnp.bfloat16)
    for block in range(count):
        ref = messages[block]
        at = slice(block * rows, (block + 1) * rows)
        pos = ref[rows : rows + EXTRA, 256 : 256 + rows][0:1].astype(jnp.float32)
        later = (pos - own_pos) * float(rows) + ahead
        bias = jnp.where(later > 0.0, NEG, 0.0).astype(jnp.bfloat16)
        for a in range(kv_heads):
            key_ext[a, at, 0:HEAD_SIZE] = ref[0:rows, a * HEAD_SIZE : (a + 1) * HEAD_SIZE]
            key_ext[a, at, HEAD_SIZE : HEAD_SIZE + rows] = bias
            value_ext[a, at, 0:HEAD_SIZE] = ref[
                0:rows, width + a * HEAD_SIZE : width + (a + 1) * HEAD_SIZE
            ]
            value_ext[a, at, HEAD_SIZE : 2 * HEAD_SIZE] = ones
    eye = jnp.where(sub == lane, 1.0, 0.0).astype(jnp.bfloat16)[mine]
    rate = math.log2(math.e) / math.sqrt(HEAD_SIZE) / QUERY_SCALE
    step = min(512 if span % 512 == 0 else 256, span)
    pair = 4
    squares = jnp.zeros((some, HEAD_SIZE), jnp.float32)

    def scores_of(first):
        stacked = jnp.concatenate(
            [
                jnp.concatenate([query_ref[mine, h * HEAD_SIZE : (h + 1) * HEAD_SIZE], eye], axis=1)
                for h in range(first, first + pair)
            ],
            axis=0,
        )
        return [
            lax.dot_general(
                stacked,
                key_ext[first // group, at : at + step, :],
                (((1,), (1,)), ((), ())),
                preferred_element_type=jnp.float32,
            )
            for at in range(0, span, step)
        ]

    ready = scores_of(0)
    for first in range(0, heads, pair):
        a = first // group
        scores = ready
        if first + pair < heads:
            ready = scores_of(first + pair)
        best = functools.reduce(jnp.maximum, scores)
        best = jnp.max(best, axis=1, keepdims=True)
        total = None
        at = slice(first * some, (first + pair) * some)
        if begun:
            before = begun_best[at]
            best = jnp.maximum(best, before[:, 0:1])
            shrink = jnp.exp2((before - best) * rate)
            total = begun_sums[at] * jnp.concatenate([shrink, shrink], axis=1)
        for i, part in enumerate(scores):
            probs = jnp.exp2((part - best) * rate).astype(jnp.bfloat16)
            term = jnp.dot(
                probs,
                value_ext[a, i * step : (i + 1) * step, :],
                preferred_element_type=jnp.float32,
            )
            total = term if total is None else total + term
        if not ended:
            sums_ref[at] = total
            best_ref[at] = jnp.broadcast_to(best, (pair * some, HEAD_SIZE))
            continue
        attended = (total[:, 0:HEAD_SIZE] / total[:, HEAD_SIZE:]).astype(jnp.bfloat16)
        for j in range(pair):
            cols = slice((first + j) * HEAD_SIZE, (first + j + 1) * HEAD_SIZE)
            state = residual_ref[mine, cols] + attended[
                j * some : (j + 1) * some
            ].astype(jnp.float32)
            hidden_ref[:, cols] = state
            squares = squares + state * state
    if not ended:
        return
    meansq = jnp.sum(squares, axis=1, keepdims=True) / float(heads * HEAD_SIZE)
    inverse = lax.rsqrt(meansq + 1e-06)
    for h in range(heads):
        cols = slice(h * HEAD_SIZE, (h + 1) * HEAD_SIZE)
        normed_ref[:, cols] = (hidden_ref[:, cols] * inverse * gain_ref[0:1, cols]).astype(
            jnp.bfloat16
        )


def attend_call(half, begun, ended, queries, messages, inputs, out_shape):
    rows, features = queries.shape
    count = len(messages) - 1
    kv_heads = messages[0].shape[1] // (2 * HEAD_SIZE)
    vmem = pl.BlockSpec(memory_space=pltpu.VMEM)
    span = count * rows
    return pl.pallas_call(
        functools.partial(attend_kernel, count, half, begun, ended),
        out_shape=out_shape,
        in_specs=[vmem] * (1 + len(messages) + len(inputs)),
        out_specs=(vmem,) * len(out_shape),
        scratch_shapes=[
            pltpu.VMEM((kv_heads, span, 2 * HEAD_SIZE), jnp.bfloat16),
            pltpu.VMEM((kv_heads, span, 2 * HEAD_SIZE), jnp.bfloat16),
        ],
        compiler_params=pltpu.CompilerParams(vmem_limit_bytes=28 * 1024 * 1024),
        cost_estimate=pl.CostEstimate(
            flops=4 * rows * span * features if ended else 0,
            bytes_accessed=4 * 1024 * 1024 if ended else 1024,
            transcendentals=0,
        ),
        name="attend",
    )(queries, *messages, *inputs)


def attend_start(half, queries, own, messages):
    rows, features = queries.shape
    lines = rows // 2 * (features // HEAD_SIZE)
    return attend_call(
        half,
        False,
        False,
        queries,
        [own] + messages,
        (),
        (
            jax.ShapeDtypeStruct((lines, 2 * HEAD_SIZE), jnp.float32),
            jax.ShapeDtypeStruct((lines, HEAD_SIZE), jnp.float32),
        ),
    )


def attend(half, staged, own, messages, begun=()):
    queries, residual, gain = staged
    rows, features = queries.shape
    return attend_call(
        half,
        len(begun) > 0,
        True,
        queries,
        [own] + messages,
        (*begun, residual, gain),
        (
            jax.ShapeDtypeStruct((rows // 2, features), jnp.float32),
            jax.ShapeDtypeStruct((rows // 2, features), jnp.bfloat16),
        ),
    )


def expert_kernel(places, count, *refs):
    pieces = len(places)
    tokens = refs[:pieces]
    messages = refs[pieces : pieces + count]
    weights = refs[pieces + count : pieces + count + 3 * CORES]
    outs = refs[pieces + count + 3 * CORES :]
    rows, features = tokens[0].shape
    whole = messages[0].shape[0] - EXTRA
    top = EXTRA // 2
    me = lax.axis_index("ctx")
    normed = jnp.concatenate([ref[...] for ref in tokens], axis=0)
    shares, acts = [], []
    for e in range(CORES):
        gate_ref, up_ref = weights[3 * e], weights[3 * e + 1]
        gate = jnp.dot(normed, gate_ref[0], preferred_element_type=jnp.float32)
        upper = jnp.dot(normed, up_ref[0], preferred_element_type=jnp.float32)
        acts.append((gate / (1.0 + jnp.exp(-gate)) * upper).astype(jnp.bfloat16))
        name = jnp.bitwise_xor(me, e).astype(jnp.float32)
        columns = []
        for ref in messages:
            extra = ref[whole : whole + EXTRA, 0 : 2 * whole].astype(jnp.float32)
            value = extra[top : 2 * top, 0:whole] + extra[0:top, whole : 2 * whole]
            hit = jnp.where(extra[0:top, 0:whole] == name, value, 0.0)
            line = jnp.sum(hit, axis=0, keepdims=True)
            columns.append(jnp.broadcast_to(line, (whole, whole)).T)
        shares.append([columns[m][half * rows : (half + 1) * rows] for m, half in places])
    step = 512
    for at in range(0, features, step):
        parts = [
            jnp.dot(acts[e], weights[3 * e + 2][0, :, at : at + step], preferred_element_type=jnp.float32)
            .astype(jnp.bfloat16)
            .astype(jnp.float32)
            for e in range(CORES)
        ]
        for b in range(pieces):
            for c in range(0, step, whole):
                mixed = sum(
                    shares[e][b] * parts[e][b * rows : (b + 1) * rows, c : c + whole]
                    for e in range(CORES)
                )
                outs[b][:, at + c : at + c + whole] = mixed.astype(jnp.bfloat16)


def run_experts(pieces, messages, weights):
    tokens = [piece[0] for piece in pieces]
    rows, features = tokens[0].shape
    hidden = weights[0].shape[2]
    vmem = pl.BlockSpec(memory_space=pltpu.VMEM)
    return pl.pallas_call(
        functools.partial(expert_kernel, [piece[1:] for piece in pieces], len(messages)),
        out_shape=[jax.ShapeDtypeStruct((rows, features), jnp.bfloat16)] * len(pieces),
        in_specs=[vmem] * (len(pieces) + len(messages) + len(weights)),
        out_specs=[vmem] * len(pieces),
        compiler_params=pltpu.CompilerParams(vmem_limit_bytes=24 * 1024 * 1024),
        cost_estimate=pl.CostEstimate(
            flops=12 * len(pieces) * rows * features * hidden,
            bytes_accessed=12 * features * hidden,
            transcendentals=0,
        ),
        name="experts",
    )(*tokens, *messages, *weights)


def add_parts(*parts):
    total = parts[0].astype(jnp.float32)
    for part in parts[1:]:
        total = total + part.astype(jnp.float32)
    return total.astype(jnp.bfloat16)


def ring_device(
    queries,
    rotated_keys,
    value_matrix,
    stretch_pos,
    residual,
    norm_gain,
    routes,
    combine,
    gate_weight,
    up_weight,
    down_weight,
):
    chips = lax.axis_size("ctx") // CORES
    far = chips // 2
    onward, back, swap = ring_pairs(chips)

    def send(array, pairs):
        return lax.ppermute(array, "ctx", pairs)

    message = pack_message(stretch_pos, rotated_keys, value_matrix, routes, combine)

    tie = lax.optimization_barrier
    left, right = {0: message}, {0: message}
    for hop in range(1, far + 1):
        if hop == 3:
            inputs, unused = tie(((queries, residual, norm_gain), (left[1], right[1])))
            staged = (
                inputs[0] * jnp.bfloat16(QUERY_SCALE),
                inputs[1].astype(jnp.float32),
                jnp.broadcast_to(inputs[2][None, :], (8, inputs[2].shape[0])),
            )
            left[2], staged = tie((left[2], staged))
        left[hop] = send(left[hop - 1], onward)
        if hop < far:
            right[hop] = send(right[hop - 1], back)
    plane = [message] + [left[h] for h in range(1, far + 1)] + [right[h] for h in range(1, far)]
    near = [message] + [left[h] for h in range(1, far)] + [right[h] for h in range(1, far)]
    last = [left[far - 1], right[far - 1]]
    near = near + [send(m, swap) for m in near if all(m is not other for other in last)]
    begun = attend_start(0, staged[0], message, near)
    left[far], begun = tie((left[far], begun))
    distant = [left[far]] + [send(m, swap) for m in [*last, left[far]]]
    everything = near + distant
    everything, own_weights = tie((everything, (gate_weight, up_weight, down_weight)))
    twin_gate, twin_up, twin_down = [send(w, swap) for w in own_weights]
    hidden_upper, upper = attend(0, staged, message, everything[len(near) :], begun)
    everything, upper = tie((everything, upper))
    hidden_lower, lower = attend(1, staged, message, everything)
    lower, twin_gate, twin_up = tie((lower, twin_gate, twin_up))
    weights = (gate_weight, up_weight, down_weight, twin_gate, twin_up, twin_down)

    from_left, from_right = {(0, 0): upper, (0, 1): lower}, {(0, 0): upper, (0, 1): lower}
    outs = {}

    def later(array, than):
        return tie((array, than))[0]

    def experts_on(tokens, used, after):
        used, after = tie((used, after))
        return run_experts(tokens, used, weights), after

    def experts_of(hop, half, after):
        tokens = [(from_left[hop, half], 0, half), (from_right[hop, half], 1, half)]
        return experts_on(tokens, [left[hop], right[hop]], after)

    last = (upper, lower)
    for hop in range(1, far + 1):
        for half in range(2):
            onto, backto = from_left[hop - 1, half], from_right[hop - 1, half]
            if hop > 1:
                before = (hop - 1, 1 - half) if half == 1 else (hop - 2, 1)
                if before[0] > 0:
                    outs[before], unused = experts_of(*before, last)
                    last = outs[before]
                    onto, backto, last = tie((onto, backto, last))
                    outs[before] = last
            if hop < far or half == 0:
                from_left[hop, half] = send(onto, onward)
            if hop < far or half == 1:
                from_right[hop, half] = send(backto, back)
    outs[far - 1, 1], unused = experts_of(far - 1, 1, last)
    outs[far - 1, 0], outs[far - 1, 1] = tie((outs[far - 1, 0], outs[far - 1, 1]))
    out_left = {key: pair[0] for key, pair in outs.items()}
    out_right = {key: pair[1] for key, pair in outs.items()}

    sums_on = {1: send(out_right[far - 1, 1], onward)}
    sums_back = {0: send(out_left[far - 1, 0], back)}
    (far_upper, far_lower), unused = experts_on(
        [(from_left[far, 0], 0, 0), (from_right[far, 1], 0, 1)], [left[far]], outs[far - 1, 1]
    )
    sums_on[0] = send(far_upper, onward)
    sums_back[1] = send(far_lower, back)
    own_out, unused = experts_on(
        [(upper, 0, 0), (lower, 0, 1)], [message], (far_upper, far_lower, sums_on[1], sums_back[0])
    )
    for hop in range(far - 1, 0, -1):
        onto, backto = sums_on[0], sums_back[1]
        if hop < far - 1:
            sums_on[1] = later(sums_on[1], earlier)
            sums_back[0] = later(sums_back[0], earlier)
            sums_on[1] = send(add_parts(sums_on[1], out_right[hop, 1]), onward)
            sums_back[0] = send(add_parts(sums_back[0], out_left[hop, 0]), back)
        if hop == 1:
            onto, backto = later(onto, own_out), later(backto, own_out)
        earlier = (add_parts(onto, out_right[hop, 0]), add_parts(backto, out_left[hop, 1]))
        sums_on[0], sums_back[1] = send(earlier[0], onward), send(earlier[1], back)
    hidden_state = (hidden_upper, hidden_lower)
    return jnp.concatenate(
        [
            (
                hidden_state[half]
                + own_out[half].astype(jnp.float32)
                + sums_on[half].astype(jnp.float32)
                + sums_back[half].astype(jnp.float32)
            ).astype(jnp.bfloat16)
            for half in range(2)
        ],
        axis=0,
    )


def exchange_device(
    queries,
    rotated_keys,
    value_matrix,
    stretch_pos,
    residual,
    norm_gain,
    routes,
    combine,
    gate_weight,
    up_weight,
    down_weight,
):
    tok_rows = queries.shape[0]
    kv_heads = rotated_keys.shape[1] // HEAD_SIZE
    head_group = queries.shape[1] // rotated_keys.shape[1]
    ctx_count = lax.axis_size("ctx")
    positions = stretch_pos[0] * tok_rows + jnp.arange(tok_rows, dtype=jnp.int32)
    latest = jnp.max(positions)
    query_heads = queries.reshape(tok_rows, kv_heads, head_group, HEAD_SIZE)
    scale_factor = 1.0 / math.sqrt(HEAD_SIZE)

    def update(state, key_block, value_block, key_pos):
        best, total, accum = state
        scores = (
            jnp.einsum(
                "tagd,sad->agts",
                query_heads,
                key_block.reshape(-1, kv_heads, HEAD_SIZE),
                preferred_element_type=jnp.float32,
            )
            * scale_factor
        )
        scores = jnp.where(
            key_pos[None, None, None, :] <= positions[None, None, :, None], scores, jnp.float32(NEG)
        )
        fresh = jnp.maximum(best, jnp.max(scores, axis=-1))
        shrink = jnp.exp(best - fresh)
        expo = jnp.exp(scores - fresh[..., None])
        total = total * shrink + jnp.sum(expo, axis=-1)
        weighted = jnp.einsum(
            "agts,sad->agtd",
            expo.astype(jnp.bfloat16),
            value_block.reshape(-1, kv_heads, HEAD_SIZE),
            preferred_element_type=jnp.float32,
        )
        accum = accum * shrink[..., None] + weighted
        return (fresh, total, accum)

    start_state = (
        jnp.full((kv_heads, head_group, tok_rows), NEG, jnp.float32),
        jnp.zeros((kv_heads, head_group, tok_rows), jnp.float32),
        jnp.zeros((kv_heads, head_group, tok_rows, HEAD_SIZE), jnp.float32),
    )
    key_part = lax.all_gather(rotated_keys, "ctx", axis=0, tiled=True)
    value_part = lax.all_gather(value_matrix, "ctx", axis=0, tiled=True)
    pos_part = lax.all_gather(positions, "ctx", axis=0, tiled=True)
    span = key_part.shape[0]
    width = 512
    blocks = span // width
    stacked = (
        key_part.reshape(blocks, width, -1),
        value_part.reshape(blocks, width, -1),
        pos_part.reshape(blocks, width),
    )

    def advance(inner, item):
        key_block, value_block, key_pos = item
        result = lax.cond(
            jnp.min(key_pos) > latest,
            lambda kept: kept,
            lambda kept: update(kept, key_block, value_block, key_pos),
            inner,
        )
        return (result, None)

    final, unused = lax.scan(advance, start_state, stacked)
    best, total, accum = final
    attended = (
        jnp.transpose(accum / total[..., None], (2, 0, 1, 3))
        .reshape(tok_rows, -1)
        .astype(jnp.bfloat16)
    )
    hidden_state = residual.astype(jnp.float32) + attended.astype(jnp.float32)
    meansq = jnp.mean(hidden_state * hidden_state, axis=-1, keepdims=True)
    normed = (hidden_state * lax.rsqrt(meansq + 1e-06) * norm_gain).astype(jnp.bfloat16)
    local_experts = gate_weight.shape[0]
    total_experts = local_experts * ctx_count
    top_count = routes.shape[1]
    capacity = min(
        tok_rows,
        tok_rows * top_count // total_experts + max(1, tok_rows * top_count // (8 * total_experts)),
    )
    flat_routes = routes.reshape(-1)
    onehot = (flat_routes[:, None] == jnp.arange(total_experts, dtype=jnp.int32)[None, :]).astype(
        jnp.int32
    )
    earlier = jnp.cumsum(onehot, axis=0) - onehot
    ranking = jnp.sum(earlier * onehot, axis=1)
    slot_ids = flat_routes * capacity + ranking
    selector = jnp.any(
        slot_ids.reshape(tok_rows, top_count)[:, :, None]
        == jnp.arange(total_experts * capacity, dtype=jnp.int32)[None, None, :],
        axis=1,
    ).astype(jnp.bfloat16)
    outgoing = jnp.einsum("ts,td->sd", selector, normed, preferred_element_type=jnp.float32).astype(
        jnp.bfloat16
    )
    outgoing = outgoing.reshape(ctx_count, local_experts, capacity, D)
    incoming = lax.all_to_all(outgoing, "ctx", split_axis=0, concat_axis=0, tiled=True)
    gate = jnp.einsum("secd,edh->sech", incoming, gate_weight, preferred_element_type=jnp.float32)
    upper = jnp.einsum("secd,edh->sech", incoming, up_weight, preferred_element_type=jnp.float32)
    act = (jax.nn.silu(gate) * upper).astype(jnp.bfloat16)
    returned = lax.all_to_all(
        jnp.einsum("sech,ehd->secd", act, down_weight, preferred_element_type=jnp.float32).astype(
            jnp.bfloat16
        ),
        "ctx",
        split_axis=0,
        concat_axis=0,
        tiled=True,
    )
    flat_back = returned.reshape(total_experts * capacity, D)
    picked = jnp.take(flat_back, slot_ids, axis=0).reshape(tok_rows, top_count, D)
    mixture = jnp.sum(combine[:, :, None] * picked.astype(jnp.float32), axis=1)
    return (hidden_state + mixture).astype(jnp.bfloat16)


def solution(mesh):
    placed = (
        P(("groups", "ctx"), None),
        P(("groups", "ctx"), None),
        P(("groups", "ctx"), None),
        P(("groups", "ctx")),
        P(("groups", "ctx"), None),
        P(),
        P(("groups", "ctx"), None),
        P(("groups", "ctx"), None),
        P("ctx", None, None),
        P("ctx", None, None),
        P("ctx", None, None),
    )
    ctx_count = mesh.shape["ctx"]

    def on_device(*arguments):
        routes, gate_weight = arguments[6], arguments[8]
        dense = 4 * routes.shape[1] >= gate_weight.shape[0] * ctx_count
        ringed = gate_weight.shape[0] == 1 and ctx_count % (2 * CORES) == 0
        ringed = ringed and ctx_count >= 6 * CORES and 2 * routes.shape[1] == EXTRA
        return (ring_device if dense and ringed else exchange_device)(*arguments)

    return jax.shard_map(
        on_device, mesh=mesh, in_specs=placed, out_specs=P(("groups", "ctx"), None), check_vma=False
    )
```

```python
import functools
import math

import jax
import jax.numpy as jnp
from jax import lax
from jax.experimental import pallas as pl
from jax.experimental.pallas import tpu as pltpu
from jax.sharding import PartitionSpec as P

D = 2048
HEAD_SIZE = 128
CORES = 2
EXTRA = 16
QUERY_SCALE = 0.125


NEG = -1e30


def ring_pairs(chips):
    order = list(range(0, chips, 2)) + list(range(chips - 1, 0, -2))
    onward = [
        (order[i] * CORES + core, order[(i + 1) % chips] * CORES + core)
        for i in range(chips)
        for core in range(CORES)
    ]
    back = [(b, a) for a, b in onward]
    swap = [(i, i ^ 1) for i in range(chips * CORES)]
    return onward, back, swap


def pack_kernel(pos_ref, key_ref, value_ref, routes_ref, combine_ref, out_ref):
    rows, width = key_ref.shape
    top = routes_ref.shape[0]
    out_ref[0:rows, 0:width] = key_ref[...]
    out_ref[0:rows, width : 2 * width] = value_ref[...]
    weight = combine_ref[...]
    high = weight.astype(jnp.bfloat16).astype(jnp.float32)
    low = weight - high
    names = routes_ref[...].astype(jnp.float32)
    place = jnp.full((EXTRA, 2 * width - 2 * rows), pos_ref[0].astype(jnp.float32), jnp.float32)
    tail = slice(rows, rows + EXTRA)
    out_ref[tail, 0:rows] = jnp.concatenate([names, high], axis=0).astype(jnp.bfloat16)
    out_ref[tail, rows : 2 * rows] = jnp.concatenate([low, jnp.zeros_like(low)], axis=0).astype(
        jnp.bfloat16
    )
    out_ref[tail, 2 * rows : 2 * width] = place.astype(jnp.bfloat16)


def pack_message(stretch_pos, keys, values, routes, combine):
    rows, width = keys.shape
    vmem = pl.BlockSpec(memory_space=pltpu.VMEM)
    return pl.pallas_call(
        pack_kernel,
        out_shape=jax.ShapeDtypeStruct((rows + EXTRA, 2 * width), jnp.bfloat16),
        in_specs=[pl.BlockSpec(memory_space=pltpu.SMEM), vmem, vmem, vmem, vmem],
        out_specs=vmem,
        name="pack_message",
    )(stretch_pos, keys, values, routes.T, combine.T)


def attend_kernel(count, half, begun, ended, *refs):
    refs = list(refs)

    def take(number):
        taken, refs[:number] = refs[:number], []
        return taken

    query_ref, own_ref = take(2)
    messages = take(count)
    if begun:
        begun_sums, begun_best = take(2)
    if ended:
        residual_ref, gain_ref, hidden_ref, normed_ref = take(4)
    else:
        sums_ref, best_ref = take(2)
    key_ext, value_ext = refs
    features = query_ref.shape[1]
    some = query_ref.shape[0] // 2
    mine = slice(half * some, (half + 1) * some)
    rows = messages[0].shape[0] - EXTRA
    kv_heads = key_ext.shape[0]
    heads = features // HEAD_SIZE
    group = heads // kv_heads
    span = count * rows
    width = kv_heads * HEAD_SIZE
    sub = lax.broadcasted_iota(jnp.int32, (rows, rows), 0)
    lane = lax.broadcasted_iota(jnp.int32, (rows, rows), 1)
    ahead = (sub - lane).astype(jnp.float32)
    own_pos = own_ref[rows : rows + EXTRA, 256 : 256 + rows][0:1].astype(jnp.float32)
    ones = jnp.ones((rows, HEAD_SIZE), jnp.bfloat16)
    for block in range(count):
        ref = messages[block]
        at = slice(block * rows, (block + 1) * rows)
        pos = ref[rows : rows + EXTRA, 256 : 256 + rows][0:1].astype(jnp.float32)
        later = (pos - own_pos) * float(rows) + ahead
        bias = jnp.where(later > 0.0, NEG, 0.0).astype(jnp.bfloat16)
        for a in range(kv_heads):
            key_ext[a, at, 0:HEAD_SIZE] = ref[0:rows, a * HEAD_SIZE : (a + 1) * HEAD_SIZE]
            key_ext[a, at, HEAD_SIZE : HEAD_SIZE + rows] = bias
            value_ext[a, at, 0:HEAD_SIZE] = ref[
                0:rows, width + a * HEAD_SIZE : width + (a + 1) * HEAD_SIZE
            ]
            value_ext[a, at, HEAD_SIZE : 2 * HEAD_SIZE] = ones
    eye = jnp.where(sub == lane, 1.0, 0.0).astype(jnp.bfloat16)[mine]
    rate = math.log2(math.e) / math.sqrt(HEAD_SIZE) / QUERY_SCALE
    step = min(512 if span % 512 == 0 else 256, span)
    pair = 4
    squares = jnp.zeros((some, HEAD_SIZE), jnp.float32)

    def scores_of(first):
        stacked = jnp.concatenate(
            [
                jnp.concatenate([query_ref[mine, h * HEAD_SIZE : (h + 1) * HEAD_SIZE], eye], axis=1)
                for h in range(first, first + pair)
            ],
            axis=0,
        )
        return [
            lax.dot_general(
                stacked,
                key_ext[first // group, at : at + step, :],
                (((1,), (1,)), ((), ())),
                preferred_element_type=jnp.float32,
            )
            for at in range(0, span, step)
        ]

    ready = scores_of(0)
    for first in range(0, heads, pair):
        a = first // group
        scores = ready
        if first + pair < heads:
            ready = scores_of(first + pair)
        best = functools.reduce(jnp.maximum, scores)
        best = jnp.max(best, axis=1, keepdims=True)
        total = None
        at = slice(first * some, (first + pair) * some)
        if begun:
            before = begun_best[at]
            best = jnp.maximum(best, before[:, 0:1])
            shrink = jnp.exp2((before - best) * rate)
            total = begun_sums[at] * jnp.concatenate([shrink, shrink], axis=1)
        for i, part in enumerate(scores):
            probs = jnp.exp2((part - best) * rate).astype(jnp.bfloat16)
            term = jnp.dot(
                probs,
                value_ext[a, i * step : (i + 1) * step, :],
                preferred_element_type=jnp.float32,
            )
            total = term if total is None else total + term
        if not ended:
            sums_ref[at] = total
            best_ref[at] = jnp.broadcast_to(best, (pair * some, HEAD_SIZE))
            continue
        attended = (total[:, 0:HEAD_SIZE] / total[:, HEAD_SIZE:]).astype(jnp.bfloat16)
        for j in range(pair):
            cols = slice((first + j) * HEAD_SIZE, (first + j + 1) * HEAD_SIZE)
            state = residual_ref[mine, cols] + attended[
                j * some : (j + 1) * some
            ].astype(jnp.float32)
            hidden_ref[:, cols] = state
            squares = squares + state * state
    if not ended:
        return
    meansq = jnp.sum(squares, axis=1, keepdims=True) / float(heads * HEAD_SIZE)
    inverse = lax.rsqrt(meansq + 1e-06)
    for h in range(heads):
        cols = slice(h * HEAD_SIZE, (h + 1) * HEAD_SIZE)
        normed_ref[:, cols] = (hidden_ref[:, cols] * inverse * gain_ref[0:1, cols]).astype(
            jnp.bfloat16
        )


def attend_call(half, begun, ended, queries, messages, inputs, out_shape):
    rows, features = queries.shape
    count = len(messages) - 1
    kv_heads = messages[0].shape[1] // (2 * HEAD_SIZE)
    vmem = pl.BlockSpec(memory_space=pltpu.VMEM)
    span = count * rows
    return pl.pallas_call(
        functools.partial(attend_kernel, count, half, begun, ended),
        out_shape=out_shape,
        in_specs=[vmem] * (1 + len(messages) + len(inputs)),
        out_specs=(vmem,) * len(out_shape),
        scratch_shapes=[
            pltpu.VMEM((kv_heads, span, 2 * HEAD_SIZE), jnp.bfloat16),
            pltpu.VMEM((kv_heads, span, 2 * HEAD_SIZE), jnp.bfloat16),
        ],
        compiler_params=pltpu.CompilerParams(vmem_limit_bytes=28 * 1024 * 1024),
        cost_estimate=pl.CostEstimate(
            flops=4 * rows * span * features if ended else 0,
            bytes_accessed=4 * 1024 * 1024 if ended else 1024,
            transcendentals=0,
        ),
        name="attend",
    )(queries, *messages, *inputs)


def attend_start(half, queries, own, messages):
    rows, features = queries.shape
    lines = rows // 2 * (features // HEAD_SIZE)
    return attend_call(
        half,
        False,
        False,
        queries,
        [own] + messages,
        (),
        (
            jax.ShapeDtypeStruct((lines, 2 * HEAD_SIZE), jnp.float32),
            jax.ShapeDtypeStruct((lines, HEAD_SIZE), jnp.float32),
        ),
    )


def attend(half, staged, own, messages, begun=()):
    queries, residual, gain = staged
    rows, features = queries.shape
    return attend_call(
        half,
        len(begun) > 0,
        True,
        queries,
        [own] + messages,
        (*begun, residual, gain),
        (
            jax.ShapeDtypeStruct((rows // 2, features), jnp.float32),
            jax.ShapeDtypeStruct((rows // 2, features), jnp.bfloat16),
        ),
    )


def expert_kernel(places, count, *refs):
    pieces = len(places)
    tokens = refs[:pieces]
    messages = refs[pieces : pieces + count]
    weights = refs[pieces + count : pieces + count + 3 * CORES]
    outs = refs[pieces + count + 3 * CORES :]
    rows, features = tokens[0].shape
    whole = messages[0].shape[0] - EXTRA
    top = EXTRA // 2
    me = lax.axis_index("ctx")
    normed = jnp.concatenate([ref[...] for ref in tokens], axis=0)
    shares, acts = [], []
    for e in range(CORES):
        gate_ref, up_ref = weights[3 * e], weights[3 * e + 1]
        gate = jnp.dot(normed, gate_ref[0], preferred_element_type=jnp.float32)
        upper = jnp.dot(normed, up_ref[0], preferred_element_type=jnp.float32)
        acts.append((gate / (1.0 + jnp.exp(-gate)) * upper).astype(jnp.bfloat16))
        name = jnp.bitwise_xor(me, e).astype(jnp.float32)
        columns = []
        for ref in messages:
            extra = ref[whole : whole + EXTRA, 0 : 2 * whole].astype(jnp.float32)
            value = extra[top : 2 * top, 0:whole] + extra[0:top, whole : 2 * whole]
            hit = jnp.where(extra[0:top, 0:whole] == name, value, 0.0)
            line = jnp.sum(hit, axis=0, keepdims=True)
            columns.append(jnp.broadcast_to(line, (whole, whole)).T)
        shares.append([columns[m][half * rows : (half + 1) * rows] for m, half in places])
    step = 512
    for at in range(0, features, step):
        parts = [
            jnp.dot(acts[e], weights[3 * e + 2][0, :, at : at + step], preferred_element_type=jnp.float32)
            .astype(jnp.bfloat16)
            .astype(jnp.float32)
            for e in range(CORES)
        ]
        for b in range(pieces):
            for c in range(0, step, whole):
                mixed = sum(
                    shares[e][b] * parts[e][b * rows : (b + 1) * rows, c : c + whole]
                    for e in range(CORES)
                )
                outs[b][:, at + c : at + c + whole] = mixed.astype(jnp.bfloat16)


def run_experts(pieces, messages, weights):
    tokens = [piece[0] for piece in pieces]
    rows, features = tokens[0].shape
    hidden = weights[0].shape[2]
    vmem = pl.BlockSpec(memory_space=pltpu.VMEM)
    return pl.pallas_call(
        functools.partial(expert_kernel, [piece[1:] for piece in pieces], len(messages)),
        out_shape=[jax.ShapeDtypeStruct((rows, features), jnp.bfloat16)] * len(pieces),
        in_specs=[vmem] * (len(pieces) + len(messages) + len(weights)),
        out_specs=[vmem] * len(pieces),
        compiler_params=pltpu.CompilerParams(vmem_limit_bytes=24 * 1024 * 1024),
        cost_estimate=pl.CostEstimate(
            flops=12 * len(pieces) * rows * features * hidden,
            bytes_accessed=12 * features * hidden,
            transcendentals=0,
        ),
        name="experts",
    )(*tokens, *messages, *weights)


def add_parts(*parts):
    total = parts[0].astype(jnp.float32)
    for part in parts[1:]:
        total = total + part.astype(jnp.float32)
    return total.astype(jnp.bfloat16)


def ring_device(
    queries,
    rotated_keys,
    value_matrix,
    stretch_pos,
    residual,
    norm_gain,
    routes,
    combine,
    gate_weight,
    up_weight,
    down_weight,
):
    chips = lax.axis_size("ctx") // CORES
    far = chips // 2
    onward, back, swap = ring_pairs(chips)

    def send(array, pairs):
        return lax.ppermute(array, "ctx", pairs)

    message = pack_message(stretch_pos, rotated_keys, value_matrix, routes, combine)

    tie = lax.optimization_barrier
    left, right = {0: message}, {0: message}
    for hop in range(1, far + 1):
        if hop == 3:
            inputs, unused = tie(((queries, residual, norm_gain), (left[1], right[1])))
            staged = (
                inputs[0] * jnp.bfloat16(QUERY_SCALE),
                inputs[1].astype(jnp.float32),
                jnp.broadcast_to(inputs[2][None, :], (8, inputs[2].shape[0])),
            )
            left[2], staged = tie((left[2], staged))
        left[hop] = send(left[hop - 1], onward)
        if hop < far:
            right[hop] = send(right[hop - 1], back)
    plane = [message] + [left[h] for h in range(1, far + 1)] + [right[h] for h in range(1, far)]
    near = [message] + [left[h] for h in range(1, far)] + [right[h] for h in range(1, far)]
    last = [left[far - 1], right[far - 1]]
    near = near + [send(m, swap) for m in near if all(m is not other for other in last)]
    begun = attend_start(0, staged[0], message, near)
    left[far], begun = tie((left[far], begun))
    distant = [left[far]] + [send(m, swap) for m in [*last, left[far]]]
    everything = near + distant
    everything, own_weights = tie((everything, (gate_weight, up_weight, down_weight)))
    twin_gate, twin_up, twin_down = [send(w, swap) for w in own_weights]
    hidden_upper, upper = attend(0, staged, message, everything[len(near) :], begun)
    everything, upper = tie((everything, upper))
    hidden_lower, lower = attend(1, staged, message, everything)
    lower, twin_gate, twin_up = tie((lower, twin_gate, twin_up))
    weights = (gate_weight, up_weight, down_weight, twin_gate, twin_up, twin_down)

    from_left, from_right = {(0, 0): upper, (0, 1): lower}, {(0, 0): upper, (0, 1): lower}
    outs = {}

    def later(array, than):
        return tie((array, than))[0]

    def experts_on(tokens, used, after):
        used, after = tie((used, after))
        return run_experts(tokens, used, weights), after

    def experts_of(hop, half, after):
        tokens = [(from_left[hop, half], 0, half), (from_right[hop, half], 1, half)]
        return experts_on(tokens, [left[hop], right[hop]], after)

    last = (upper, lower)
    for hop in range(1, far + 1):
        for half in range(2):
            onto, backto = from_left[hop - 1, half], from_right[hop - 1, half]
            if hop > 1:
                before = (hop - 1, 1 - half) if half == 1 else (hop - 2, 1)
                if before[0] > 0:
                    outs[before], unused = experts_of(*before, last)
                    last = outs[before]
                    onto, backto, last = tie((onto, backto, last))
                    outs[before] = last
            if hop < far or half == 0:
                from_left[hop, half] = send(onto, onward)
            if hop < far or half == 1:
                from_right[hop, half] = send(backto, back)
    outs[far - 1, 1], unused = experts_of(far - 1, 1, last)
    outs[far - 1, 0], outs[far - 1, 1] = tie((outs[far - 1, 0], outs[far - 1, 1]))
    out_left = {key: pair[0] for key, pair in outs.items()}
    out_right = {key: pair[1] for key, pair in outs.items()}

    sums_on = {1: send(out_right[far - 1, 1], onward)}
    sums_back = {0: send(later(out_left[far - 1, 0], from_right[far, 1]), back)}
    (far_upper, far_lower), unused = experts_on(
        [(from_left[far, 0], 0, 0), (from_right[far, 1], 0, 1)], [left[far]], outs[far - 1, 1]
    )
    sums_on[0] = send(far_upper, onward)
    sums_back[1] = send(far_lower, back)
    own_out, unused = experts_on(
        [(upper, 0, 0), (lower, 0, 1)], [message], (far_upper, far_lower, sums_on[1])
    )
    for hop in range(far - 1, 0, -1):
        onto, backto = sums_on[0], sums_back[1]
        if hop < far - 1:
            sums_on[1] = later(sums_on[1], earlier)
            sums_back[0] = later(sums_back[0], earlier)
            sums_on[1] = send(add_parts(sums_on[1], out_right[hop, 1]), onward)
            sums_back[0] = send(add_parts(sums_back[0], out_left[hop, 0]), back)
        if hop == 1:
            onto, backto = later(onto, own_out), later(backto, own_out)
        earlier = (add_parts(onto, out_right[hop, 0]), add_parts(backto, out_left[hop, 1]))
        sums_on[0], sums_back[1] = send(earlier[0], onward), send(earlier[1], back)
    hidden_state = (hidden_upper, hidden_lower)
    return jnp.concatenate(
        [
            (
                hidden_state[half]
                + own_out[half].astype(jnp.float32)
                + sums_on[half].astype(jnp.float32)
                + sums_back[half].astype(jnp.float32)
            ).astype(jnp.bfloat16)
            for half in range(2)
        ],
        axis=0,
    )


def exchange_device(
    queries,
    rotated_keys,
    value_matrix,
    stretch_pos,
    residual,
    norm_gain,
    routes,
    combine,
    gate_weight,
    up_weight,
    down_weight,
):
    tok_rows = queries.shape[0]
    kv_heads = rotated_keys.shape[1] // HEAD_SIZE
    head_group = queries.shape[1] // rotated_keys.shape[1]
    ctx_count = lax.axis_size("ctx")
    positions = stretch_pos[0] * tok_rows + jnp.arange(tok_rows, dtype=jnp.int32)
    latest = jnp.max(positions)
    query_heads = queries.reshape(tok_rows, kv_heads, head_group, HEAD_SIZE)
    scale_factor = 1.0 / math.sqrt(HEAD_SIZE)

    def update(state, key_block, value_block, key_pos):
        best, total, accum = state
        scores = (
            jnp.einsum(
                "tagd,sad->agts",
                query_heads,
                key_block.reshape(-1, kv_heads, HEAD_SIZE),
                preferred_element_type=jnp.float32,
            )
            * scale_factor
        )
        scores = jnp.where(
            key_pos[None, None, None, :] <= positions[None, None, :, None], scores, jnp.float32(NEG)
        )
        fresh = jnp.maximum(best, jnp.max(scores, axis=-1))
        shrink = jnp.exp(best - fresh)
        expo = jnp.exp(scores - fresh[..., None])
        total = total * shrink + jnp.sum(expo, axis=-1)
        weighted = jnp.einsum(
            "agts,sad->agtd",
            expo.astype(jnp.bfloat16),
            value_block.reshape(-1, kv_heads, HEAD_SIZE),
            preferred_element_type=jnp.float32,
        )
        accum = accum * shrink[..., None] + weighted
        return (fresh, total, accum)

    start_state = (
        jnp.full((kv_heads, head_group, tok_rows), NEG, jnp.float32),
        jnp.zeros((kv_heads, head_group, tok_rows), jnp.float32),
        jnp.zeros((kv_heads, head_group, tok_rows, HEAD_SIZE), jnp.float32),
    )
    key_part = lax.all_gather(rotated_keys, "ctx", axis=0, tiled=True)
    value_part = lax.all_gather(value_matrix, "ctx", axis=0, tiled=True)
    pos_part = lax.all_gather(positions, "ctx", axis=0, tiled=True)
    span = key_part.shape[0]
    width = 512
    blocks = span // width
    stacked = (
        key_part.reshape(blocks, width, -1),
        value_part.reshape(blocks, width, -1),
        pos_part.reshape(blocks, width),
    )

    def advance(inner, item):
        key_block, value_block, key_pos = item
        result = lax.cond(
            jnp.min(key_pos) > latest,
            lambda kept: kept,
            lambda kept: update(kept, key_block, value_block, key_pos),
            inner,
        )
        return (result, None)

    final, unused = lax.scan(advance, start_state, stacked)
    best, total, accum = final
    attended = (
        jnp.transpose(accum / total[..., None], (2, 0, 1, 3))
        .reshape(tok_rows, -1)
        .astype(jnp.bfloat16)
    )
    hidden_state = residual.astype(jnp.float32) + attended.astype(jnp.float32)
    meansq = jnp.mean(hidden_state * hidden_state, axis=-1, keepdims=True)
    normed = (hidden_state * lax.rsqrt(meansq + 1e-06) * norm_gain).astype(jnp.bfloat16)
    local_experts = gate_weight.shape[0]
    total_experts = local_experts * ctx_count
    top_count = routes.shape[1]
    capacity = min(
        tok_rows,
        tok_rows * top_count // total_experts + max(1, tok_rows * top_count // (8 * total_experts)),
    )
    flat_routes = routes.reshape(-1)
    onehot = (flat_routes[:, None] == jnp.arange(total_experts, dtype=jnp.int32)[None, :]).astype(
        jnp.int32
    )
    earlier = jnp.cumsum(onehot, axis=0) - onehot
    ranking = jnp.sum(earlier * onehot, axis=1)
    slot_ids = flat_routes * capacity + ranking
    selector = jnp.any(
        slot_ids.reshape(tok_rows, top_count)[:, :, None]
        == jnp.arange(total_experts * capacity, dtype=jnp.int32)[None, None, :],
        axis=1,
    ).astype(jnp.bfloat16)
    outgoing = jnp.einsum("ts,td->sd", selector, normed, preferred_element_type=jnp.float32).astype(
        jnp.bfloat16
    )
    outgoing = outgoing.reshape(ctx_count, local_experts, capacity, D)
    incoming = lax.all_to_all(outgoing, "ctx", split_axis=0, concat_axis=0, tiled=True)
    gate = jnp.einsum("secd,edh->sech", incoming, gate_weight, preferred_element_type=jnp.float32)
    upper = jnp.einsum("secd,edh->sech", incoming, up_weight, preferred_element_type=jnp.float32)
    act = (jax.nn.silu(gate) * upper).astype(jnp.bfloat16)
    returned = lax.all_to_all(
        jnp.einsum("sech,ehd->secd", act, down_weight, preferred_element_type=jnp.float32).astype(
            jnp.bfloat16
        ),
        "ctx",
        split_axis=0,
        concat_axis=0,
        tiled=True,
    )
    flat_back = returned.reshape(total_experts * capacity, D)
    picked = jnp.take(flat_back, slot_ids, axis=0).reshape(tok_rows, top_count, D)
    mixture = jnp.sum(combine[:, :, None] * picked.astype(jnp.float32), axis=1)
    return (hidden_state + mixture).astype(jnp.bfloat16)


def solution(mesh):
    placed = (
        P(("groups", "ctx"), None),
        P(("groups", "ctx"), None),
        P(("groups", "ctx"), None),
        P(("groups", "ctx")),
        P(("groups", "ctx"), None),
        P(),
        P(("groups", "ctx"), None),
        P(("groups", "ctx"), None),
        P("ctx", None, None),
        P("ctx", None, None),
        P("ctx", None, None),
    )
    ctx_count = mesh.shape["ctx"]

    def on_device(*arguments):
        routes, gate_weight = arguments[6], arguments[8]
        dense = 4 * routes.shape[1] >= gate_weight.shape[0] * ctx_count
        ringed = gate_weight.shape[0] == 1 and ctx_count % (2 * CORES) == 0
        ringed = ringed and ctx_count >= 6 * CORES and 2 * routes.shape[1] == EXTRA
        return (ring_device if dense and ringed else exchange_device)(*arguments)

    return jax.shard_map(
        on_device, mesh=mesh, in_specs=placed, out_specs=P(("groups", "ctx"), None), check_vma=False
    )
```
